32 devices in a mesh: section: 4 (over y, x), dp: 8 (over z, core).
Axes of the slice: x: 2, y: 2, z: 4, core: 2. Of those that a mesh axis runs over, the one named last changes fastest.
Arguments:
- inputs: bfloat16 [8, 2, 502, 768], P('dp', None, None, 'section'), may hold values from -6 to 6
- out_grad: bfloat16 [8, 2, 502, 768], P('dp', None, None, 'section'), may hold values from -6 to 6
- memory: bfloat16 [8, 10, 768], P('dp', None, 'section'), may hold values from -6 to 6
- lengths: int32 [8], P('dp'), may hold values from 251 to 1004, as said below
- w_qkv: bfloat16 [4, 768, 2304], P('section'), may hold values from -0.21875 to 0.21875
- w_proj: bfloat16 [4, 768, 768], P('section'), may hold values from -3 to 3
- gain_one: float32 [4, 768], P('section'), may hold values from 0.1 to 1.9
- shift_one: float32 [4, 768], P('section'), may hold values from -3 to 3
- w_in: bfloat16 [4, 768, 3072], P('section'), may hold values from -0.21875 to 0.21875
- b_in: float32 [4, 3072], P('section'), may hold values from -3 to 3
- w_down: bfloat16 [4, 3072, 768], P('section'), may hold values from -0.109375 to 0.109375
- gain_two: float32 [4, 768], P('section'), may hold values from 0.1 to 1.9
- shift_two: float32 [4, 768], P('section'), may hold values from -3 to 3
Outputs:
- outputs: bfloat16 [8, 2, 502, 768], P('dp', None, None, 'section')
- input_grad: bfloat16 [8, 2, 502, 768], P('dp', None, None, 'section')
- memory_grad: float32 [8, 10, 768], P('dp', None, 'section')
- grad_w_qkv: float32 [4, 768, 2304], P('section', 'dp')
- grad_w_proj: float32 [4, 768, 768], P('section', 'dp')
- grad_gain_one: float32 [4, 768], P('section', 'dp')
- grad_shift_one: float32 [4, 768], P('section', 'dp')
- grad_w_in: float32 [4, 768, 3072], P('section', 'dp')
- grad_b_in: float32 [4, 3072], P('section', 'dp')
- grad_w_down: float32 [4, 3072, 768], P('section', 'dp')
- grad_gain_two: float32 [4, 768], P('section', 'dp')
- grad_shift_two: float32 [4, 768], P('section', 'dp')
The draws below stay inside these ranges and needn't reach their ends.
Inputs may be any that keep to these rules, and one draw needn't show every extreme that they name: `lengths`: an item's tokens fill its segments in order; one item of the batch has exactly 1004 tokens.
All inputs are finite; a program needn't handle non-finite values.
Results may differ from the reference program's by a relative error of at most 0.018.
Values may be sent and summed in bfloat16 or wider, within the bound.
A program may use at most 320 MiB of HBM per device.

```python
import jax
import jax.numpy as jnp
from jax import lax

D = 768
H = 12
HEAD = 64
FF = 3072
MEM = 10
TOK_SEG = 502
SEGS = 2
ROWS = 522
LAYERS = 4
ITEMS = 8


def draw_lengths(key, part):
    key = jax.random.fold_in(key, 7)
    first_key, second_key = jax.random.split(key)
    drawn = jax.random.randint(first_key, (ITEMS,), TOK_SEG // 2, SEGS * TOK_SEG + 1)
    chosen = jax.random.randint(second_key, (), 0, ITEMS)
    return jnp.where(jnp.arange(ITEMS) == chosen, SEGS * TOK_SEG, drawn).astype(jnp.int32)


def strengthened(values, own_key, source, target, shards_of, factor):
    def block_of(dim):
        return (jnp.arange(values.shape[dim]) // (values.shape[dim] // shards_of)).reshape((-1,) + (1,) * (values.ndim - 1 - dim))

    near = jax.random.permutation(own_key, shards_of)[block_of(target)]
    second = (block_of(target) + shards_of // 2) % shards_of
    return jnp.where((block_of(source) == near) | (block_of(source) == second), factor * values, values)


def block_levels(stream_key, extent, cuts, least, high):
    loudness, own = 1.0, jax.random.fold_in(stream_key, 6)
    for dim, parts in cuts:
        draws = jnp.exp(jax.random.uniform(jax.random.fold_in(own, dim), (parts,), jnp.float32, least / len(cuts), high / len(cuts)))
        loudness = loudness * jnp.repeat(draws, extent[dim] // parts).reshape([-1 if axis == dim else 1 for axis in range(len(extent))])
    return loudness


def noise(own_key, shape, scale, bound, cuts=(), held_as=jnp.bfloat16):
    loudness = block_levels(own_key, shape, cuts, -0.22, 0.18) if cuts else 1.0
    result = jax.random.normal(own_key, shape, jnp.float32) * scale * loudness
    return jnp.minimum(jnp.maximum(result, -bound), bound).astype(held_as)


def noise_with(rng, extent, scale, most, cuts, heavy, kind=jnp.bfloat16):
    array = scale * jax.random.normal(rng, extent, jnp.float32)
    if cuts:
        array = array * block_levels(rng, extent, cuts, -0.22, 0.18)
    return jnp.clip(strengthened(array, jax.random.fold_in(rng, 3), *heavy), -most, most).astype(kind)


def setup_inputs(seed: int = 0) -> dict:
    streams_of = jax.random.split(jax.random.key(seed), 14)
    inputs = noise_with(streams_of[0], (ITEMS, SEGS, TOK_SEG, D), 1.0, 6.0, ((0, 8), (3, 4)), (0, 3, 8, 2.0))
    out_grad = noise(streams_of[1], (ITEMS, SEGS, TOK_SEG, D), 1.0, 6.0, ((0, 8), (3, 4)))
    memory = noise(streams_of[2], (ITEMS, MEM, D), 1.0, 6.0, ((0, 8), (2, 4)))
    lengths = draw_lengths(jax.random.fold_in(streams_of[13], 71), 0)
    w_qkv = noise(streams_of[4], (LAYERS, D, 3 * D), D ** -0.5, 0.21875, ((0, 4),))
    w_proj = noise(streams_of[5], (LAYERS, D, D), (max(3 * D // ROWS, 1)) ** -0.5, 3.0, ((0, 4),))
    gain_one = jnp.clip(1.0 + 0.18 * jax.random.normal(streams_of[6], (LAYERS, D), jnp.float32), 0.1, 1.9)
    shift_one = noise(streams_of[7], (LAYERS, D), 0.3, 3.0, ((0, 4),), jnp.float32)
    w_in = noise(streams_of[8], (LAYERS, D, FF), D ** -0.5, 0.21875, ((0, 4),))
    b_in = noise(streams_of[9], (LAYERS, FF), 0.5, 3.0, ((0, 4),), jnp.float32)
    w_down = noise(streams_of[10], (LAYERS, FF, D), FF ** -0.5, 0.109375, ((0, 4),))
    gain_two = jnp.clip(1.0 + 0.18 * jax.random.normal(streams_of[11], (LAYERS, D), jnp.float32), 0.1, 1.9)
    shift_two = noise(streams_of[12], (LAYERS, D), 0.3, 3.0, ((0, 4),), jnp.float32)
    return dict(inputs=inputs, out_grad=out_grad, memory=memory, lengths=lengths, w_qkv=w_qkv, w_proj=w_proj, gain_one=gain_one, shift_one=shift_one, w_in=w_in, b_in=b_in, w_down=w_down, gain_two=gain_two, shift_two=shift_two)


@jax.custom_vjp
def low(v):
    return lax.optimization_barrier(v.astype(jnp.bfloat16)).astype(jnp.float32)

@jax.custom_vjp
def low_back(v):
    return v

def low_keep(v):
    return (low(v), None)

def low_pass(kept, grad):
    return (grad,)

def back_keep(v):
    return (v, None)

def back_low(kept, grad):
    return (low(grad),)
low.defvjp(low_keep, low_pass)
low_back.defvjp(back_keep, back_low)

def product(left_side, right_side):
    return jnp.matmul(left_side, right_side, precision=lax.Precision.HIGHEST)

def layer_norm(summed, norm_gain, norm_shift):
    center = summed - lax.optimization_barrier(jnp.mean(summed, axis=-1, keepdims=True))
    spread = lax.optimization_barrier(jnp.mean(center * center, axis=-1, keepdims=True))
    return center * lax.rsqrt(spread + 1e-06) * norm_gain + norm_shift

def attention(projected, key_valid):
    num_rows = projected.shape[0]
    pieces = projected.reshape(num_rows, 3, H, HEAD)
    queries, keys, values = (pieces[:, 0], pieces[:, 1], pieces[:, 2])
    scores = jnp.einsum('qhc,khc->hqk', queries, keys, precision=lax.Precision.HIGHEST) * HEAD ** (-0.5)
    scores = low_back(scores)
    scores = jnp.where(key_valid[None, None, :], scores, -1e+30)
    attn_probs = low(jax.nn.softmax(scores, axis=-1))
    mixed_heads = jnp.einsum('hqk,khc->qhc', attn_probs, values, precision=lax.Precision.HIGHEST)
    return low(low_back(mixed_heads.reshape(num_rows, D)))

def encoder_layer(hidden, key_valid, params):
    w_qkv, w_proj, gain_one, shift_one, w_in, b_in, w_down, gain_two, shift_two = params
    projected = low(low_back(product(low(hidden), w_qkv)))
    attended = attention(projected, key_valid)
    branch = low_back(product(attended, w_proj))
    normed = layer_norm(hidden + branch, gain_one, shift_one)
    pre_act = low_back(product(low(normed), w_in) + b_in)
    activated = low(jax.nn.gelu(pre_act, approximate=False))
    feed_out = low_back(product(activated, w_down))
    return layer_norm(normed + feed_out, gain_two, shift_two)

def run_item(weights, item_tokens, memory_init, length):
    memory_now = memory_init
    results = []
    for segment in range(SEGS):
        position = segment * TOK_SEG + jnp.arange(TOK_SEG, dtype=jnp.int32)
        token_valid = position < length
        memory_edge = jnp.ones((MEM,), dtype=bool)
        key_valid = jnp.concatenate([memory_edge, token_valid, memory_edge])
        hidden = jnp.concatenate([memory_now, item_tokens[segment], memory_now], axis=0)
        for layer_index in range(LAYERS):
            hidden = low(low_back(hidden))
            params = tuple((weight[layer_index] for weight in weights))
            hidden = jax.checkpoint(encoder_layer)(hidden, key_valid, params)
        token_rows = low(hidden[MEM:MEM + TOK_SEG])
        results.append(token_rows * token_valid.astype(jnp.float32)[:, None])
        memory_now = low(hidden[MEM + TOK_SEG:])
    return jnp.stack(results)

def reference(inputs, out_grad, memory, lengths, w_qkv, w_proj, gain_one, shift_one, w_in, b_in, w_down, gain_two, shift_two):
    weights = tuple((weight.astype(jnp.float32) for weight in (w_qkv, w_proj, gain_one, shift_one, w_in, b_in, w_down, gain_two, shift_two)))

    def forward(weight_set, tokens_all, memory_all):

        def one_item(item_data):
            return run_item(weight_set, item_data[0], item_data[1], item_data[2])
        return lax.map(one_item, (tokens_all, memory_all, lengths))
    outputs, pull_back = jax.vjp(forward, weights, inputs.astype(jnp.float32), memory.astype(jnp.float32))
    weight_grads, input_grad, memory_grad = pull_back(out_grad.astype(jnp.float32))
    return (outputs.astype(jnp.bfloat16), input_grad.astype(jnp.bfloat16), memory_grad, weight_grads[0], weight_grads[1], weight_grads[2], weight_grads[3], weight_grads[4], weight_grads[5], weight_grads[6], weight_grads[7], weight_grads[8])
```

```python
import functools

import jax
import jax.numpy as jnp
from jax import lax
from jax.experimental import pallas as pl
from jax.experimental.pallas import tpu as pltpu
from jax.sharding import PartitionSpec as P

D = 768
H = 12
HEAD = 64
FF = 3072
PAIRS = H // 2
WIDE = 2 * HEAD
STEP = 256
BLOCK = 16
BF = jnp.bfloat16
F32 = jnp.float32
MESH = pl.DeviceIdType.MESH
ANY = pl.BlockSpec(memory_space=pl.ANY)
VMEM = pl.BlockSpec(memory_space=pltpu.VMEM)
VMEM_LIMIT = 63 * 1024 * 1024


def dot(a, b):
    return jnp.dot(a, b, preferred_element_type=F32)


def dot_nt(a, b):
    return lax.dot_general(a, b, (((1,), (1,)), ((), ())), preferred_element_type=F32)


def dot_tn(a, b):
    return lax.dot_general(a, b, (((0,), (0,)), ((), ())), preferred_element_type=F32)


def cols(index):
    return pl.ds(index * STEP, STEP)


def remote(src, dst, send, recv, target):
    return pltpu.make_async_remote_copy(
        src_ref=src, dst_ref=dst, send_sem=send, recv_sem=recv, device_id=target, device_id_type=MESH
    )


class Place:
    def __init__(self, sections):
        self.s = lax.axis_index("section")
        self.d = lax.axis_index("dp")
        self.c = lax.rem(self.d, 2)
        self.base = self.d - self.c
        self.other = self.base + 1 - self.c
        self.next = lax.rem(self.s + 1, sections)
        self.prev = lax.rem(self.s + sections - 1, sections)


def plane_barrier(place, sections):
    barrier = pltpu.get_barrier_semaphore()
    for section in range(sections):
        for core in range(2):

            @pl.when((place.s != section) | (place.c != core))
            def _():
                pl.semaphore_signal(
                    barrier, inc=1, device_id=(section, place.base + core), device_id_type=MESH
                )

    pl.semaphore_wait(barrier, 2 * sections - 1)


def spread_kernel(sections, a_ref, g_ref, len_ref, x_ref, gr_ref, lens_ref, send, got_x, got_g, got_l, local):
    place = Place(sections)
    s, c = place.s, place.c
    plane_barrier(place, sections)
    moves = []
    for core in range(2):
        for which, (src, dst, target, got) in enumerate(
            ((a_ref, x_ref, 0, got_x), (g_ref, gr_ref, sections - 1, got_g))
        ):
            here = (s == target) & (c == core)
            slot = 2 * which + core
            far = remote(
                src.at[core], dst.at[c, s], send.at[slot], got.at[c, s], (target, place.base + core)
            )
            near = pltpu.make_async_copy(src.at[core], dst.at[c, s], local.at[which])
            moves.append((here, far, near))
    for here, far, near in moves:
        pl.when(jnp.logical_not(here))(far.start)
        pl.when(here)(near.start)
    far_len = remote(len_ref, lens_ref.at[c], send.at[4], got_l.at[0], (s, place.other))
    near_len = pltpu.make_async_copy(len_ref, lens_ref.at[c], local.at[2])
    far_len.start()
    near_len.start()
    for here, far, near in moves:
        pl.when(jnp.logical_not(here))(far.wait_send)
        pl.when(here)(near.wait)
    for which, (src, dst, target, got) in enumerate(
        ((a_ref, x_ref, 0, got_x), (g_ref, gr_ref, sections - 1, got_g))
    ):
        for core in range(2):
            for section in range(sections):

                @pl.when((s == target) & ((c != core) | (s != section)))
                def _():
                    remote(
                        src.at[0], dst.at[core, section], send.at[0], got.at[core, section], (s, place.d)
                    ).wait_recv()

    far_len.wait_send()
    near_len.wait()
    remote(len_ref, lens_ref.at[1 - c], send.at[4], got_l.at[0], (s, place.other)).wait_recv()


def spread(sections, a, g, length_tile):
    half = a.shape[2]
    block = (2, sections) + a.shape[1:]
    return pl.pallas_call(
        functools.partial(spread_kernel, sections),
        name="spread_items",
        out_shape=(
            jax.ShapeDtypeStruct(block, BF),
            jax.ShapeDtypeStruct(block, BF),
            jax.ShapeDtypeStruct((2, 8, 128), F32),
        ),
        in_specs=[ANY, ANY, ANY],
        out_specs=(ANY, ANY, ANY),
        scratch_shapes=[
            pltpu.SemaphoreType.DMA((5,)),
            pltpu.SemaphoreType.DMA((2, sections)),
            pltpu.SemaphoreType.DMA((2, sections)),
            pltpu.SemaphoreType.DMA((1,)),
            pltpu.SemaphoreType.DMA((3,)),
        ],
        compiler_params=pltpu.CompilerParams(collective_id=0, has_side_effects=True),
    )(a, g, length_tile)


def collect_kernel(sections, h_ref, x_ref, m_ref, oh_ref, ox_ref, om_ref, send, got_h, got_x, got_m, local):
    place = Place(sections)
    s, c = place.s, place.c
    plane_barrier(place, sections)
    last = sections - 1
    jobs = (
        (h_ref, oh_ref, last, got_h, 0),
        (x_ref, ox_ref, 0, got_x, 1),
    )
    for src, dst, origin, got, which in jobs:
        for item in range(2):
            for section in range(sections):
                here = (s == section) & (c == item)
                mine = s == origin
                far = remote(
                    src.at[item, section], dst.at[c], send.at[which, item, section], got.at[c], (section, place.base + item)
                )
                near = pltpu.make_async_copy(src.at[item, section], dst.at[c], local.at[which])
                pl.when(mine & jnp.logical_not(here))(far.start)
                pl.when(mine & here)(near.start)
    for item in range(2):
        for section in range(sections):
            here = (s == section) & (c == item)
            mine = (s == 0) & (c == 0)
            far = remote(
                m_ref.at[item, section], om_ref, send.at[2, item, section], got_m.at[0], (section, place.base + item)
            )
            near = pltpu.make_async_copy(m_ref.at[item, section], om_ref, local.at[2])
            pl.when(mine & jnp.logical_not(here))(far.start)
            pl.when(mine & here)(near.start)
    for src, dst, origin, got, which in jobs:
        for item in range(2):
            for section in range(sections):
                here = (s == section) & (c == item)
                mine = s == origin
                far = remote(
                    src.at[item, section], dst.at[c], send.at[which, item, section], got.at[c], (section, place.base + item)
                )
                near = pltpu.make_async_copy(src.at[item, section], dst.at[c], local.at[which])
                pl.when(mine & jnp.logical_not(here))(far.wait_send)
                pl.when(mine & here)(near.wait)
        for core in range(2):

            @pl.when((s != origin) | (c != core))
            def _():
                remote(
                    src.at[0, 0], dst.at[core], send.at[which, 0, 0], got.at[core], (s, place.d)
                ).wait_recv()

    for item in range(2):
        for section in range(sections):
            here = (s == section) & (c == item)
            mine = (s == 0) & (c == 0)
            far = remote(
                m_ref.at[item, section], om_ref, send.at[2, item, section], got_m.at[0], (section, place.base + item)
            )
            near = pltpu.make_async_copy(m_ref.at[item, section], om_ref, local.at[2])
            pl.when(mine & jnp.logical_not(here))(far.wait_send)
            pl.when(mine & here)(near.wait)

    @pl.when((s != 0) | (c != 0))
    def _():
        remote(m_ref.at[0, 0], om_ref, send.at[2, 0, 0], got_m.at[0], (s, place.d)).wait_recv()


def collect(sections, h, x, m):
    block = (2,) + h.shape[2:]
    return pl.pallas_call(
        functools.partial(collect_kernel, sections),
        name="collect_results",
        out_shape=(
            jax.ShapeDtypeStruct(block, BF),
            jax.ShapeDtypeStruct(block, BF),
            jax.ShapeDtypeStruct(m.shape[2:], F32),
        ),
        in_specs=[ANY, ANY, ANY],
        out_specs=(ANY, ANY, ANY),
        scratch_shapes=[
            pltpu.SemaphoreType.DMA((3, 2, sections)),
            pltpu.SemaphoreType.DMA((2,)),
            pltpu.SemaphoreType.DMA((2,)),
            pltpu.SemaphoreType.DMA((1,)),
            pltpu.SemaphoreType.DMA((3,)),
        ],
        compiler_params=pltpu.CompilerParams(collective_id=1, has_side_effects=True),
    )(h, x, m)


def key_bias(geometry, segment, length):
    mem, slot, tok, rows = geometry
    row = lax.broadcasted_iota(jnp.int32, (1, rows), 1)
    position = row - 2 * slot + segment * tok
    is_token = (row >= 2 * slot) & (row < 2 * slot + tok) & (position.astype(F32) < length)
    is_memory = (row < mem) | ((row >= slot) & (row < slot + mem))
    return jnp.where(is_token | is_memory, 0.0, -1e30)


def stacked_pair(pair):
    lane = lax.broadcasted_iota(jnp.int32, pair.shape, 1)
    zero = jnp.zeros_like(pair)
    return jnp.concatenate(
        [jnp.where(lane < HEAD, pair, zero), jnp.where(lane >= HEAD, pair, zero)], axis=0
    )


def folded_pair(both):
    half = both.shape[0] // 2
    lane = lax.broadcasted_iota(jnp.int32, (half, WIDE), 1)
    return jnp.where(lane < HEAD, both[:half], both[half:])


def pair_probs(queries, keys, bias, s_ref, p_ref, base=()):
    s_ref[...] = dot_nt(stacked_pair(queries * jnp.asarray(HEAD**-0.5, BF)), keys)
    total = s_ref.shape[0]
    for start in range(0, total, 2 * BLOCK):
        span = pl.ds(start, 2 * BLOCK)
        scores = s_ref[span, :] + bias
        exponent = jnp.exp(scores - jnp.max(scores, axis=-1, keepdims=True))
        inverse = 1.0 / jnp.sum(exponent, axis=-1, keepdims=True)
        p_ref[base + (span, slice(None))] = (exponent * inverse).astype(BF)


def normalized(rows):
    center = rows - jnp.mean(rows, axis=-1, keepdims=True)
    spread_of = jnp.mean(center * center, axis=-1, keepdims=True)
    scale = lax.rsqrt(spread_of + 1e-06)
    return center * scale, scale


def row_blocks(half):
    return [pl.ds(start, BLOCK) for start in range(0, half, BLOCK)]


def forward_kernel(
    segment,
    sections,
    geometry,
    x0_ref,
    memory_ref,
    lens_ref,
    w_qkv,
    w_proj,
    w_in,
    w_down,
    gain_one,
    shift_one,
    b_in,
    gain_two,
    shift_two,
    o_x,
    o_q,
    o_kv,
    o_att,
    o_nb,
    o_act,
    o_gp,
    o_s1,
    o_s2,
    o_hid,
    o_mem,
    vqkv,
    vproj,
    vin,
    vdown,
    xb,
    qb,
    kvb,
    attb,
    nbb,
    actb,
    gpb,
    preb,
    s1b,
    s2b,
    hb,
    nf,
    memb,
    s_tmp,
    p_tmp,
    wsem,
    xsem,
    osem,
    kv_send,
    kv_recv,
    h_send,
    h_recv,
    m_send,
    m_recv,
):
    place = Place(sections)
    s, c = place.s, place.c
    mem, slot, tok, rows = geometry
    half = rows // 2
    own = pl.ds(pl.multiple_of(c * half, BLOCK), half)
    last = sections - 1
    weights = [
        pltpu.make_async_copy(src, dst, wsem.at[k])
        for k, (src, dst) in enumerate(((w_qkv, vqkv), (w_proj, vproj), (w_in, vin), (w_down, vdown)))
    ]

    @pl.when(s == 0)
    def _():
        for item in range(2):
            pltpu.make_async_copy(x0_ref.at[item], xb.at[item], xsem.at[item]).start()

    for copy in weights:
        copy.start()
    barrier = pltpu.get_barrier_semaphore()
    pl.semaphore_signal(barrier, inc=1, device_id=(place.prev, place.d), device_id_type=MESH)
    pl.semaphore_signal(barrier, inc=1, device_id=(s, place.other), device_id_type=MESH)
    pl.semaphore_wait(barrier, 2)

    def outgoing(item):
        pairs = (
            (xb, o_x),
            (qb, o_q),
            (kvb, o_kv),
            (attb, o_att),
            (nbb, o_nb),
            (actb, o_act),
            (gpb, o_gp),
            (s1b, o_s1),
            (s2b, o_s2),
            (hb, o_hid),
        )
        return [
            pltpu.make_async_copy(src.at[item], dst.at[item], osem.at[item, k])
            for k, (src, dst) in enumerate(pairs)
        ]

    def handoff(item):
        return remote(hb.at[item], xb.at[item], h_send.at[item], h_recv.at[item], (place.next, place.d))

    def memory_move(item):
        return remote(
            hb.at[item, pl.ds(slot, slot)], memb.at[item], m_send.at[item], m_recv.at[item], (0, place.d)
        )

    def one_item(item):
        @pl.when(s == 0)
        def _():
            pltpu.make_async_copy(x0_ref.at[item], xb.at[item], xsem.at[item]).wait()
            if segment > 0:

                @pl.when(c == 0)
                def _():
                    xb[item, :slot] = memory_ref[item]
                    xb[item, slot : 2 * slot] = memory_ref[item]

        @pl.when(s > 0)
        def _():
            handoff(item).wait_recv()

        if item == 0:
            weights[0].wait()
        for k in range(2 * D // STEP):
            kvb[item, own, k * STEP : (k + 1) * STEP] = dot(
                xb[item], vqkv[:, D + k * STEP : D + (k + 1) * STEP]
            ).astype(BF)
        exchange = remote(
            kvb.at[item, own], kvb.at[item, own], kv_send.at[item], kv_recv.at[item], (s, place.other)
        )
        exchange.start()
        for k in range(D // STEP):
            qb[item, :, k * STEP : (k + 1) * STEP] = dot(
                xb[item], vqkv[:, k * STEP : (k + 1) * STEP]
            ).astype(BF)
        bias = key_bias(geometry, segment, lens_ref[item, :1, :1])
        exchange.wait_recv()
        for pair in range(PAIRS):
            span = slice(pair * WIDE, (pair + 1) * WIDE)
            pair_probs(qb[item, :, span], kvb[item, :, span], bias, s_tmp.at[pair % 2], p_tmp.at[pair % 2])
            values = kvb[item, :, D + pair * WIDE : D + (pair + 1) * WIDE]
            attb[item, :, span] = folded_pair(dot(p_tmp[pair % 2], values)).astype(BF)
        if item == 0:
            weights[1].wait()
        for k in range(D // STEP):
            span = slice(k * STEP, (k + 1) * STEP)
            s1b[item, :, span] = xb[item, :, span].astype(F32) + dot(attb[item], vproj[:, span])
        for span in row_blocks(half):
            z, _ = normalized(s1b[item, span, :])
            normed = z * gain_one[...] + shift_one[...]
            nf[span, :] = normed
            nbb[item, span, :] = normed.astype(BF)
        if item == 0:
            weights[2].wait()
        for k in range(FF // STEP):
            span = slice(k * STEP, (k + 1) * STEP)
            pre = dot(nbb[item], vin[:, span]) + b_in[:, span]
            preb[:, span] = pre
            actb[item, :, span] = (0.5 * pre * (1.0 + lax.erf(pre * 0.7071067811865476))).astype(BF)
        if item == 0:
            weights[3].wait()
        for k in range(D // STEP):
            span = slice(k * STEP, (k + 1) * STEP)
            s2b[item, :, span] = nf[:, span] + dot(actb[item], vdown[:, span])
        for span in row_blocks(half):
            z, _ = normalized(s2b[item, span, :])
            hb[item, span, :] = (z * gain_two[...] + shift_two[...]).astype(BF)

        @pl.when(s < last)
        def _():
            handoff(item).start()

        if segment == 0:

            @pl.when((s == last) & (c == 0))
            def _():
                memory_move(item).start()

        for start in range(0, half, BLOCK):
            span = pl.ds(start, BLOCK)
            pre = preb[span, :]
            density = jnp.exp(-0.5 * pre * pre) * 0.3989422804014327
            slope = 0.5 * (1.0 + lax.erf(pre * 0.7071067811865476)) + pre * density
            gpb[item, span, :] = slope.astype(BF)
        for copy in outgoing(item):
            copy.start()
        exchange.wait_send()

    one_item(0)
    one_item(1)

    for item in range(2):

        @pl.when(s < last)
        def _():
            handoff(item).wait_send()

        if segment == 0:

            @pl.when((s == last) & (c == 0))
            def _():
                memory_move(item).wait_send()

            @pl.when((s == 0) & (c == 0))
            def _():
                memory_move(item).wait_recv()
                out = pltpu.make_async_copy(memb.at[item], o_mem.at[item], xsem.at[item])
                out.start()
                out.wait()

        for copy in outgoing(item):
            copy.wait()


def forward(segment, sections, geometry, collective, x0, memory, lens, weights):
    mem, slot, tok, rows = geometry
    half = rows // 2

    def pair(width, kind, height=half):
        return jax.ShapeDtypeStruct((2, height, width), kind)

    outs = (
        pair(D, BF),
        pair(D, BF),
        pair(2 * D, BF, rows),
        pair(D, BF),
        pair(D, BF),
        pair(FF, BF),
        pair(FF, BF),
        pair(D, F32),
        pair(D, F32),
        pair(D, BF),
        pair(D, BF, slot),
    )
    dma = pltpu.SemaphoreType.DMA
    return pl.pallas_call(
        functools.partial(forward_kernel, segment, sections, geometry),
        name="forward_layer",
        out_shape=outs,
        in_specs=[ANY, VMEM, VMEM] + [ANY] * 4 + [VMEM] * 5,
        out_specs=(ANY,) * len(outs),
        scratch_shapes=[
            pltpu.VMEM((D, 3 * D), BF),
            pltpu.VMEM((D, D), BF),
            pltpu.VMEM((D, FF), BF),
            pltpu.VMEM((FF, D), BF),
            pltpu.VMEM((2, half, D), BF),
            pltpu.VMEM((2, half, D), BF),
            pltpu.VMEM((2, rows, 2 * D), BF),
            pltpu.VMEM((2, half, D), BF),
            pltpu.VMEM((2, half, D), BF),
            pltpu.VMEM((2, half, FF), BF),
            pltpu.VMEM((2, half, FF), BF),
            pltpu.VMEM((half, FF), F32),
            pltpu.VMEM((2, half, D), F32),
            pltpu.VMEM((2, half, D), F32),
            pltpu.VMEM((2, half, D), BF),
            pltpu.VMEM((half, D), F32),
            pltpu.VMEM((2, slot, D), BF),
            pltpu.VMEM((2, rows, rows), F32),
            pltpu.VMEM((2, rows, rows), BF),
            dma((4,)),
            dma((2,)),
            dma((2, 10)),
            dma((2,)),
            dma((2,)),
            dma((2,)),
            dma((2,)),
            dma((2,)),
            dma((2,)),
        ],
        compiler_params=pltpu.CompilerParams(
            collective_id=collective, has_side_effects=True, vmem_limit_bytes=VMEM_LIMIT
        ),
    )(x0, memory, lens, *weights)


def backward_kernel(
    segment,
    sections,
    segments,
    geometry,
    g0_ref,
    carry_ref,
    lens_ref,
    r_q,
    r_kv,
    r_gp,
    r_s1,
    r_s2,
    w_qkv,
    w_proj,
    w_in,
    w_down,
    gain_one,
    gain_two,
    o_dpj,
    o_dbr,
    o_dpre,
    o_dfe,
    o_dx,
    o_mg,
    o_carry,
    o_small,
    vqkv,
    vproj,
    vin,
    vdown,
    gb,
    qb,
    kvb,
    gpb,
    z1b,
    z2b,
    r1b,
    r2b,
    pf,
    work,
    dsec,
    dfe,
    dpre,
    dbr,
    da,
    s_tmp,
    ds_tmp,
    dkv,
    dkv_in,
    dpj,
    dxb,
    mgb,
    carb,
    wsem,
    rsem,
    gsem,
    osem,
    kv_send,
    kv_recv,
    h_send,
    h_recv,
    m_send,
    m_recv,
):
    place = Place(sections)
    s, c = place.s, place.c
    mem, slot, tok, rows = geometry
    half = rows // 2
    own = pl.ds(pl.multiple_of(c * half, BLOCK), half)
    theirs = pl.ds(pl.multiple_of((1 - c) * half, BLOCK), half)
    last = sections - 1
    weights = [
        pltpu.make_async_copy(src, dst, wsem.at[k])
        for k, (src, dst) in enumerate(((w_down, vdown), (w_in, vin), (w_proj, vproj), (w_qkv, vqkv)))
    ]

    def residuals(item):
        pairs = ((r_q, qb), (r_kv, kvb), (r_s2, z2b), (r_gp, gpb), (r_s1, z1b))
        return [
            pltpu.make_async_copy(src.at[item], dst.at[item], rsem.at[item, k])
            for k, (src, dst) in enumerate(pairs)
        ]

    def seed_copy(item):
        return pltpu.make_async_copy(g0_ref.at[item], gb.at[item], gsem.at[item])

    for item in range(2):
        for copy in residuals(item):
            copy.start()
        if item == 0:
            for copy in weights:
                copy.start()
        pl.when(s == last)(seed_copy(item).start)
    o_small[...] = jnp.zeros_like(o_small)

    barrier = pltpu.get_barrier_semaphore()
    pl.semaphore_signal(barrier, inc=1, device_id=(place.next, place.d), device_id_type=MESH)
    pl.semaphore_signal(barrier, inc=1, device_id=(s, place.other), device_id_type=MESH)
    pl.semaphore_wait(barrier, 2)

    def outgoing(item):
        pairs = (
            (dpj, o_dpj),
            (dbr, o_dbr),
            (dpre, o_dpre),
            (dfe, o_dfe),
            (dxb.at[item], o_dx),
        )
        return [
            pltpu.make_async_copy(src, dst.at[item], osem.at[item, k])
            for k, (src, dst) in enumerate(pairs)
        ]

    def handoff(item):
        return remote(dxb.at[item], gb.at[item], h_send.at[item], h_recv.at[item], (place.prev, place.d))

    def carry_move(item):
        return remote(mgb.at[item], carb.at[item], m_send.at[item], m_recv.at[item], (last, place.d))

    def prologue(item):
        for copy in residuals(item):
            copy.wait()
        bias = key_bias(geometry, segment, lens_ref[item, :1, :1])
        for z_ref, r_ref in ((z2b, r2b), (z1b, r1b)):
            for span in row_blocks(half):
                z, scale = normalized(z_ref[item, span, :])
                z_ref[item, span, :] = z
                r_ref[item, span, :] = jnp.broadcast_to(scale, (BLOCK, 128))
        for pair in range(PAIRS):
            span = slice(pair * WIDE, (pair + 1) * WIDE)
            pair_probs(
                qb[item, :, span], kvb[item, :, span], bias, s_tmp.at[pair % 2], pf, (item, pair)
            )

    def norm_back(g, z, scale, gain):
        scaled = g * gain
        mean_u = jnp.mean(scaled, axis=-1, keepdims=True)
        mean_uz = jnp.mean(scaled * z, axis=-1, keepdims=True)
        return (scaled - mean_u - z * mean_uz) * scale

    def folded_rows(value):
        return value[: BLOCK // 2] + value[BLOCK // 2 :]

    def main(item):
        @pl.when(s == last)
        def _():
            seed_copy(item).wait()
            length = lens_ref[item, :1, :1]
            for index, span in enumerate(row_blocks(half)):
                row = c * half + index * BLOCK + lax.broadcasted_iota(jnp.int32, (BLOCK, D), 0)
                position = row - 2 * slot + segment * tok
                valid = (row >= 2 * slot) & (position.astype(F32) < length)
                work[span, :] = jnp.where(valid, gb[item, span, :].astype(F32), 0.0)
            if segment < segments - 1:

                @pl.when(c == 0)
                def _():
                    work[slot : 2 * slot, :] = carry_ref[item]

        @pl.when(s < last)
        def _():
            handoff(item).wait_recv()
            for span in row_blocks(half):
                work[span, :] = gb[item, span, :].astype(F32)

        if item > 0:
            for copy in outgoing(item - 1):
                copy.wait()
        gain_sum = jnp.zeros((BLOCK // 2, D), F32)
        shift_sum = jnp.zeros((BLOCK // 2, D), F32)
        for span in row_blocks(half):
            g = work[span, :]
            z = z2b[item, span, :]
            back = norm_back(g, z, r2b[item, span, :1], gain_two[...])
            dsec[span, :] = back
            dfe[span, :] = back.astype(BF)
            gain_sum += folded_rows(g * z)
            shift_sum += folded_rows(g)
        o_small[2:3, :] += jnp.sum(gain_sum, axis=0, keepdims=True)
        o_small[3:4, :] += jnp.sum(shift_sum, axis=0, keepdims=True)
        if item == 0:
            weights[0].wait()
        for k in range(FF // STEP):
            span = slice(k * STEP, (k + 1) * STEP)
            pre = (dot_nt(dfe[...], vdown[span, :]) * gpb[item, :, span].astype(F32)).astype(BF)
            dpre[:, span] = pre
            start = (k * STEP) % D
            row = 4 + (k * STEP) // D
            o_small[row : row + 1, start : start + STEP] += jnp.sum(pre.astype(F32), axis=0, keepdims=True)
        if item == 0:
            weights[1].wait()
        for k in range(D // STEP):
            span = slice(k * STEP, (k + 1) * STEP)
            work[:, span] = dsec[:, span] + dot_nt(dpre[...], vin[span, :])
        gain_sum = jnp.zeros((BLOCK // 2, D), F32)
        shift_sum = jnp.zeros((BLOCK // 2, D), F32)
        for span in row_blocks(half):
            g = work[span, :]
            z = z1b[item, span, :]
            back = norm_back(g, z, r1b[item, span, :1], gain_one[...])
            work[span, :] = back
            dbr[span, :] = back.astype(BF)
            gain_sum += folded_rows(g * z)
            shift_sum += folded_rows(g)
        o_small[0:1, :] += jnp.sum(gain_sum, axis=0, keepdims=True)
        o_small[1:2, :] += jnp.sum(shift_sum, axis=0, keepdims=True)
        if item == 0:
            weights[2].wait()
        for k in range(D // STEP):
            span = slice(k * STEP, (k + 1) * STEP)
            da[:, span] = dot_nt(dbr[...], vproj[span, :]).astype(BF)
        sends = []
        for pair in range(PAIRS):
            span = slice(pair * WIDE, (pair + 1) * WIDE)
            keys = kvb[item, :, span]
            values = kvb[item, :, D + pair * WIDE : D + (pair + 1) * WIDE]
            da2 = stacked_pair(da[:, span])
            q2 = stacked_pair(qb[item, :, span] * jnp.asarray(HEAD**-0.5, BF))
            dp_ref = s_tmp.at[pair % 2]
            ds_ref = ds_tmp.at[pair % 2]
            dp_ref[...] = dot_nt(da2, values)
            for start in range(0, rows, 2 * BLOCK):
                block = pl.ds(start, 2 * BLOCK)
                probs = pf[item, pair, block, :].astype(F32)
                grads = dp_ref[block, :]
                total = jnp.sum(probs * grads, axis=-1, keepdims=True)
                ds_ref[block, :] = (probs * (grads - total)).astype(BF)
            dkv[pair, :, :WIDE] = dot_tn(ds_ref[...], q2)
            dkv[pair, :, WIDE:] = dot_tn(pf[item, pair], da2)
            move = remote(
                dkv.at[pair, theirs],
                dkv_in.at[item, pair],
                kv_send.at[item, pair],
                kv_recv.at[item, pair],
                (s, place.other),
            )
            move.start()
            sends.append(move)
            dpj[:, span] = (folded_pair(dot(ds_ref[...], keys)) * HEAD**-0.5).astype(BF)
        if item == 0:
            weights[3].wait()
        for pair in range(PAIRS):
            sends[pair].wait_recv()
            for part in range(2):
                start = (part + 1) * D + pair * WIDE
                lanes = slice(part * WIDE, (part + 1) * WIDE)
                dpj[:, start : start + WIDE] = (
                    dkv[pair, own, lanes] + dkv_in[item, pair, :, lanes]
                ).astype(BF)
        for k in range(D // STEP):
            span = slice(k * STEP, (k + 1) * STEP)
            dxb[item, :, span] = (work[:, span] + dot_nt(dpj[...], vqkv[span, :])).astype(BF)

        pl.when(s > 0)(handoff(item).start)

        @pl.when((s == 0) & (c == 0))
        def _():
            mgb[item] = dxb[item, :slot].astype(F32) + dxb[item, slot : 2 * slot].astype(F32)
            if segment > 0:
                carry_move(item).start()

        for copy in outgoing(item):
            copy.start()
        for move in sends:
            move.wait_send()

    prologue(0)
    pl.when(s < last)(functools.partial(prologue, 1))
    main(0)
    pl.when(s == last)(functools.partial(prologue, 1))
    main(1)

    for item in range(2):
        pl.when(s > 0)(handoff(item).wait_send)
        if item == 1:
            for copy in outgoing(item):
                copy.wait()

        @pl.when((s == 0) & (c == 0))
        def _():
            out = pltpu.make_async_copy(mgb.at[item], o_mg.at[item], gsem.at[item])
            out.start()
            out.wait()
            if segment > 0:
                carry_move(item).wait_send()

        if segment > 0:

            @pl.when((s == last) & (c == 0))
            def _():
                carry_move(item).wait_recv()
                out = pltpu.make_async_copy(carb.at[item], o_carry.at[item], gsem.at[item])
                out.start()
                out.wait()


def backward(segment, sections, segments, geometry, collective, g0, carry, lens, kept, weights):
    mem, slot, tok, rows = geometry
    half = rows // 2

    def pair(width, kind, height=half):
        return jax.ShapeDtypeStruct((2, height, width), kind)

    outs = (
        pair(3 * D, BF),
        pair(D, BF),
        pair(FF, BF),
        pair(D, BF),
        pair(D, BF),
        pair(D, F32, slot),
        pair(D, F32, slot),
        jax.ShapeDtypeStruct((8, D), F32),
    )
    dma = pltpu.SemaphoreType.DMA
    return pl.pallas_call(
        functools.partial(backward_kernel, segment, sections, segments, geometry),
        name="backward_layer",
        out_shape=outs,
        in_specs=[ANY, VMEM, VMEM] + [ANY] * 5 + [ANY] * 4 + [VMEM] * 2,
        out_specs=(ANY,) * 7 + (VMEM,),
        scratch_shapes=[
            pltpu.VMEM((D, 3 * D), BF),
            pltpu.VMEM((D, D), BF),
            pltpu.VMEM((D, FF), BF),
            pltpu.VMEM((FF, D), BF),
            pltpu.VMEM((2, half, D), BF),
            pltpu.VMEM((2, half, D), BF),
            pltpu.VMEM((2, rows, 2 * D), BF),
            pltpu.VMEM((2, half, FF), BF),
            pltpu.VMEM((2, half, D), F32),
            pltpu.VMEM((2, half, D), F32),
            pltpu.VMEM((2, half, 128), F32),
            pltpu.VMEM((2, half, 128), F32),
            pltpu.VMEM((2, PAIRS, rows, rows), BF),
            pltpu.VMEM((half, D), F32),
            pltpu.VMEM((half, D), F32),
            pltpu.VMEM((half, D), BF),
            pltpu.VMEM((half, FF), BF),
            pltpu.VMEM((half, D), BF),
            pltpu.VMEM((half, D), BF),
            pltpu.VMEM((2, rows, rows), F32),
            pltpu.VMEM((2, rows, rows), BF),
            pltpu.VMEM((PAIRS, rows, 2 * WIDE), F32),
            pltpu.VMEM((2, PAIRS, half, 2 * WIDE), F32),
            pltpu.VMEM((half, 3 * D), BF),
            pltpu.VMEM((2, half, D), BF),
            pltpu.VMEM((2, slot, D), F32),
            pltpu.VMEM((2, slot, D), F32),
            dma((4,)),
            dma((2, 5)),
            dma((2,)),
            dma((2, 5)),
            dma((2, PAIRS)),
            dma((2, PAIRS)),
            dma((2,)),
            dma((2,)),
            dma((2,)),
            dma((2,)),
        ],
        compiler_params=pltpu.CompilerParams(
            collective_id=collective, has_side_effects=True, vmem_limit_bytes=VMEM_LIMIT
        ),
    )(g0, carry, lens, *kept, *weights)


def on_device(
    sections,
    inputs,
    out_grad,
    memory,
    lengths,
    w_qkv,
    w_proj,
    gain_one,
    shift_one,
    w_in,
    b_in,
    w_down,
    gain_two,
    shift_two,
):
    segs, tok, part = inputs.shape[1:]
    mem = memory.shape[1]
    slot = -(-mem // BLOCK) * BLOCK
    rows = -(-(2 * slot + tok) // (2 * BLOCK)) * 2 * BLOCK
    half = rows // 2
    geometry = (mem, slot, tok, rows)
    back_pad = rows - 2 * slot - tok

    def in_slots(array):
        return jnp.pad(array, ((0, 0), (2 * slot, back_pad), (0, 0)))

    def halves(array):
        return array.reshape(segs, 2, half, part).transpose(1, 0, 2, 3)

    tokens = in_slots(inputs[0])
    tokens = tokens.at[0, :mem].set(memory[0]).at[0, slot : slot + mem].set(memory[0])
    cotangent = in_slots(out_grad[0])
    length_tile = jnp.broadcast_to(lengths.astype(F32), (8, 128))
    x_all, g_all, lens = spread(sections, halves(tokens), halves(cotangent), length_tile)

    def of_segment(array, segment):
        return array[:, :, segment].transpose(0, 2, 1, 3).reshape(2, half, D)

    matrices = (w_qkv[0], w_proj[0], w_in[0], w_down[0])
    forward_weights = matrices + (gain_one, shift_one, b_in, gain_two, shift_two)
    backward_weights = matrices + (gain_one, gain_two)
    carried = jnp.zeros((2, slot, D), BF)
    kept = []
    for segment in range(segs):
        kept.append(
            forward(
                segment, sections, geometry, 2 + segment, of_segment(x_all, segment), carried, lens, forward_weights
            )
        )
        carried = kept[-1][-1]
    grads = [None] * segs
    carry = jnp.zeros((2, slot, D), F32)
    for segment in reversed(range(segs)):
        x, q, kv, att, nb, act, gp, s1, s2, hid, _ = kept[segment]
        grads[segment] = backward(
            segment,
            sections,
            segs,
            geometry,
            2 + segs + segment,
            of_segment(g_all, segment),
            carry,
            lens,
            (q, kv, gp, s1, s2),
            backward_weights,
        )
        carry = grads[segment][6]

    def per_owner(arrays):
        stacked = jnp.stack(arrays, axis=1)
        return stacked.reshape(2, segs, half, sections, part).transpose(0, 3, 1, 2, 4)

    memory_term = grads[0][5].reshape(2, slot, sections, part).transpose(0, 2, 1, 3)
    out_parts, in_parts, memory_part = collect(
        sections, per_owner([k[9] for k in kept]), per_owner([g[4] for g in grads]), memory_term
    )

    def owned(parts):
        return parts.transpose(1, 0, 2, 3).reshape(segs, rows, part)[:, 2 * slot : 2 * slot + tok]

    position = jnp.arange(segs * tok, dtype=jnp.int32).reshape(segs, tok)
    token_valid = position < lengths[0]
    outputs = jnp.where(token_valid[:, :, None], owned(out_parts), jnp.zeros((), BF))
    input_grad = owned(in_parts)
    memory_grad = memory_part[:mem]

    def weight_grad(left, right):
        lefts = jnp.concatenate([k.reshape(2 * half, -1) for k in left])
        rights = jnp.concatenate([g.reshape(2 * half, -1) for g in right])
        full = jnp.einsum("rd,re->de", lefts, rights, preferred_element_type=F32)
        return lax.psum_scatter(full.astype(BF), "dp", scatter_dimension=0, tiled=True).astype(F32)

    def kept_of(index):
        return [k[index] for k in kept]

    def grad_of(index):
        return [g[index] for g in grads]

    d_qkv = weight_grad(kept_of(0), grad_of(0))
    d_proj = weight_grad(kept_of(3), grad_of(1))
    d_in = weight_grad(kept_of(4), grad_of(2))
    d_down = weight_grad(kept_of(5), grad_of(3))
    small = lax.psum(sum(g[7] for g in grads), "dp")
    devices = lax.axis_size("dp")
    index = lax.axis_index("dp")

    def vector(value):
        size = value.size // devices
        return lax.dynamic_slice_in_dim(value.reshape(-1), index * size, size, 0)[None]

    return (
        outputs[None],
        input_grad[None],
        memory_grad[None],
        d_qkv[None],
        d_proj[None],
        vector(small[0]),
        vector(small[1]),
        d_in[None],
        vector(small[4:8]),
        d_down[None],
        vector(small[2]),
        vector(small[3]),
    )


def solution(mesh):
    return jax.shard_map(
        functools.partial(on_device, mesh.shape["section"]),
        mesh=mesh,
        in_specs=(
            P("dp", None, None, "section"),
            P("dp", None, None, "section"),
            P("dp", None, "section"),
            P("dp"),
            P("section", None, None),
            P("section", None, None),
            P("section", None),
            P("section", None),
            P("section", None, None),
            P("section", None),
            P("section", None, None),
            P("section", None),
            P("section", None),
        ),
        out_specs=(
            P("dp", None, None, "section"),
            P("dp", None, None, "section"),
            P("dp", None, "section"),
            P("section", "dp", None),
            P("section", "dp", None),
            P("section", "dp"),
            P("section", "dp"),
            P("section", "dp", None),
            P("section", "dp"),
            P("section", "dp", None),
            P("section", "dp"),
            P("section", "dp"),
        ),
        check_vma=False,
    )
```

```python
import functools

import jax
import jax.numpy as jnp
from jax import lax
from jax.experimental import pallas as pl
from jax.experimental.pallas import tpu as pltpu
from jax.sharding import PartitionSpec as P

D = 768
H = 12
HEAD = 64
FF = 3072
PAIRS = H // 2
WIDE = 2 * HEAD
STEP = 256
BLOCK = 16
BF = jnp.bfloat16
F32 = jnp.float32
MESH = pl.DeviceIdType.MESH
ANY = pl.BlockSpec(memory_space=pl.ANY)
VMEM = pl.BlockSpec(memory_space=pltpu.VMEM)
VMEM_LIMIT = 63 * 1024 * 1024


def dot(a, b):
    return jnp.dot(a, b, preferred_element_type=F32)


def dot_nt(a, b):
    return lax.dot_general(a, b, (((1,), (1,)), ((), ())), preferred_element_type=F32)


def dot_tn(a, b):
    return lax.dot_general(a, b, (((0,), (0,)), ((), ())), preferred_element_type=F32)


def cols(index):
    return pl.ds(index * STEP, STEP)


def remote(src, dst, send, recv, target):
    return pltpu.make_async_remote_copy(
        src_ref=src, dst_ref=dst, send_sem=send, recv_sem=recv, device_id=target, device_id_type=MESH
    )


class Place:
    def __init__(self, sections):
        self.s = lax.axis_index("section")
        self.d = lax.axis_index("dp")
        self.c = lax.rem(self.d, 2)
        self.base = self.d - self.c
        self.other = self.base + 1 - self.c
        self.next = lax.rem(self.s + 1, sections)
        self.prev = lax.rem(self.s + sections - 1, sections)


def plane_barrier(place, sections):
    barrier = pltpu.get_barrier_semaphore()
    for section in range(sections):
        for core in range(2):

            @pl.when((place.s != section) | (place.c != core))
            def _():
                pl.semaphore_signal(
                    barrier, inc=1, device_id=(section, place.base + core), device_id_type=MESH
                )

    pl.semaphore_wait(barrier, 2 * sections - 1)


def spread_kernel(sections, a_ref, g_ref, len_ref, x_ref, gr_ref, lens_ref, send, got_x, got_g, got_l, local):
    place = Place(sections)
    s, c = place.s, place.c
    plane_barrier(place, sections)
    moves = []
    for core in range(2):
        for which, (src, dst, target, got) in enumerate(
            ((a_ref, x_ref, 0, got_x), (g_ref, gr_ref, sections - 1, got_g))
        ):
            here = (s == target) & (c == core)
            slot = 2 * which + core
            far = remote(
                src.at[core], dst.at[c, s], send.at[slot], got.at[c, s], (target, place.base + core)
            )
            near = pltpu.make_async_copy(src.at[core], dst.at[c, s], local.at[which])
            moves.append((here, far, near))
    for here, far, near in moves:
        pl.when(jnp.logical_not(here))(far.start)
        pl.when(here)(near.start)
    far_len = remote(len_ref, lens_ref.at[c], send.at[4], got_l.at[0], (s, place.other))
    near_len = pltpu.make_async_copy(len_ref, lens_ref.at[c], local.at[2])
    far_len.start()
    near_len.start()
    for here, far, near in moves:
        pl.when(jnp.logical_not(here))(far.wait_send)
        pl.when(here)(near.wait)
    for which, (src, dst, target, got) in enumerate(
        ((a_ref, x_ref, 0, got_x), (g_ref, gr_ref, sections - 1, got_g))
    ):
        for core in range(2):
            for section in range(sections):

                @pl.when((s == target) & ((c != core) | (s != section)))
                def _():
                    remote(
                        src.at[0], dst.at[core, section], send.at[0], got.at[core, section], (s, place.d)
                    ).wait_recv()

    far_len.wait_send()
    near_len.wait()
    remote(len_ref, lens_ref.at[1 - c], send.at[4], got_l.at[0], (s, place.other)).wait_recv()


def spread(sections, a, g, length_tile):
    half = a.shape[2]
    block = (2, sections) + a.shape[1:]
    return pl.pallas_call(
        functools.partial(spread_kernel, sections),
        name="spread_items",
        out_shape=(
            jax.ShapeDtypeStruct(block, BF),
            jax.ShapeDtypeStruct(block, BF),
            jax.ShapeDtypeStruct((2, 8, 128), F32),
        ),
        in_specs=[ANY, ANY, ANY],
        out_specs=(ANY, ANY, ANY),
        scratch_shapes=[
            pltpu.SemaphoreType.DMA((5,)),
            pltpu.SemaphoreType.DMA((2, sections)),
            pltpu.SemaphoreType.DMA((2, sections)),
            pltpu.SemaphoreType.DMA((1,)),
            pltpu.SemaphoreType.DMA((3,)),
        ],
        compiler_params=pltpu.CompilerParams(collective_id=0, has_side_effects=True),
    )(a, g, length_tile)


def collect_kernel(sections, h_ref, x_ref, m_ref, oh_ref, ox_ref, om_ref, send, got_h, got_x, got_m, local):
    place = Place(sections)
    s, c = place.s, place.c
    plane_barrier(place, sections)
    last = sections - 1
    jobs = (
        (h_ref, oh_ref, last, got_h, 0),
        (x_ref, ox_ref, 0, got_x, 1),
    )
    for src, dst, origin, got, which in jobs:
        for item in range(2):
            for section in range(sections):
                here = (s == section) & (c == item)
                mine = s == origin
                far = remote(
                    src.at[item, section], dst.at[c], send.at[which, item, section], got.at[c], (section, place.base + item)
                )
                near = pltpu.make_async_copy(src.at[item, section], dst.at[c], local.at[which])
                pl.when(mine & jnp.logical_not(here))(far.start)
                pl.when(mine & here)(near.start)
    for item in range(2):
        for section in range(sections):
            here = (s == section) & (c == item)
            mine = (s == 0) & (c == 0)
            far = remote(
                m_ref.at[item, section], om_ref, send.at[2, item, section], got_m.at[0], (section, place.base + item)
            )
            near = pltpu.make_async_copy(m_ref.at[item, section], om_ref, local.at[2])
            pl.when(mine & jnp.logical_not(here))(far.start)
            pl.when(mine & here)(near.start)
    for src, dst, origin, got, which in jobs:
        for item in range(2):
            for section in range(sections):
                here = (s == section) & (c == item)
                mine = s == origin
                far = remote(
                    src.at[item, section], dst.at[c], send.at[which, item, section], got.at[c], (section, place.base + item)
                )
                near = pltpu.make_async_copy(src.at[item, section], dst.at[c], local.at[which])
                pl.when(mine & jnp.logical_not(here))(far.wait_send)
                pl.when(mine & here)(near.wait)
        for core in range(2):

            @pl.when((s != origin) | (c != core))
            def _():
                remote(
                    src.at[0, 0], dst.at[core], send.at[which, 0, 0], got.at[core], (s, place.d)
                ).wait_recv()

    for item in range(2):
        for section in range(sections):
            here = (s == section) & (c == item)
            mine = (s == 0) & (c == 0)
            far = remote(
                m_ref.at[item, section], om_ref, send.at[2, item, section], got_m.at[0], (section, place.base + item)
            )
            near = pltpu.make_async_copy(m_ref.at[item, section], om_ref, local.at[2])
            pl.when(mine & jnp.logical_not(here))(far.wait_send)
            pl.when(mine & here)(near.wait)

    @pl.when((s != 0) | (c != 0))
    def _():
        remote(m_ref.at[0, 0], om_ref, send.at[2, 0, 0], got_m.at[0], (s, place.d)).wait_recv()


def collect(sections, h, x, m):
    block = (2,) + h.shape[2:]
    return pl.pallas_call(
        functools.partial(collect_kernel, sections),
        name="collect_results",
        out_shape=(
            jax.ShapeDtypeStruct(block, BF),
            jax.ShapeDtypeStruct(block, BF),
            jax.ShapeDtypeStruct(m.shape[2:], F32),
        ),
        in_specs=[ANY, ANY, ANY],
        out_specs=(ANY, ANY, ANY),
        scratch_shapes=[
            pltpu.SemaphoreType.DMA((3, 2, sections)),
            pltpu.SemaphoreType.DMA((2,)),
            pltpu.SemaphoreType.DMA((2,)),
            pltpu.SemaphoreType.DMA((1,)),
            pltpu.SemaphoreType.DMA((3,)),
        ],
        compiler_params=pltpu.CompilerParams(collective_id=1, has_side_effects=True),
    )(h, x, m)


def key_bias(geometry, segment, length, shape, dim):
    mem, slot, tok, rows = geometry
    row = lax.broadcasted_iota(jnp.int32, shape, dim)
    position = row - 2 * slot + segment * tok
    is_token = (row >= 2 * slot) & (row < 2 * slot + tok) & (position.astype(F32) < length)
    is_memory = (row < mem) | ((row >= slot) & (row < slot + mem))
    return jnp.where(is_token | is_memory, 0.0, -1e30)


def stacked_pair(pair):
    lane = lax.broadcasted_iota(jnp.int32, pair.shape, 1)
    zero = jnp.zeros_like(pair)
    return jnp.concatenate(
        [jnp.where(lane < HEAD, pair, zero), jnp.where(lane >= HEAD, pair, zero)], axis=0
    )


def folded_pair(both):
    half = both.shape[0] // 2
    lane = lax.broadcasted_iota(jnp.int32, (half, WIDE), 1)
    return jnp.where(lane < HEAD, both[:half], both[half:])


def scaled_queries(queries):
    return stacked_pair(queries * jnp.asarray(HEAD**-0.5, BF))


def normalized(rows):
    center = rows - jnp.mean(rows, axis=-1, keepdims=True)
    spread_of = jnp.mean(center * center, axis=-1, keepdims=True)
    scale = lax.rsqrt(spread_of + 1e-06)
    return center * scale, scale


def pieces(width, step=STEP):
    return [slice(start, start + step) for start in range(0, width, step)]


def row_chunks(half):
    first = half // 2 // BLOCK * BLOCK
    return ((0, first), (first, half - first))


def row_blocks(start, size):
    return [pl.ds(start + offset, BLOCK) for offset in range(0, size, BLOCK)]


def pair_span(pair, offset=0):
    return slice(offset + pair * WIDE, offset + (pair + 1) * WIDE)


def forward_kernel(
    sections,
    segments,
    geometry,
    x0_ref,
    lens_ref,
    w_qkv,
    w_proj,
    w_in,
    w_down,
    gain_one,
    shift_one,
    b_in,
    gain_two,
    shift_two,
    o_x,
    o_q,
    o_kv,
    o_att,
    o_nb,
    o_act,
    o_gp,
    o_s1,
    o_s2,
    o_hid,
    t_qkv,
    t_proj,
    t_in,
    t_down,
    vqkv,
    vproj,
    vin,
    vdown,
    xb,
    kvb,
    qb,
    attb,
    nbb,
    actb,
    gpb,
    s1b,
    s2b,
    hb,
    preb,
    nf,
    memb,
    s_tmp,
    probs,
    turned,
    wsem,
    xsem,
    osem,
    kv_send,
    kv_recv,
    h_send,
    h_recv,
    m_send,
    m_recv,
    tsem,
):
    place = Place(sections)
    s, c = place.s, place.c
    mem, slot, tok, rows = geometry
    half = rows // 2
    last = sections - 1
    steps = 2 * segments
    chunks = row_chunks(half)
    early = s >= 2
    weights = [
        pltpu.make_async_copy(src, dst, wsem.at[k])
        for k, (src, dst) in enumerate(((w_qkv, vqkv), (w_proj, vproj), (w_in, vin), (w_down, vdown)))
    ]

    @pl.when(s == 0)
    def _():
        for step in range(steps):
            pltpu.make_async_copy(x0_ref.at[step], xb.at[step], xsem.at[step]).start()

    for copy in weights:
        copy.start()
    barrier = pltpu.get_barrier_semaphore()
    pl.semaphore_signal(barrier, inc=1, device_id=(place.prev, place.d), device_id_type=MESH)
    pl.semaphore_signal(barrier, inc=1, device_id=(s, place.other), device_id_type=MESH)
    pl.semaphore_wait(barrier, 2)

    def outgoing(step):
        side = lax.rem(step, 2)
        pairs = (
            (xb.at[step], o_x),
            (kvb.at[step], o_kv),
            (qb.at[side], o_q),
            (attb.at[side], o_att),
            (nbb.at[side], o_nb),
            (actb.at[side], o_act),
            (gpb.at[side], o_gp),
            (s1b.at[side], o_s1),
            (s2b.at[side], o_s2),
            (hb.at[side], o_hid),
        )
        return [
            pltpu.make_async_copy(src, dst.at[step], osem.at[side, k])
            for k, (src, dst) in enumerate(pairs)
        ]

    def handoff(step, index):
        start, size = chunks[index]
        side = lax.rem(step, 2)
        span = pl.ds(start, size)
        return remote(
            hb.at[side, span],
            xb.at[step, span],
            h_send.at[side, index],
            h_recv.at[step, index],
            (place.next, place.d),
        )

    def memory_move(step):
        side = lax.rem(step, 2)
        return remote(
            hb.at[side, pl.ds(slot, slot)], memb.at[step], m_send.at[side], m_recv.at[step], (0, place.d)
        )

    def exchange(step, index):
        start, size = chunks[index]
        span = pl.ds(pl.multiple_of(c * half + start, BLOCK), size)
        return remote(
            kvb.at[step, span],
            kvb.at[step, span],
            kv_send.at[index],
            kv_recv.at[step, index],
            (s, place.other),
        )

    def settle(step):
        @pl.when(s < last)
        def _():
            for index in range(len(chunks)):
                handoff(step, index).wait_send()

        @pl.when((s == last) & (c == 0) & (step < steps - 2))
        def _():
            memory_move(step).wait_send()

        for copy in outgoing(step):
            copy.wait()

    def turn_weights():
        @pl.when(early)
        def _():
            for copy in weights:
                copy.wait()

        blocks = []
        for src, dst in ((vqkv, t_qkv), (vproj, t_proj), (vin, t_in), (vdown, t_down)):
            for block in range(src.shape[0] * src.shape[1] // (D * D)):
                span = pl.ds(block * D, D)
                if src.shape[0] == D:
                    blocks.append((src, (slice(None), span), dst.at[span]))
                else:
                    blocks.append((src, (span, slice(None)), dst.at[:, span]))
        moves = []
        for index, (src, where, dst) in enumerate(blocks):
            spot = index % 3
            if index >= 3:
                moves[index - 3].wait()
            turned[spot] = jnp.transpose(src[where])
            moves.append(pltpu.make_async_copy(turned.at[spot], dst, tsem.at[spot]))
            moves[-1].start()
        for move in moves[-3:]:
            move.wait()

    def one_step(step, state):
        pl.when(step == jnp.where(early, 0, steps))(turn_weights)
        pl.when(step < steps)(lambda: compute_step(step))
        return state

    def compute_step(step):
        side = lax.rem(step, 2)
        segment = lax.div(step, 2)
        first = (step == 0) & jnp.logical_not(early)

        @pl.when(s == 0)
        def _():
            pltpu.make_async_copy(x0_ref.at[step], xb.at[step], xsem.at[step]).wait()

            @pl.when((c == 0) & (step >= 2))
            def _():
                memory_move(step - 2).wait_recv()
                xb[step, :slot] = memb[step - 2]
                xb[step, slot : 2 * slot] = memb[step - 2]

        pl.when(step >= 2)(lambda: settle(step - 2))
        for index, (start, size) in enumerate(chunks):
            span = pl.ds(start, size)

            @pl.when(s > 0)
            def _():
                handoff(step, index).wait_recv()

            if index == 0:
                pl.when(first)(weights[0].wait)
            own = pl.ds(pl.multiple_of(c * half + start, BLOCK), size)
            for lanes in pieces(2 * D):
                kvb[step, own, lanes] = dot(
                    xb[step, span], vqkv[:, D + lanes.start : D + lanes.stop]
                ).astype(BF)
            exchange(step, index).start()
            for lanes in pieces(D):
                qb[side, span, lanes] = dot(xb[step, span], vqkv[:, lanes]).astype(BF)
        bias = key_bias(geometry, segment, lens_ref[side, :1, :1], (1, rows), 1)
        for index in range(len(chunks)):
            exchange(step, index).wait_recv()
        for index, (start, size) in enumerate(chunks):
            span = pl.ds(start, size)
            for pair in range(PAIRS):
                lanes = pair_span(pair)
                s_tmp[pair % 2, : 2 * size] = dot_nt(
                    scaled_queries(qb[side, span, lanes]), kvb[step, :, lanes]
                )
                for offset in range(0, 2 * size, 2 * BLOCK):
                    block = pl.ds(offset, 2 * BLOCK)
                    scores = s_tmp[pair % 2, block, :] + bias
                    exponent = jnp.exp(scores - jnp.max(scores, axis=-1, keepdims=True))
                    inverse = 1.0 / jnp.sum(exponent, axis=-1, keepdims=True)
                    probs[pair, block, :] = (exponent * inverse).astype(BF)
            for pair in range(PAIRS):
                mixed = dot(probs[pair, : 2 * size], kvb[step, :, pair_span(pair, D)])
                attb[side, span, pair_span(pair)] = folded_pair(mixed).astype(BF)
            if index == 0:
                pl.when(first)(weights[1].wait)
            for lanes in pieces(D):
                s1b[side, span, lanes] = xb[step, span, lanes].astype(F32) + dot(
                    attb[side, span], vproj[:, lanes]
                )
            for block in row_blocks(start, size):
                z, _ = normalized(s1b[side, block, :])
                normed = z * gain_one[...] + shift_one[...]
                nf[block, :] = normed
                nbb[side, block, :] = normed.astype(BF)
            if index == 0:
                pl.when(first)(weights[2].wait)
            for lanes in pieces(FF):
                pre = dot(nbb[side, span], vin[:, lanes]) + b_in[:, lanes]
                preb[span, lanes] = pre
                actb[side, span, lanes] = (
                    0.5 * pre * (1.0 + lax.erf(pre * 0.7071067811865476))
                ).astype(BF)
            if index == 0:
                pl.when(first)(weights[3].wait)
            for lanes in pieces(D):
                s2b[side, span, lanes] = nf[span, lanes] + dot(actb[side, span], vdown[:, lanes])
            for block in row_blocks(start, size):
                z, _ = normalized(s2b[side, block, :])
                hb[side, block, :] = (z * gain_two[...] + shift_two[...]).astype(BF)

            pl.when(s < last)(handoff(step, index).start)
            if index == 0:

                @pl.when((s == last) & (c == 0) & (step < steps - 2))
                def _():
                    memory_move(step).start()

        for block in row_blocks(0, half):
            pre = preb[block, :]
            density = jnp.exp(-0.5 * pre * pre) * 0.3989422804014327
            slope = 0.5 * (1.0 + lax.erf(pre * 0.7071067811865476)) + pre * density
            gpb[side, block, :] = slope.astype(BF)
        for copy in outgoing(step):
            copy.start()
        for index in range(len(chunks)):
            exchange(step, index).wait_send()

    lax.fori_loop(0, steps + 1, one_step, 0)
    settle(steps - 2)
    settle(steps - 1)


def forward(sections, segments, geometry, collective, x0, lens, weights):
    mem, slot, tok, rows = geometry
    half = rows // 2
    steps = 2 * segments

    def kept(width, kind, height=half):
        return jax.ShapeDtypeStruct((steps, height, width), kind)

    outs = (
        kept(D, BF),
        kept(D, BF),
        kept(2 * D, BF, rows),
        kept(D, BF),
        kept(D, BF),
        kept(FF, BF),
        kept(FF, BF),
        kept(D, F32),
        kept(D, F32),
        kept(D, BF),
        jax.ShapeDtypeStruct((3 * D, D), BF),
        jax.ShapeDtypeStruct((D, D), BF),
        jax.ShapeDtypeStruct((FF, D), BF),
        jax.ShapeDtypeStruct((D, FF), BF),
    )
    dma = pltpu.SemaphoreType.DMA
    return pl.pallas_call(
        functools.partial(forward_kernel, sections, segments, geometry),
        name="forward_layer",
        out_shape=outs,
        in_specs=[ANY, VMEM] + [ANY] * 4 + [VMEM] * 5,
        out_specs=(ANY,) * len(outs),
        scratch_shapes=[
            pltpu.VMEM((D, 3 * D), BF),
            pltpu.VMEM((D, D), BF),
            pltpu.VMEM((D, FF), BF),
            pltpu.VMEM((FF, D), BF),
            pltpu.VMEM((steps, half, D), BF),
            pltpu.VMEM((steps, rows, 2 * D), BF),
            pltpu.VMEM((2, half, D), BF),
            pltpu.VMEM((2, half, D), BF),
            pltpu.VMEM((2, half, D), BF),
            pltpu.VMEM((2, half, FF), BF),
            pltpu.VMEM((2, half, FF), BF),
            pltpu.VMEM((2, half, D), F32),
            pltpu.VMEM((2, half, D), F32),
            pltpu.VMEM((2, half, D), BF),
            pltpu.VMEM((half, FF), F32),
            pltpu.VMEM((half, D), F32),
            pltpu.VMEM((steps, slot, D), BF),
            pltpu.VMEM((2, rows, rows), F32),
            pltpu.VMEM((PAIRS, rows, rows), BF),
            pltpu.VMEM((3, D, D), BF),
            dma((4,)),
            dma((steps,)),
            dma((2, 10)),
            dma((2,)),
            dma((steps, 2)),
            dma((2, 2)),
            dma((steps, 2)),
            dma((2,)),
            dma((steps,)),
            dma((3,)),
        ],
        compiler_params=pltpu.CompilerParams(
            collective_id=collective, has_side_effects=True, vmem_limit_bytes=VMEM_LIMIT
        ),
    )(x0, lens, *weights)


def backward_kernel(
    sections,
    segments,
    geometry,
    g0_ref,
    lens_ref,
    r_q,
    r_kv,
    r_gp,
    r_s1,
    r_s2,
    w_qkv,
    w_proj,
    w_in,
    w_down,
    gain_one,
    gain_two,
    o_dpj,
    o_dbr,
    o_dpre,
    o_dfe,
    o_dx,
    o_mg,
    o_small,
    vqkv,
    vproj,
    vin,
    vdown,
    gb,
    qb,
    kvb,
    gpb,
    z1b,
    z2b,
    r1b,
    r2b,
    probs,
    work,
    dsec,
    dfe,
    dpre,
    dbr,
    da,
    dp_tmp,
    ds_tmp,
    dkv,
    dkv_in,
    dpj,
    dxb,
    mgb,
    carb,
    wsem,
    rsem,
    gsem,
    osem,
    kv_send,
    kv_recv,
    h_send,
    h_recv,
    m_send,
    m_recv,
):
    place = Place(sections)
    s, c = place.s, place.c
    mem, slot, tok, rows = geometry
    half = rows // 2
    own = pl.ds(pl.multiple_of(c * half, BLOCK), half)
    theirs = pl.ds(pl.multiple_of((1 - c) * half, BLOCK), half)
    last = sections - 1
    steps = 2 * segments
    chunks = row_chunks(half)
    weights = [
        pltpu.make_async_copy(src, dst, wsem.at[k])
        for k, (src, dst) in enumerate(((w_down, vdown), (w_in, vin), (w_proj, vproj), (w_qkv, vqkv)))
    ]

    def kept_index(step):
        return 2 * (segments - 1 - lax.div(step, 2)) + lax.rem(step, 2)

    def residuals(step):
        side = lax.rem(step, 2)
        pairs = ((r_q, qb), (r_kv, kvb), (r_s2, z2b), (r_gp, gpb), (r_s1, z1b))
        return [
            pltpu.make_async_copy(src.at[kept_index(step)], dst.at[side], rsem.at[side, k])
            for k, (src, dst) in enumerate(pairs)
        ]

    def seed_copy(step):
        return pltpu.make_async_copy(g0_ref.at[kept_index(step)], gb.at[step], gsem.at[step])

    for step in range(2):
        for copy in residuals(step):
            copy.start()
        if step == 0:
            for copy in weights:
                copy.start()

    @pl.when(s == last)
    def _():
        for step in range(steps):
            seed_copy(step).start()

    o_small[...] = jnp.zeros_like(o_small)
    barrier = pltpu.get_barrier_semaphore()
    pl.semaphore_signal(barrier, inc=1, device_id=(place.next, place.d), device_id_type=MESH)
    pl.semaphore_signal(barrier, inc=1, device_id=(s, place.other), device_id_type=MESH)
    pl.semaphore_wait(barrier, 2)

    def outgoing(step):
        pairs = (
            (dpj, o_dpj),
            (dbr, o_dbr),
            (dpre, o_dpre),
            (dfe, o_dfe),
        )
        return [
            pltpu.make_async_copy(src, dst.at[kept_index(step)], osem.at[k])
            for k, (src, dst) in enumerate(pairs)
        ]

    def outgoing_dx(step):
        side = lax.rem(step, 2)
        return pltpu.make_async_copy(dxb.at[side], o_dx.at[kept_index(step)], osem.at[4 + side])

    def outgoing_memory(step):
        return pltpu.make_async_copy(mgb.at[step], o_mg.at[lax.rem(step, 2)], gsem.at[step])

    def handoff(step, index):
        start, size = chunks[index]
        side = lax.rem(step, 2)
        span = pl.ds(start, size)
        return remote(
            dxb.at[side, span],
            gb.at[step, span],
            h_send.at[side, index],
            h_recv.at[step, index],
            (place.prev, place.d),
        )

    def carry_move(step):
        return remote(mgb.at[step], carb.at[step], m_send.at[step], m_recv.at[step], (last, place.d))

    def settle(step):
        @pl.when(s > 0)
        def _():
            for index in range(len(chunks)):
                handoff(step, index).wait_send()

        outgoing_dx(step).wait()

    def prologue(step):
        side = lax.rem(step, 2)
        segment = segments - 1 - lax.div(step, 2)
        for copy in residuals(step):
            copy.wait()
        for z_ref, r_ref in ((z2b, r2b), (z1b, r1b)):
            for block in row_blocks(0, half):
                z, scale = normalized(z_ref[side, block, :])
                z_ref[side, block, :] = z
                r_ref[side, block, :] = jnp.broadcast_to(scale, (BLOCK, 128))
        bias = key_bias(geometry, segment, lens_ref[side, :1, :1], (rows, 128), 0)
        for pair in range(PAIRS):
            lanes = pair_span(pair)
            keys = kvb[side, :, lanes]
            for start, size in chunks:
                queries = scaled_queries(qb[side, pl.ds(start, size), lanes])
                tiles = [bias] * (2 * size // 128)
                if 2 * size % 128:
                    tiles.append(bias[:, : 2 * size % 128])
                scores = dot_nt(keys, queries) + jnp.concatenate(tiles, axis=1)
                exponent = jnp.exp(scores - jnp.max(scores, axis=0, keepdims=True))
                inverse = 1.0 / jnp.sum(exponent, axis=0, keepdims=True)
                probs[side, pair, :, 2 * start : 2 * (start + size)] = (exponent * inverse).astype(BF)

    def norm_back(g, z, scale, gain):
        scaled = g * gain
        mean_u = jnp.mean(scaled, axis=-1, keepdims=True)
        mean_uz = jnp.mean(scaled * z, axis=-1, keepdims=True)
        return (scaled - mean_u - z * mean_uz) * scale

    def folded_rows(value):
        return value[: BLOCK // 2] + value[BLOCK // 2 :]

    def main(step):
        side = lax.rem(step, 2)
        segment = segments - 1 - lax.div(step, 2)
        first = step == 0
        pl.when(step >= 2)(lambda: settle(step - 2))

        @pl.when(step >= 1)
        def _():
            for copy in outgoing(step - 1):
                copy.wait()

        @pl.when(s == last)
        def _():
            seed_copy(step).wait()
            length = lens_ref[side, :1, :1]
            for index, block in enumerate(row_blocks(0, half)):
                row = c * half + index * BLOCK + lax.broadcasted_iota(jnp.int32, (BLOCK, D), 0)
                position = row - 2 * slot + segment * tok
                valid = (row >= 2 * slot) & (position.astype(F32) < length)
                work[block, :] = jnp.where(valid, gb[step, block, :].astype(F32), 0.0)

            @pl.when((c == 0) & (step >= 2))
            def _():
                carry_move(step - 2).wait_recv()
                work[slot : 2 * slot, :] = carb[step - 2]

        sends = []
        for index, (start, size) in enumerate(chunks):
            span = pl.ds(start, size)

            @pl.when(s < last)
            def _():
                handoff(step, index).wait_recv()
                for block in row_blocks(start, size):
                    work[block, :] = gb[step, block, :].astype(F32)

            gain_sum = jnp.zeros((BLOCK // 2, D), F32)
            shift_sum = jnp.zeros((BLOCK // 2, D), F32)
            for block in row_blocks(start, size):
                g = work[block, :]
                z = z2b[side, block, :]
                back = norm_back(g, z, r2b[side, block, :1], gain_two[...])
                dsec[block, :] = back
                dfe[block, :] = back.astype(BF)
                gain_sum += folded_rows(g * z)
                shift_sum += folded_rows(g)
            o_small[2:3, :] += jnp.sum(gain_sum, axis=0, keepdims=True)
            o_small[3:4, :] += jnp.sum(shift_sum, axis=0, keepdims=True)
            if index == 0:
                pl.when(first)(weights[0].wait)
            for lanes in pieces(FF):
                slope = gpb[side, span, lanes].astype(F32)
                pre = (dot(dfe[span], vdown[:, lanes]) * slope).astype(BF)
                dpre[span, lanes] = pre
                row, column = divmod(lanes.start, D)
                o_small[4 + row : 5 + row, column : column + STEP] += jnp.sum(
                    pre.astype(F32), axis=0, keepdims=True
                )
            if index == 0:
                pl.when(first)(weights[1].wait)
            for lanes in pieces(D):
                work[span, lanes] = dsec[span, lanes] + dot(dpre[span], vin[:, lanes])
            gain_sum = jnp.zeros((BLOCK // 2, D), F32)
            shift_sum = jnp.zeros((BLOCK // 2, D), F32)
            for block in row_blocks(start, size):
                g = work[block, :]
                z = z1b[side, block, :]
                back = norm_back(g, z, r1b[side, block, :1], gain_one[...])
                work[block, :] = back
                dbr[block, :] = back.astype(BF)
                gain_sum += folded_rows(g * z)
                shift_sum += folded_rows(g)
            o_small[0:1, :] += jnp.sum(gain_sum, axis=0, keepdims=True)
            o_small[1:2, :] += jnp.sum(shift_sum, axis=0, keepdims=True)
            if index == 0:
                pl.when(first)(weights[2].wait)
            for lanes in pieces(D):
                da[span, lanes] = dot(dbr[span], vproj[:, lanes]).astype(BF)
            for pair in range(PAIRS):
                keys = kvb[side, :, pair_span(pair)]
                values = kvb[side, :, pair_span(pair, D)]
                da2 = stacked_pair(da[span, pair_span(pair)])
                q2 = scaled_queries(qb[side, span, pair_span(pair)])
                dp_ref = dp_tmp.at[pair % 2]
                ds_ref = ds_tmp.at[pair % 2]
                wide = 2 * size
                dp_ref[:, :wide] = dot_nt(values, da2)
                for begin in range(0, wide, 128):
                    lanes = slice(begin, min(begin + 128, wide))
                    kept_lanes = slice(2 * start + begin, 2 * start + lanes.stop)
                    total = jnp.zeros((BLOCK, lanes.stop - begin), F32)
                    for offset in range(0, rows, BLOCK):
                        block = pl.ds(offset, BLOCK)
                        total += probs[side, pair, block, kept_lanes].astype(F32) * dp_ref[block, lanes]
                    total = jnp.sum(total, axis=0, keepdims=True)
                    for offset in range(0, rows, BLOCK):
                        block = pl.ds(offset, BLOCK)
                        ds_ref[block, lanes] = (
                            probs[side, pair, block, kept_lanes].astype(F32) * (dp_ref[block, lanes] - total)
                        ).astype(BF)
                d_keys = dot(ds_ref[:, :wide], q2)
                d_values = dot(probs[side, pair, :, 2 * start : 2 * start + wide], da2)
                if index == 0:
                    dkv[pair, :, :WIDE] = d_keys
                    dkv[pair, :, WIDE:] = d_values
                else:
                    dkv[pair, :, :WIDE] += d_keys
                    dkv[pair, :, WIDE:] += d_values
                if index == len(chunks) - 1:
                    move = remote(
                        dkv.at[pair, theirs],
                        dkv_in.at[side, pair],
                        kv_send.at[pair],
                        kv_recv.at[step, pair],
                        (s, place.other),
                    )
                    move.start()
                    sends.append(move)
                both = dot_tn(keys, ds_ref[:, :wide])
                lane = lax.broadcasted_iota(jnp.int32, (WIDE, size), 0)
                upright = jnp.where(lane < HEAD, both[:, :size], both[:, size:])
                dpj[span, pair_span(pair)] = (jnp.transpose(upright) * HEAD**-0.5).astype(BF)
        pl.when(first)(weights[3].wait)
        for pair in range(PAIRS):
            sends[pair].wait_recv()
            for part in range(2):
                lanes = slice(part * WIDE, (part + 1) * WIDE)
                dpj[:, pair_span(pair, (part + 1) * D)] = (
                    dkv[pair, own, lanes] + dkv_in[side, pair, :, lanes]
                ).astype(BF)
        for index, (start, size) in enumerate(chunks):
            span = pl.ds(start, size)
            for lanes in pieces(D):
                dxb[side, span, lanes] = (
                    work[span, lanes] + dot(dpj[span], vqkv[:, lanes])
                ).astype(BF)
            pl.when(s > 0)(handoff(step, index).start)
            if index == 0:

                @pl.when((s == 0) & (c == 0))
                def _():
                    mgb[step] = dxb[side, :slot].astype(F32) + dxb[side, slot : 2 * slot].astype(F32)
                    pl.when(step < steps - 2)(carry_move(step).start)

        for copy in outgoing(step):
            copy.start()
        outgoing_dx(step).start()
        for move in sends:
            move.wait_send()

        @pl.when(step < steps - 2)
        def _():
            for copy in residuals(step + 2):
                copy.start()

    def one_round(turn, state):
        even, odd = 2 * turn, 2 * turn + 1
        late = (s == last) & (turn == 0)
        prologue(even)
        pl.when(jnp.logical_not(late))(lambda: prologue(odd))
        main(even)
        pl.when(late)(lambda: prologue(odd))
        main(odd)
        return state

    lax.fori_loop(0, segments, one_round, 0)
    settle(steps - 2)
    settle(steps - 1)
    for copy in outgoing(steps - 1):
        copy.wait()

    @pl.when((s == 0) & (c == 0))
    def _():
        for step in range(steps - 2, steps):
            outgoing_memory(step).start()
        for step in range(steps - 2, steps):
            outgoing_memory(step).wait()
        for step in range(steps - 2):
            carry_move(step).wait_send()


def backward(sections, segments, geometry, collective, g0, lens, kept, weights):
    mem, slot, tok, rows = geometry
    half = rows // 2
    steps = 2 * segments

    def grad(width):
        return jax.ShapeDtypeStruct((steps, half, width), BF)

    outs = (
        grad(3 * D),
        grad(D),
        grad(FF),
        grad(D),
        grad(D),
        jax.ShapeDtypeStruct((2, slot, D), F32),
        jax.ShapeDtypeStruct((8, D), F32),
    )
    dma = pltpu.SemaphoreType.DMA
    return pl.pallas_call(
        functools.partial(backward_kernel, sections, segments, geometry),
        name="backward_layer",
        out_shape=outs,
        in_specs=[ANY, VMEM] + [ANY] * 5 + [ANY] * 4 + [VMEM] * 2,
        out_specs=(ANY,) * 6 + (VMEM,),
        scratch_shapes=[
            pltpu.VMEM((3 * D, D), BF),
            pltpu.VMEM((D, D), BF),
            pltpu.VMEM((FF, D), BF),
            pltpu.VMEM((D, FF), BF),
            pltpu.VMEM((steps, half, D), BF),
            pltpu.VMEM((2, half, D), BF),
            pltpu.VMEM((2, rows, 2 * D), BF),
            pltpu.VMEM((2, half, FF), BF),
            pltpu.VMEM((2, half, D), F32),
            pltpu.VMEM((2, half, D), F32),
            pltpu.VMEM((2, half, 128), F32),
            pltpu.VMEM((2, half, 128), F32),
            pltpu.VMEM((2, PAIRS, rows, rows), BF),
            pltpu.VMEM((half, D), F32),
            pltpu.VMEM((half, D), F32),
            pltpu.VMEM((half, D), BF),
            pltpu.VMEM((half, FF), BF),
            pltpu.VMEM((half, D), BF),
            pltpu.VMEM((half, D), BF),
            pltpu.VMEM((2, rows, rows), F32),
            pltpu.VMEM((2, rows, rows), BF),
            pltpu.VMEM((PAIRS, rows, 2 * WIDE), F32),
            pltpu.VMEM((2, PAIRS, half, 2 * WIDE), F32),
            pltpu.VMEM((half, 3 * D), BF),
            pltpu.VMEM((2, half, D), BF),
            pltpu.VMEM((steps, slot, D), F32),
            pltpu.VMEM((steps, slot, D), F32),
            dma((4,)),
            dma((2, 5)),
            dma((steps,)),
            dma((6,)),
            dma((PAIRS,)),
            dma((steps, PAIRS)),
            dma((2, 2)),
            dma((steps, 2)),
            dma((steps,)),
            dma((steps,)),
        ],
        compiler_params=pltpu.CompilerParams(
            collective_id=collective, has_side_effects=True, vmem_limit_bytes=VMEM_LIMIT
        ),
    )(g0, lens, *kept, *weights)


def on_device(
    sections,
    inputs,
    out_grad,
    memory,
    lengths,
    w_qkv,
    w_proj,
    gain_one,
    shift_one,
    w_in,
    b_in,
    w_down,
    gain_two,
    shift_two,
):
    segs, tok, part = inputs.shape[1:]
    mem = memory.shape[1]
    slot = -(-mem // BLOCK) * BLOCK
    rows = -(-(2 * slot + tok) // (2 * BLOCK)) * 2 * BLOCK
    half = rows // 2
    geometry = (mem, slot, tok, rows)
    back_pad = rows - 2 * slot - tok

    def in_slots(array):
        return jnp.pad(array, ((0, 0), (2 * slot, back_pad), (0, 0)))

    def halves(array):
        return array.reshape(segs, 2, half, part).transpose(1, 0, 2, 3)

    tokens = in_slots(inputs[0])
    tokens = tokens.at[0, :mem].set(memory[0]).at[0, slot : slot + mem].set(memory[0])
    cotangent = in_slots(out_grad[0])
    length_tile = jnp.broadcast_to(lengths.astype(F32), (8, 128))
    x_all, g_all, lens = spread(sections, halves(tokens), halves(cotangent), length_tile)

    def by_step(array):
        return array.transpose(2, 0, 3, 1, 4).reshape(2 * segs, half, D)

    matrices = (w_qkv[0], w_proj[0], w_in[0], w_down[0])
    forward_weights = matrices + (gain_one, shift_one, b_in, gain_two, shift_two)
    x, q, kv, att, nb, act, gp, s1, s2, hid, *turned = forward(
        sections, segs, geometry, 2, by_step(x_all), lens, forward_weights
    )
    dpj, dbr, dpre, dfe, dx, memory_term, small = backward(
        sections, segs, geometry, 3, by_step(g_all), lens, (q, kv, gp, s1, s2), (*turned, gain_one, gain_two)
    )

    def per_owner(array):
        return array.reshape(segs, 2, half, sections, part).transpose(1, 3, 0, 2, 4)

    memory_term = memory_term.reshape(2, slot, sections, part).transpose(0, 2, 1, 3)
    out_parts, in_parts, memory_part = collect(sections, per_owner(hid), per_owner(dx), memory_term)

    def owned(parts):
        return parts.transpose(1, 0, 2, 3).reshape(segs, rows, part)[:, 2 * slot : 2 * slot + tok]

    position = jnp.arange(segs * tok, dtype=jnp.int32).reshape(segs, tok)
    token_valid = position < lengths[0]
    outputs = jnp.where(token_valid[:, :, None], owned(out_parts), jnp.zeros((), BF))
    input_grad = owned(in_parts)
    memory_grad = memory_part[:mem]

    def weight_grad(left, right):
        lefts = left.reshape(2 * segs * half, -1)
        rights = right.reshape(2 * segs * half, -1)
        full = jnp.einsum("rd,re->de", lefts, rights, preferred_element_type=F32)
        return lax.psum_scatter(full.astype(BF), "dp", scatter_dimension=0, tiled=True).astype(F32)

    d_qkv = weight_grad(x, dpj)
    d_proj = weight_grad(att, dbr)
    d_in = weight_grad(nb, dpre)
    d_down = weight_grad(act, dfe)
    small = lax.psum(small, "dp")
    devices = lax.axis_size("dp")
    index = lax.axis_index("dp")

    def vector(value):
        size = value.size // devices
        return lax.dynamic_slice_in_dim(value.reshape(-1), index * size, size, 0)[None]

    return (
        outputs[None],
        input_grad[None],
        memory_grad[None],
        d_qkv[None],
        d_proj[None],
        vector(small[0]),
        vector(small[1]),
        d_in[None],
        vector(small[4:8]),
        d_down[None],
        vector(small[2]),
        vector(small[3]),
    )


def solution(mesh):
    return jax.shard_map(
        functools.partial(on_device, mesh.shape["section"]),
        mesh=mesh,
        in_specs=(
            P("dp", None, None, "section"),
            P("dp", None, None, "section"),
            P("dp", None, "section"),
            P("dp"),
            P("section", None, None),
            P("section", None, None),
            P("section", None),
            P("section", None),
            P("section", None, None),
            P("section", None),
            P("section", None, None),
            P("section", None),
            P("section", None),
        ),
        out_specs=(
            P("dp", None, None, "section"),
            P("dp", None, None, "section"),
            P("dp", None, "section"),
            P("section", "dp", None),
            P("section", "dp", None),
            P("section", "dp"),
            P("section", "dp"),
            P("section", "dp", None),
            P("section", "dp"),
            P("section", "dp", None),
            P("section", "dp"),
            P("section", "dp"),
        ),
        check_vma=False,
    )
```

```python
import functools

import jax
import jax.numpy as jnp
from jax import lax
from jax.experimental import pallas as pl
from jax.experimental.pallas import tpu as pltpu
from jax.sharding import PartitionSpec as P

D = 768
H = 12
HEAD = 64
FF = 3072
PAIRS = H // 2
WIDE = 2 * HEAD
STEP = 256
BLOCK = 16
BF = jnp.bfloat16
F32 = jnp.float32
MESH = pl.DeviceIdType.MESH
ANY = pl.BlockSpec(memory_space=pl.ANY)
VMEM = pl.BlockSpec(memory_space=pltpu.VMEM)
VMEM_LIMIT = 63 * 1024 * 1024


def dot(a, b):
    return jnp.dot(a, b, preferred_element_type=F32)


def dot_nt(a, b):
    return lax.dot_general(a, b, (((1,), (1,)), ((), ())), preferred_element_type=F32)


def dot_tn(a, b):
    return lax.dot_general(a, b, (((0,), (0,)), ((), ())), preferred_element_type=F32)


def cols(index):
    return pl.ds(index * STEP, STEP)


def remote(src, dst, send, recv, target):
    return pltpu.make_async_remote_copy(
        src_ref=src, dst_ref=dst, send_sem=send, recv_sem=recv, device_id=target, device_id_type=MESH
    )


class Place:
    def __init__(self, sections):
        self.s = lax.axis_index("section")
        self.d = lax.axis_index("dp")
        self.c = lax.rem(self.d, 2)
        self.base = self.d - self.c
        self.other = self.base + 1 - self.c
        self.next = lax.rem(self.s + 1, sections)
        self.prev = lax.rem(self.s + sections - 1, sections)


def greet_plane(place, sections):
    barrier = pltpu.get_barrier_semaphore()
    for section in range(sections):
        for core in range(2):

            @pl.when((place.s != section) | (place.c != core))
            def _():
                pl.semaphore_signal(
                    barrier, inc=1, device_id=(section, place.base + core), device_id_type=MESH
                )


def plane_wait(sections, extra):
    pl.semaphore_wait(pltpu.get_barrier_semaphore(), 2 * sections - 1 + extra)


def key_bias(geometry, segment, length, shape, dim):
    mem, slot, tok, rows = geometry
    row = lax.broadcasted_iota(jnp.int32, shape, dim)
    position = row - 2 * slot + segment * tok
    is_token = (row >= 2 * slot) & (row < 2 * slot + tok) & (position.astype(F32) < length)
    is_memory = (row < mem) | ((row >= slot) & (row < slot + mem))
    return jnp.where(is_token | is_memory, 0.0, -1e30)


def stacked_pair(pair):
    lane = lax.broadcasted_iota(jnp.int32, pair.shape, 1)
    zero = jnp.zeros_like(pair)
    return jnp.concatenate(
        [jnp.where(lane < HEAD, pair, zero), jnp.where(lane >= HEAD, pair, zero)], axis=0
    )


def folded_pair(both):
    half = both.shape[0] // 2
    lane = lax.broadcasted_iota(jnp.int32, (half, WIDE), 1)
    return jnp.where(lane < HEAD, both[:half], both[half:])


def scaled_queries(queries):
    return stacked_pair(queries * jnp.asarray(HEAD**-0.5, BF))


def normalized(rows):
    center = rows - jnp.mean(rows, axis=-1, keepdims=True)
    spread_of = jnp.mean(center * center, axis=-1, keepdims=True)
    scale = lax.rsqrt(spread_of + 1e-06)
    return center * scale, scale


def pieces(width, step=STEP):
    return [slice(start, start + step) for start in range(0, width, step)]


def row_chunks(half):
    first = half // 2 // BLOCK * BLOCK
    return ((0, first), (first, half - first))


def row_blocks(start, size):
    return [pl.ds(start + offset, BLOCK) for offset in range(0, size, BLOCK)]


def pair_span(pair, offset=0):
    return slice(offset + pair * WIDE, offset + (pair + 1) * WIDE)


def forward_kernel(
    sections,
    segments,
    geometry,
    a_ref,
    g_ref,
    len_ref,
    w_qkv,
    w_proj,
    w_in,
    w_down,
    gain_one,
    shift_one,
    b_in,
    gain_two,
    shift_two,
    o_x,
    o_q,
    o_kv,
    o_att,
    o_nb,
    o_act,
    o_gp,
    o_s1,
    o_s2,
    o_hid,
    t_qkv,
    t_proj,
    t_in,
    t_down,
    o_g,
    o_lens,
    vqkv,
    vproj,
    vin,
    vdown,
    xb,
    kvb,
    qb,
    attb,
    nbb,
    actb,
    gpb,
    s1b,
    s2b,
    hb,
    preb,
    nf,
    memb,
    s_tmp,
    probs,
    turned,
    xp,
    hg,
    lens_ref,
    wsem,
    osem,
    kv_send,
    kv_recv,
    h_send,
    h_recv,
    m_send,
    m_recv,
    tsem,
    a_send,
    a_got,
    g_send,
    g_got,
    l_send,
    l_got,
):
    place = Place(sections)
    s, c = place.s, place.c
    mem, slot, tok, rows = geometry
    half = rows // 2
    last = sections - 1
    steps = 2 * segments
    chunks = row_chunks(half)
    early = s >= 2
    weights = [
        pltpu.make_async_copy(src, dst, wsem.at[k])
        for k, (src, dst) in enumerate(((w_qkv, vqkv), (w_proj, vproj), (w_in, vin), (w_down, vdown)))
    ]

    part = a_ref.shape[-1]
    greet_plane(place, sections)
    plane_wait(sections, 0)

    def spread(src, dst, target, send, got, segment):
        step = 2 * segment + c
        for core in range(2):
            here = (s == target) & (c == core)
            far = functools.partial(remote,
                src.at[segment, core],
                dst.at[step, s],
                send.at[segment, core],
                got.at[step, s],
                (target, place.base + core),
            )
            near = functools.partial(pltpu.make_async_copy, src.at[segment, core], dst.at[step, s], got.at[step, s])
            yield here, far, near

    def tokens(segment):
        return spread(a_ref, xp, 0, a_send, a_got, segment)

    def cotangents(segment):
        return spread(g_ref, o_g, last, g_send, g_got, segment)

    def begin(moves):
        for here, far, near in moves:
            pl.when(jnp.logical_not(here))(lambda far=far: far().start())
            pl.when(here)(lambda near=near: near().start())

    def sent(moves):
        for here, far, _ in moves:
            pl.when(jnp.logical_not(here))(lambda far=far: far().wait_send())

    def arrived(src, dst, got, target, step, section):
        side = lax.rem(step, 2)
        here = (section == target) & (side == c)
        far = functools.partial(remote,
            src.at[0, 0], dst.at[step, section], a_send.at[0, 0], got.at[step, section], (s, place.d)
        )
        near = functools.partial(pltpu.make_async_copy, src.at[0, 0], dst.at[step, section], got.at[step, section])
        pl.when(jnp.logical_not(here))(lambda far=far: far().wait_recv())
        pl.when(here)(lambda near=near: near().wait())

    begin(tokens(0))
    length_move = remote(len_ref, lens_ref.at[c], l_send.at[0], l_got.at[0], (s, place.other))
    length_move.start()
    lens_ref[c] = len_ref[...]
    for copy in weights:
        copy.start()
    sent(tokens(0))
    for segment in range(1, segments):
        begin(tokens(segment))
    for segment in range(segments):
        begin(cotangents(segment))
    remote(len_ref, lens_ref.at[1 - c], l_send.at[0], l_got.at[0], (s, place.other)).wait_recv()

    def outgoing(step):
        side = lax.rem(step, 2)
        pairs = (
            (xb.at[step], o_x),
            (kvb.at[step], o_kv),
            (qb.at[side], o_q),
            (attb.at[side], o_att),
            (nbb.at[side], o_nb),
            (actb.at[side], o_act),
            (gpb.at[side], o_gp),
            (s1b.at[side], o_s1),
            (s2b.at[side], o_s2),
            (hg.at[side], o_hid),
        )
        return [
            pltpu.make_async_copy(src, dst.at[step], osem.at[side, k])
            for k, (src, dst) in enumerate(pairs)
        ]

    def handoff(step, index):
        start, size = chunks[index]
        side = lax.rem(step, 2)
        span = pl.ds(start, size)
        return remote(
            hb.at[side, span],
            xb.at[step, span],
            h_send.at[side, index],
            h_recv.at[step, index],
            (place.next, place.d),
        )

    def memory_move(step):
        side = lax.rem(step, 2)
        return remote(
            hb.at[side, pl.ds(slot, slot)], memb.at[step], m_send.at[side], m_recv.at[step], (0, place.d)
        )

    def exchange(step, index):
        start, size = chunks[index]
        span = pl.ds(pl.multiple_of(c * half + start, BLOCK), size)
        return remote(
            kvb.at[step, span],
            kvb.at[step, span],
            kv_send.at[index],
            kv_recv.at[step, index],
            (s, place.other),
        )

    def settle(step):
        @pl.when(s < last)
        def _():
            for index in range(len(chunks)):
                handoff(step, index).wait_send()

        @pl.when((s == last) & (c == 0) & (step < steps - 2))
        def _():
            memory_move(step).wait_send()

        for copy in outgoing(step):
            copy.wait()

    def turn_weights():
        @pl.when(early)
        def _():
            for copy in weights:
                copy.wait()

        blocks = []
        for src, dst in ((vqkv, t_qkv), (vproj, t_proj), (vin, t_in), (vdown, t_down)):
            for block in range(src.shape[0] * src.shape[1] // (D * D)):
                span = pl.ds(block * D, D)
                if src.shape[0] == D:
                    blocks.append((src, (slice(None), span), dst.at[span]))
                else:
                    blocks.append((src, (span, slice(None)), dst.at[:, span]))
        moves = []
        for index, (src, where, dst) in enumerate(blocks):
            spot = index % 3
            if index >= 3:
                moves[index - 3].wait()
            turned[spot] = jnp.transpose(src[where])
            moves.append(pltpu.make_async_copy(turned.at[spot], dst, tsem.at[spot]))
            moves[-1].start()
        for move in moves[-3:]:
            move.wait()

    def one_step(step, state):
        pl.when(step == jnp.where(early, 0, steps))(turn_weights)
        pl.when(step < steps)(lambda: compute_step(step))
        return state

    def compute_step(step):
        side = lax.rem(step, 2)
        segment = lax.div(step, 2)
        first = (step == 0) & jnp.logical_not(early)

        @pl.when(s == 0)
        def _():
            for section in range(sections):
                arrived(a_ref, xp, a_got, 0, step, section)
                xb[step, :, section * part : (section + 1) * part] = xp[step, section]

            @pl.when((c == 0) & (step >= 2))
            def _():
                memory_move(step - 2).wait_recv()
                xb[step, :slot] = memb[step - 2]
                xb[step, slot : 2 * slot] = memb[step - 2]

        pl.when(step >= 2)(lambda: settle(step - 2))
        for index, (start, size) in enumerate(chunks):
            span = pl.ds(start, size)

            @pl.when(s > 0)
            def _():
                handoff(step, index).wait_recv()

            if index == 0:
                pl.when(first)(weights[0].wait)
            own = pl.ds(pl.multiple_of(c * half + start, BLOCK), size)
            for lanes in pieces(2 * D):
                kvb[step, own, lanes] = dot(
                    xb[step, span], vqkv[:, D + lanes.start : D + lanes.stop]
                ).astype(BF)
            exchange(step, index).start()
            for lanes in pieces(D):
                qb[side, span, lanes] = dot(xb[step, span], vqkv[:, lanes]).astype(BF)
        bias = key_bias(geometry, segment, lens_ref[side, :1, :1], (1, rows), 1)
        for index in range(len(chunks)):
            exchange(step, index).wait_recv()
        for index, (start, size) in enumerate(chunks):
            span = pl.ds(start, size)
            for pair in range(PAIRS):
                lanes = pair_span(pair)
                s_tmp[pair % 2, : 2 * size] = dot_nt(
                    scaled_queries(qb[side, span, lanes]), kvb[step, :, lanes]
                )
                for offset in range(0, 2 * size, 2 * BLOCK):
                    block = pl.ds(offset, 2 * BLOCK)
                    scores = s_tmp[pair % 2, block, :] + bias
                    exponent = jnp.exp(scores - jnp.max(scores, axis=-1, keepdims=True))
                    inverse = 1.0 / jnp.sum(exponent, axis=-1, keepdims=True)
                    probs[pair, block, :] = (exponent * inverse).astype(BF)
            for pair in range(PAIRS):
                mixed = dot(probs[pair, : 2 * size], kvb[step, :, pair_span(pair, D)])
                attb[side, span, pair_span(pair)] = folded_pair(mixed).astype(BF)
            if index == 0:
                pl.when(first)(weights[1].wait)
            for lanes in pieces(D):
                s1b[side, span, lanes] = xb[step, span, lanes].astype(F32) + dot(
                    attb[side, span], vproj[:, lanes]
                )
            for block in row_blocks(start, size):
                z, _ = normalized(s1b[side, block, :])
                normed = z * gain_one[...] + shift_one[...]
                nf[block, :] = normed
                nbb[side, block, :] = normed.astype(BF)
            if index == 0:
                pl.when(first)(weights[2].wait)
            for lanes in pieces(FF):
                pre = dot(nbb[side, span], vin[:, lanes]) + b_in[:, lanes]
                preb[span, lanes] = pre
                actb[side, span, lanes] = (
                    0.5 * pre * (1.0 + lax.erf(pre * 0.7071067811865476))
                ).astype(BF)
            if index == 0:
                pl.when(first)(weights[3].wait)
            for lanes in pieces(D):
                s2b[side, span, lanes] = nf[span, lanes] + dot(actb[side, span], vdown[:, lanes])
            for block in row_blocks(start, size):
                z, _ = normalized(s2b[side, block, :])
                hb[side, block, :] = (z * gain_two[...] + shift_two[...]).astype(BF)

            pl.when(s < last)(handoff(step, index).start)
            if index == 0:

                @pl.when((s == last) & (c == 0) & (step < steps - 2))
                def _():
                    memory_move(step).start()

        for block in row_blocks(0, half):
            pre = preb[block, :]
            density = jnp.exp(-0.5 * pre * pre) * 0.3989422804014327
            slope = 0.5 * (1.0 + lax.erf(pre * 0.7071067811865476)) + pre * density
            gpb[side, block, :] = slope.astype(BF)
        for section in range(sections):
            hg[side, section] = hb[side, :, section * part : (section + 1) * part]
        for copy in outgoing(step):
            copy.start()
        for index in range(len(chunks)):
            exchange(step, index).wait_send()

    lax.fori_loop(0, steps + 1, one_step, 0)
    settle(steps - 2)
    settle(steps - 1)
    o_lens[...] = lens_ref[...]
    length_move.wait_send()
    for segment in range(segments):
        if segment > 0:
            sent(tokens(segment))
        sent(cotangents(segment))

    @pl.when(s == last)
    def _():
        for step in range(steps):
            for section in range(sections):
                arrived(g_ref, o_g, g_got, last, step, section)


def forward(sections, segments, geometry, collective, a, g, length_tile, weights):
    mem, slot, tok, rows = geometry
    half = rows // 2
    steps = 2 * segments
    grouped = (steps, sections, half, a.shape[-1])

    def kept(width, kind, height=half):
        return jax.ShapeDtypeStruct((steps, height, width), kind)

    outs = (
        kept(D, BF),
        kept(D, BF),
        kept(2 * D, BF, rows),
        kept(D, BF),
        kept(D, BF),
        kept(FF, BF),
        kept(FF, BF),
        kept(D, F32),
        kept(D, F32),
        jax.ShapeDtypeStruct(grouped, BF),
        jax.ShapeDtypeStruct((3 * D, D), BF),
        jax.ShapeDtypeStruct((D, D), BF),
        jax.ShapeDtypeStruct((FF, D), BF),
        jax.ShapeDtypeStruct((D, FF), BF),
        jax.ShapeDtypeStruct(grouped, BF),
        jax.ShapeDtypeStruct((2, 8, 128), F32),
    )
    dma = pltpu.SemaphoreType.DMA
    return pl.pallas_call(
        functools.partial(forward_kernel, sections, segments, geometry),
        name="forward_layer",
        out_shape=outs,
        in_specs=[ANY, ANY, VMEM] + [ANY] * 4 + [VMEM] * 5,
        out_specs=(ANY,) * (len(outs) - 1) + (VMEM,),
        scratch_shapes=[
            pltpu.VMEM((D, 3 * D), BF),
            pltpu.VMEM((D, D), BF),
            pltpu.VMEM((D, FF), BF),
            pltpu.VMEM((FF, D), BF),
            pltpu.VMEM((steps, half, D), BF),
            pltpu.VMEM((steps, rows, 2 * D), BF),
            pltpu.VMEM((2, half, D), BF),
            pltpu.VMEM((2, half, D), BF),
            pltpu.VMEM((2, half, D), BF),
            pltpu.VMEM((2, half, FF), BF),
            pltpu.VMEM((2, half, FF), BF),
            pltpu.VMEM((2, half, D), F32),
            pltpu.VMEM((2, half, D), F32),
            pltpu.VMEM((2, half, D), BF),
            pltpu.VMEM((half, FF), F32),
            pltpu.VMEM((half, D), F32),
            pltpu.VMEM((steps, slot, D), BF),
            pltpu.VMEM((2, rows, rows), F32),
            pltpu.VMEM((PAIRS, rows, rows), BF),
            pltpu.VMEM((3, D, D), BF),
            pltpu.VMEM(grouped, BF),
            pltpu.VMEM((2,) + grouped[1:], BF),
            pltpu.VMEM((2, 8, 128), F32),
            dma((4,)),
            dma((2, 10)),
            dma((2,)),
            dma((steps, 2)),
            dma((2, 2)),
            dma((steps, 2)),
            dma((2,)),
            dma((steps,)),
            dma((3,)),
            dma((segments, 2)),
            dma((steps, sections)),
            dma((segments, 2)),
            dma((steps, sections)),
            dma((1,)),
            dma((1,)),
        ],
        compiler_params=pltpu.CompilerParams(
            collective_id=collective, has_side_effects=True, vmem_limit_bytes=VMEM_LIMIT
        ),
    )(a, g, length_tile, *weights)


def backward_kernel(
    sections,
    segments,
    geometry,
    g0_ref,
    lens_ref,
    r_q,
    r_kv,
    r_gp,
    r_s1,
    r_s2,
    w_qkv,
    w_proj,
    w_in,
    w_down,
    gain_one,
    gain_two,
    o_dpj,
    o_dbr,
    o_dpre,
    o_dfe,
    o_dx,
    o_mg,
    o_small,
    vqkv,
    vproj,
    vin,
    vdown,
    gb,
    qb,
    kvb,
    gpb,
    z1b,
    z2b,
    r1b,
    r2b,
    probs,
    work,
    dsec,
    dfe,
    dpre,
    dbr,
    da,
    dp_tmp,
    ds_tmp,
    dkv,
    dkv_in,
    dpj,
    dxb,
    mgb,
    carb,
    gp_in,
    dg,
    wsem,
    rsem,
    gsem,
    osem,
    kv_send,
    kv_recv,
    h_send,
    h_recv,
    m_send,
    m_recv,
):
    place = Place(sections)
    s, c = place.s, place.c
    mem, slot, tok, rows = geometry
    half = rows // 2
    own = pl.ds(pl.multiple_of(c * half, BLOCK), half)
    theirs = pl.ds(pl.multiple_of((1 - c) * half, BLOCK), half)
    last = sections - 1
    steps = 2 * segments
    part = g0_ref.shape[-1]
    chunks = row_chunks(half)
    weights = [
        pltpu.make_async_copy(src, dst, wsem.at[k])
        for k, (src, dst) in enumerate(((w_down, vdown), (w_in, vin), (w_proj, vproj), (w_qkv, vqkv)))
    ]

    def kept_index(step):
        return 2 * (segments - 1 - lax.div(step, 2)) + lax.rem(step, 2)

    def residuals(step):
        side = lax.rem(step, 2)
        pairs = ((r_q, qb), (r_kv, kvb), (r_s2, z2b), (r_gp, gpb), (r_s1, z1b))
        return [
            pltpu.make_async_copy(src.at[kept_index(step)], dst.at[side], rsem.at[side, k])
            for k, (src, dst) in enumerate(pairs)
        ]

    def seed_copy(step):
        return pltpu.make_async_copy(g0_ref.at[kept_index(step)], gp_in.at[step], gsem.at[step])

    for step in range(2):
        for copy in residuals(step):
            copy.start()
        if step == 0:
            for copy in weights:
                copy.start()

    @pl.when(s == last)
    def _():
        for step in range(steps):
            seed_copy(step).start()

    o_small[...] = jnp.zeros_like(o_small)
    barrier = pltpu.get_barrier_semaphore()
    pl.semaphore_signal(barrier, inc=1, device_id=(place.next, place.d), device_id_type=MESH)
    pl.semaphore_signal(barrier, inc=1, device_id=(s, place.other), device_id_type=MESH)
    pl.semaphore_wait(barrier, 2)

    def outgoing(step):
        pairs = (
            (dpj, o_dpj),
            (dbr, o_dbr),
            (dpre, o_dpre),
            (dfe, o_dfe),
        )
        return [
            pltpu.make_async_copy(src, dst.at[kept_index(step)], osem.at[k])
            for k, (src, dst) in enumerate(pairs)
        ]

    def outgoing_dx(step):
        side = lax.rem(step, 2)
        return pltpu.make_async_copy(dg.at[side], o_dx.at[kept_index(step)], osem.at[4 + side])

    def outgoing_memory(step):
        return pltpu.make_async_copy(mgb.at[step], o_mg.at[lax.rem(step, 2)], gsem.at[step])

    def handoff(step, index):
        start, size = chunks[index]
        side = lax.rem(step, 2)
        span = pl.ds(start, size)
        return remote(
            dxb.at[side, span],
            gb.at[step, span],
            h_send.at[side, index],
            h_recv.at[step, index],
            (place.prev, place.d),
        )

    def carry_move(step):
        return remote(mgb.at[step], carb.at[step], m_send.at[step], m_recv.at[step], (last, place.d))

    def settle(step):
        @pl.when(s > 0)
        def _():
            for index in range(len(chunks)):
                handoff(step, index).wait_send()

        outgoing_dx(step).wait()

    def prologue(step):
        side = lax.rem(step, 2)
        segment = segments - 1 - lax.div(step, 2)
        for copy in residuals(step):
            copy.wait()
        for z_ref, r_ref in ((z2b, r2b), (z1b, r1b)):
            for block in row_blocks(0, half):
                z, scale = normalized(z_ref[side, block, :])
                z_ref[side, block, :] = z
                r_ref[side, block, :] = jnp.broadcast_to(scale, (BLOCK, 128))
        bias = key_bias(geometry, segment, lens_ref[side, :1, :1], (rows, 128), 0)
        for pair in range(PAIRS):
            lanes = pair_span(pair)
            keys = kvb[side, :, lanes]
            for start, size in chunks:
                queries = scaled_queries(qb[side, pl.ds(start, size), lanes])
                tiles = [bias] * (2 * size // 128)
                if 2 * size % 128:
                    tiles.append(bias[:, : 2 * size % 128])
                scores = dot_nt(keys, queries) + jnp.concatenate(tiles, axis=1)
                exponent = jnp.exp(scores - jnp.max(scores, axis=0, keepdims=True))
                inverse = 1.0 / jnp.sum(exponent, axis=0, keepdims=True)
                probs[side, pair, :, 2 * start : 2 * (start + size)] = (exponent * inverse).astype(BF)

    def norm_back(g, z, scale, gain):
        scaled = g * gain
        mean_u = jnp.mean(scaled, axis=-1, keepdims=True)
        mean_uz = jnp.mean(scaled * z, axis=-1, keepdims=True)
        return (scaled - mean_u - z * mean_uz) * scale

    def folded_rows(value):
        return value[: BLOCK // 2] + value[BLOCK // 2 :]

    def main(step):
        side = lax.rem(step, 2)
        segment = segments - 1 - lax.div(step, 2)
        first = step == 0
        pl.when(step >= 2)(lambda: settle(step - 2))

        @pl.when(step >= 1)
        def _():
            for copy in outgoing(step - 1):
                copy.wait()

        @pl.when(s == last)
        def _():
            seed_copy(step).wait()
            length = lens_ref[side, :1, :1]
            for index, block in enumerate(row_blocks(0, half)):
                row = c * half + index * BLOCK + lax.broadcasted_iota(jnp.int32, (BLOCK, part), 0)
                position = row - 2 * slot + segment * tok
                valid = (row >= 2 * slot) & (position.astype(F32) < length)
                for section in range(sections):
                    work[block, section * part : (section + 1) * part] = jnp.where(
                        valid, gp_in[step, section, block, :].astype(F32), 0.0
                    )

            @pl.when((c == 0) & (step >= 2))
            def _():
                carry_move(step - 2).wait_recv()
                work[slot : 2 * slot, :] = carb[step - 2]

        sends = []
        for index, (start, size) in enumerate(chunks):
            span = pl.ds(start, size)

            @pl.when(s < last)
            def _():
                handoff(step, index).wait_recv()
                for block in row_blocks(start, size):
                    work[block, :] = gb[step, block, :].astype(F32)

            gain_sum = jnp.zeros((BLOCK // 2, D), F32)
            shift_sum = jnp.zeros((BLOCK // 2, D), F32)
            for block in row_blocks(start, size):
                g = work[block, :]
                z = z2b[side, block, :]
                back = norm_back(g, z, r2b[side, block, :1], gain_two[...])
                dsec[block, :] = back
                dfe[block, :] = back.astype(BF)
                gain_sum += folded_rows(g * z)
                shift_sum += folded_rows(g)
            o_small[2:3, :] += jnp.sum(gain_sum, axis=0, keepdims=True)
            o_small[3:4, :] += jnp.sum(shift_sum, axis=0, keepdims=True)
            if index == 0:
                pl.when(first)(weights[0].wait)
            for lanes in pieces(FF):
                slope = gpb[side, span, lanes].astype(F32)
                pre = (dot(dfe[span], vdown[:, lanes]) * slope).astype(BF)
                dpre[span, lanes] = pre
                row, column = divmod(lanes.start, D)
                o_small[4 + row : 5 + row, column : column + STEP] += jnp.sum(
                    pre.astype(F32), axis=0, keepdims=True
                )
            if index == 0:
                pl.when(first)(weights[1].wait)
            for lanes in pieces(D):
                work[span, lanes] = dsec[span, lanes] + dot(dpre[span], vin[:, lanes])
            gain_sum = jnp.zeros((BLOCK // 2, D), F32)
            shift_sum = jnp.zeros((BLOCK // 2, D), F32)
            for block in row_blocks(start, size):
                g = work[block, :]
                z = z1b[side, block, :]
                back = norm_back(g, z, r1b[side, block, :1], gain_one[...])
                work[block, :] = back
                dbr[block, :] = back.astype(BF)
                gain_sum += folded_rows(g * z)
                shift_sum += folded_rows(g)
            o_small[0:1, :] += jnp.sum(gain_sum, axis=0, keepdims=True)
            o_small[1:2, :] += jnp.sum(shift_sum, axis=0, keepdims=True)
            if index == 0:
                pl.when(first)(weights[2].wait)
            for lanes in pieces(D):
                da[span, lanes] = dot(dbr[span], vproj[:, lanes]).astype(BF)
            for pair in range(PAIRS):
                keys = kvb[side, :, pair_span(pair)]
                values = kvb[side, :, pair_span(pair, D)]
                da2 = stacked_pair(da[span, pair_span(pair)])
                q2 = scaled_queries(qb[side, span, pair_span(pair)])
                dp_ref = dp_tmp.at[pair % 2]
                ds_ref = ds_tmp.at[pair % 2]
                wide = 2 * size
                dp_ref[:, :wide] = dot_nt(values, da2)
                for begin in range(0, wide, 128):
                    lanes = slice(begin, min(begin + 128, wide))
                    kept_lanes = slice(2 * start + begin, 2 * start + lanes.stop)
                    total = jnp.zeros((BLOCK, lanes.stop - begin), F32)
                    for offset in range(0, rows, BLOCK):
                        block = pl.ds(offset, BLOCK)
                        total += probs[side, pair, block, kept_lanes].astype(F32) * dp_ref[block, lanes]
                    total = jnp.sum(total, axis=0, keepdims=True)
                    for offset in range(0, rows, BLOCK):
                        block = pl.ds(offset, BLOCK)
                        ds_ref[block, lanes] = (
                            probs[side, pair, block, kept_lanes].astype(F32) * (dp_ref[block, lanes] - total)
                        ).astype(BF)
                d_keys = dot(ds_ref[:, :wide], q2)
                d_values = dot(probs[side, pair, :, 2 * start : 2 * start + wide], da2)
                if index == 0:
                    dkv[pair, :, :WIDE] = d_keys
                    dkv[pair, :, WIDE:] = d_values
                else:
                    dkv[pair, :, :WIDE] += d_keys
                    dkv[pair, :, WIDE:] += d_values
                if index == len(chunks) - 1:
                    move = remote(
                        dkv.at[pair, theirs],
                        dkv_in.at[side, pair],
                        kv_send.at[pair],
                        kv_recv.at[step, pair],
                        (s, place.other),
                    )
                    move.start()
                    sends.append(move)
                both = dot_tn(keys, ds_ref[:, :wide])
                lane = lax.broadcasted_iota(jnp.int32, (WIDE, size), 0)
                upright = jnp.where(lane < HEAD, both[:, :size], both[:, size:])
                dpj[span, pair_span(pair)] = (jnp.transpose(upright) * HEAD**-0.5).astype(BF)
        pl.when(first)(weights[3].wait)
        for pair in range(PAIRS):
            sends[pair].wait_recv()
            for which in range(2):
                lanes = slice(which * WIDE, (which + 1) * WIDE)
                dpj[:, pair_span(pair, (which + 1) * D)] = (
                    dkv[pair, own, lanes] + dkv_in[side, pair, :, lanes]
                ).astype(BF)
        for index, (start, size) in enumerate(chunks):
            span = pl.ds(start, size)
            for lanes in pieces(D):
                dxb[side, span, lanes] = (
                    work[span, lanes] + dot(dpj[span], vqkv[:, lanes])
                ).astype(BF)
            pl.when(s > 0)(handoff(step, index).start)
            if index == 0:

                @pl.when((s == 0) & (c == 0))
                def _():
                    mgb[step] = dxb[side, :slot].astype(F32) + dxb[side, slot : 2 * slot].astype(F32)
                    pl.when(step < steps - 2)(carry_move(step).start)

        for section in range(sections):
            dg[side, section] = dxb[side, :, section * part : (section + 1) * part]
        for copy in outgoing(step):
            copy.start()
        outgoing_dx(step).start()
        for move in sends:
            move.wait_send()

        @pl.when(step < steps - 2)
        def _():
            for copy in residuals(step + 2):
                copy.start()

    def one_round(turn, state):
        even, odd = 2 * turn, 2 * turn + 1
        late = (s == last) & (turn == 0)
        prologue(even)
        pl.when(jnp.logical_not(late))(lambda: prologue(odd))
        main(even)
        pl.when(late)(lambda: prologue(odd))
        main(odd)
        return state

    lax.fori_loop(0, segments, one_round, 0)
    settle(steps - 2)
    settle(steps - 1)
    for copy in outgoing(steps - 1):
        copy.wait()

    @pl.when((s == 0) & (c == 0))
    def _():
        for step in range(steps - 2, steps):
            outgoing_memory(step).start()
        for step in range(steps - 2, steps):
            outgoing_memory(step).wait()
        for step in range(steps - 2):
            carry_move(step).wait_send()


def backward(sections, segments, geometry, collective, g0, lens, kept, weights):
    mem, slot, tok, rows = geometry
    half = rows // 2
    steps = 2 * segments

    def grad(width):
        return jax.ShapeDtypeStruct((steps, half, width), BF)

    outs = (
        grad(3 * D),
        grad(D),
        grad(FF),
        grad(D),
        jax.ShapeDtypeStruct(g0.shape, BF),
        jax.ShapeDtypeStruct((2, slot, D), F32),
        jax.ShapeDtypeStruct((8, D), F32),
    )
    dma = pltpu.SemaphoreType.DMA
    return pl.pallas_call(
        functools.partial(backward_kernel, sections, segments, geometry),
        name="backward_layer",
        out_shape=outs,
        in_specs=[ANY, VMEM] + [ANY] * 5 + [ANY] * 4 + [VMEM] * 2,
        out_specs=(ANY,) * 6 + (VMEM,),
        scratch_shapes=[
            pltpu.VMEM((3 * D, D), BF),
            pltpu.VMEM((D, D), BF),
            pltpu.VMEM((FF, D), BF),
            pltpu.VMEM((D, FF), BF),
            pltpu.VMEM((steps, half, D), BF),
            pltpu.VMEM((2, half, D), BF),
            pltpu.VMEM((2, rows, 2 * D), BF),
            pltpu.VMEM((2, half, FF), BF),
            pltpu.VMEM((2, half, D), F32),
            pltpu.VMEM((2, half, D), F32),
            pltpu.VMEM((2, half, 128), F32),
            pltpu.VMEM((2, half, 128), F32),
            pltpu.VMEM((2, PAIRS, rows, rows), BF),
            pltpu.VMEM((half, D), F32),
            pltpu.VMEM((half, D), F32),
            pltpu.VMEM((half, D), BF),
            pltpu.VMEM((half, FF), BF),
            pltpu.VMEM((half, D), BF),
            pltpu.VMEM((half, D), BF),
            pltpu.VMEM((2, rows, rows), F32),
            pltpu.VMEM((2, rows, rows), BF),
            pltpu.VMEM((PAIRS, rows, 2 * WIDE), F32),
            pltpu.VMEM((2, PAIRS, half, 2 * WIDE), F32),
            pltpu.VMEM((half, 3 * D), BF),
            pltpu.VMEM((2, half, D), BF),
            pltpu.VMEM((steps, slot, D), F32),
            pltpu.VMEM((steps, slot, D), F32),
            pltpu.VMEM(g0.shape, BF),
            pltpu.VMEM((2,) + g0.shape[1:], BF),
            dma((4,)),
            dma((2, 5)),
            dma((steps,)),
            dma((6,)),
            dma((PAIRS,)),
            dma((steps, PAIRS)),
            dma((2, 2)),
            dma((steps, 2)),
            dma((steps,)),
            dma((steps,)),
        ],
        compiler_params=pltpu.CompilerParams(
            collective_id=collective, has_side_effects=True, vmem_limit_bytes=VMEM_LIMIT
        ),
    )(g0, lens, *kept, *weights)


def reduce_order(line):
    order = []
    low, high = 0, line - 1
    while low <= high:
        order.append(high)
        if low != high:
            order.append(low)
        low, high = low + 1, high - 1
    return order


def arrival_orders(line):
    def moment(chip, dest):
        upward = (line - 1 - dest) + chip
        downward = dest + (line - 1 - chip)
        if dest == chip:
            return line
        return upward if dest > chip else downward

    return [
        sorted(range(line), key=functools.partial(moment, chip)) for chip in range(line)
    ]


def finish_kernel(sections, segments, line, *refs):
    refs = list(refs)

    def take(count):
        taken = refs[:count]
        del refs[:count]
        return taken

    hid, dx, mem_in = take(3)
    lefts_in, rights_in, small_in = (take(4), take(4), take(1)[0]) if line else ((), (), None)
    o_h, o_x, o_m = take(3)
    outs = take(5) if line else ()
    h_send, h_got, x_send, x_got, m_send, m_got = take(6)
    place = Place(sections)
    s, c, d = place.s, place.c, place.d
    last = sections - 1
    steps = 2 * segments
    half = hid.shape[2]
    z = lax.div(d, 2)
    greet_plane(place, sections)
    if line:
        parts, sibs, ins, accs = take(5), take(5), take(5), take(5)
        big0, big1, flat0, flat1, flat2, flat3, turned = take(7)
        load, c_send, c_got, z_send, z_right, z_left, fin = take(7)
        up, down = (s, d + 2), (s, d - 2)

        def greet(target):
            pl.semaphore_signal(
                pltpu.get_barrier_semaphore(), inc=1, device_id=target, device_id_type=MESH
            )

        pl.when(z < line - 1)(lambda: greet(up))
        pl.when(z > 0)(lambda: greet(down))
        ends = (z == 0) | (z == line - 1)
        plane_wait(sections, jnp.where(ends, 1, 2))
    else:
        plane_wait(sections, 0)

    def deliveries():
        for src, dst, origin, send, got in (
            (hid, o_h, last, h_send, h_got),
            (dx, o_x, 0, x_send, x_got),
        ):
            for step in range(steps):
                segment, item = divmod(step, 2)
                rows = pl.ds(pl.multiple_of(c * half, BLOCK), half)
                for section in range(sections):
                    here = (s == section) & (c == item)
                    far = functools.partial(remote,
                        src.at[step, section],
                        dst.at[segment, rows],
                        send.at[step, section],
                        got.at[segment, c],
                        (section, place.base + item),
                    )
                    near = functools.partial(pltpu.make_async_copy,
                        src.at[step, section], dst.at[segment, rows], got.at[segment, c]
                    )
                    yield s == origin, here, far, near
        for item in range(2):
            for section in range(sections):
                here = (s == section) & (c == item)
                far = functools.partial(remote,
                    mem_in.at[item, section],
                    o_m,
                    m_send.at[item, section],
                    m_got.at[0],
                    (section, place.base + item),
                )
                near = functools.partial(pltpu.make_async_copy, mem_in.at[item, section], o_m, m_got.at[0])
                yield (s == 0) & (c == 0), here, far, near

    for mine, here, far, near in deliveries():
        pl.when(mine & jnp.logical_not(here))(lambda far=far: far().start())
        pl.when(mine & here)(lambda near=near: near().start())

    if line:
        act_in, nb_in, x_in, att_in = lefts_in
        dfe_in, dpre_in, dpj_in, dbr_in = rights_in

        def fetch(src, dst, slot):
            width = src.shape[-1]
            return [
                pltpu.make_async_copy(
                    src.at[step], dst.at[pl.ds(step * half, half), :width], load.at[slot, step]
                )
                for step in range(steps)
            ]

        loads = {
            "nb": fetch(nb_in, flat1, 0),
            "dpre": fetch(dpre_in, big1, 1),
            "act": fetch(act_in, big0, 2),
            "dfe": fetch(dfe_in, flat0, 3),
            "att": fetch(att_in, flat2, 4),
            "dbr": fetch(dbr_in, flat3, 5),
            "dpj": fetch(dpj_in, big0, 2),
            "x": fetch(x_in, flat0, 3),
        }

        def begin(name):
            for copy in loads[name]:
                copy.start()

        def ready(name):
            for copy in loads[name]:
                copy.wait()

        for name in ("nb", "dpre", "act", "dfe", "att", "dbr"):
            begin(name)
        order = reduce_order(line)
        flows = [(kind, dest) for kind in range(5) for dest in order]
        depth = 2
        ends_first = (
            ([flow for flow in flows if flow[1] > 0], 1, 0),
            ([flow for flow in flows if flow[1] < line - 1], -1, line - 1),
        )

        def arrival(position):
            dest = 0
            for chip, row in enumerate(arrival_orders(line)):
                for index, value in enumerate(row):
                    dest += jnp.where((z == chip) & (position == index), value, 0)
            return dest

        def own_rows(kind):
            block = parts[kind].shape[1] // 2
            return pl.ds(pl.multiple_of(c * block, 8), block)

        def core_move(kind, dest):
            block = parts[kind].shape[1] // 2
            theirs = pl.ds(pl.multiple_of((1 - c) * block, 8), block)
            return remote(
                parts[kind].at[dest, theirs],
                sibs[kind].at[dest],
                c_send.at[kind, dest],
                c_got.at[kind, dest],
                (s, place.other),
            )

        def line_move(kind, dest, towards):
            if towards > 0:
                slot, target, got = dest, up, z_right
            else:
                slot, target, got = jnp.where(z - 1 == dest, line, dest), down, z_left
            return remote(
                parts[kind].at[dest, own_rows(kind)],
                ins[kind].at[slot],
                z_send.at[kind, dest],
                got.at[kind, dest],
                target,
            )

        def add(kind, dest, ref, slot):
            acc = accs[kind]
            rows = min(BLOCK, acc.shape[0])

            def block(index, state):
                span = pl.ds(pl.multiple_of(index * rows, rows), rows)
                acc[span, :] += ref[slot, span, :].astype(F32)
                return state

            lax.fori_loop(0, acc.shape[0] // rows, block, 0)

        def hop(kind, dest):
            acc = accs[kind]
            core_move(kind, dest).wait_recv()
            acc[...] = parts[kind][dest, own_rows(kind), :].astype(F32)
            add(kind, dest, sibs[kind], dest)

            @pl.when((z > 0) & (z <= dest))
            def _():
                line_move(kind, dest, 1).wait_recv()
                add(kind, dest, ins[kind], dest)

            @pl.when((z < line - 1) & (z >= dest))
            def _():
                line_move(kind, dest, -1).wait_recv()
                add(kind, dest, ins[kind], jnp.where(z == dest, line, dest))

            @pl.when(z != dest)
            def _():
                parts[kind][dest, own_rows(kind), :] = acc[...].astype(parts[kind].dtype)

            for sequence, towards, end in ends_first if isinstance(dest, int) else ():
                spot = sequence.index((kind, dest)) if (kind, dest) in sequence else 0
                if spot >= depth:
                    earlier = functools.partial(line_move, *sequence[spot - depth], towards)
                    pl.when(z == end)(lambda earlier=earlier: earlier().wait_send())
            pl.when(z < dest)(lambda: line_move(kind, dest, 1).start())
            pl.when(z > dest)(lambda: line_move(kind, dest, -1).start())

            @pl.when(z == dest)
            def _():
                copy = pltpu.make_async_copy(acc, outs[kind], fin.at[kind])
                copy.start()
                copy.wait()

        def no_wait(dest):
            return ((z == 0) & (dest > 0)) | ((z == line - 1) & (dest < line - 1))

        matrices = (
            (flat1, big1, FF),
            (big0, flat0, D),
            (flat0, big0, 3 * D),
            (flat2, flat3, D),
        )
        for kind, (left, right, width) in enumerate(matrices):
            if kind == 0:
                ready("nb")
                ready("dpre")
            elif kind == 1:
                ready("act")
                ready("dfe")
            elif kind == 2:
                begin("dpj")
                begin("x")
                ready("dpj")
                ready("x")
            else:
                ready("att")
                ready("dbr")
            block = parts[kind].shape[1]
            for dest in order:
                turned[:block, :] = jnp.transpose(left[:, dest * block : (dest + 1) * block])
                for lanes in pieces(width):
                    parts[kind][dest, :, lanes] = dot(turned[:block, :], right[:, lanes]).astype(BF)
                core_move(kind, dest).start()
                place_in_flow = flows.index((kind, dest))
                if place_in_flow > 0:
                    before = flows[place_in_flow - 1]
                    pl.when(no_wait(before[1]))(functools.partial(hop, *before))
        for dest in order:
            copy = pltpu.make_async_copy(small_in.at[dest], parts[4].at[dest], fin.at[4])
            copy.start()
            copy.wait()
            core_move(4, dest).start()
        first_of_small = flows.index((4, order[0]))
        for kind, dest in flows[first_of_small - 1 :]:
            pl.when(no_wait(dest))(functools.partial(hop, kind, dest))
        for kind in range(5):

            def by_arrival(position, state):
                dest = arrival(position)
                pl.when(jnp.logical_not(no_wait(dest)))(lambda: hop(kind, dest))
                return state

            lax.fori_loop(0, line, by_arrival, 0)
        for kind, dest in flows:
            core_move(kind, dest).wait_send()
            for sequence, towards, end in ends_first:
                if (kind, dest) in sequence:
                    pending = (z < dest) if towards > 0 else (z > dest)
                    if (kind, dest) not in sequence[-depth:]:
                        pending &= z != end
                    pl.when(pending)(lambda: line_move(kind, dest, towards).wait_send())

    for mine, here, far, near in deliveries():
        pl.when(mine & jnp.logical_not(here))(lambda far=far: far().wait_send())
    for src, dst, origin, got in ((hid, o_h, last, h_got), (dx, o_x, 0, x_got)):
        for segment in range(segments):
            for core in range(2):
                rows = pl.ds(core * half, half)
                here = (s == origin) & (c == core)
                far = functools.partial(remote,
                    src.at[0, 0], dst.at[segment, rows], h_send.at[0, 0], got.at[segment, core], (s, d)
                )
                near = functools.partial(pltpu.make_async_copy, src.at[0, 0], dst.at[segment, rows], got.at[segment, core])
                pl.when(jnp.logical_not(here))(lambda far=far: far().wait_recv())
                pl.when(here)(lambda near=near: near().wait())
    here = (s == 0) & (c == 0)
    far = functools.partial(remote, mem_in.at[0, 0], o_m, m_send.at[0, 0], m_got.at[0], (s, d))
    near = functools.partial(pltpu.make_async_copy, mem_in.at[0, 0], o_m, m_got.at[0])
    pl.when(jnp.logical_not(here))(lambda far=far: far().wait_recv())
    pl.when(here)(lambda near=near: near().wait())


def finish(sections, segments, line, collective, hid, dx, memory_term, sums):
    steps, _, half, part = hid.shape
    slot = memory_term.shape[2]
    dma = pltpu.SemaphoreType.DMA
    outs = [
        jax.ShapeDtypeStruct((segments, 2 * half, part), BF),
        jax.ShapeDtypeStruct((segments, 2 * half, part), BF),
        jax.ShapeDtypeStruct((slot, part), F32),
    ]
    scratch = [
        dma((steps, sections)),
        dma((segments, 2)),
        dma((steps, sections)),
        dma((segments, 2)),
        dma((2, sections)),
        dma((1,)),
    ]
    operands = [hid, dx, memory_term]
    if line:
        lefts, rights, small = sums
        operands += [*lefts, *rights, small]
        block = D // (2 * line)
        shapes = (
            (block, FF, BF),
            (FF // (2 * line), D, BF),
            (block, 3 * D, BF),
            (block, D, BF),
            (8, D, F32),
        )
        outs += [jax.ShapeDtypeStruct(shape[:2], F32) for shape in shapes]
        total = steps * half
        scratch += [pltpu.VMEM((line, 2 * rows, width), kind) for rows, width, kind in shapes]
        scratch += [pltpu.VMEM((line, rows, width), kind) for rows, width, kind in shapes]
        scratch += [pltpu.VMEM((line + 1, rows, width), kind) for rows, width, kind in shapes]
        scratch += [pltpu.VMEM((rows, width), F32) for rows, width, kind in shapes]
        scratch += [pltpu.VMEM((total, FF), BF)] * 2 + [pltpu.VMEM((total, D), BF)] * 4
        scratch += [pltpu.VMEM((FF // line, total), BF)]
        scratch += [
            dma((6, steps)),
            dma((5, line)),
            dma((5, line)),
            dma((5, line)),
            dma((5, line)),
            dma((5, line)),
            dma((5,)),
        ]
    return pl.pallas_call(
        functools.partial(finish_kernel, sections, segments, line),
        name="finish",
        out_shape=tuple(outs),
        in_specs=[ANY] * len(operands),
        out_specs=(ANY,) * len(outs),
        scratch_shapes=scratch,
        compiler_params=pltpu.CompilerParams(
            collective_id=collective, has_side_effects=True, vmem_limit_bytes=VMEM_LIMIT
        ),
    )(*operands)


def on_device(
    sections,
    inputs,
    out_grad,
    memory,
    lengths,
    w_qkv,
    w_proj,
    gain_one,
    shift_one,
    w_in,
    b_in,
    w_down,
    gain_two,
    shift_two,
):
    segs, tok, part = inputs.shape[1:]
    mem = memory.shape[1]
    slot = -(-mem // BLOCK) * BLOCK
    rows = -(-(2 * slot + tok) // (2 * BLOCK)) * 2 * BLOCK
    half = rows // 2
    geometry = (mem, slot, tok, rows)
    back_pad = rows - 2 * slot - tok

    head = jnp.pad(memory[:1], ((0, segs - 1), (0, slot - mem), (0, 0)))
    blank = jnp.zeros((segs, back_pad, part), BF)
    tokens = jnp.concatenate([head, head, inputs[0], blank], axis=1)
    cotangent = jnp.pad(out_grad[0], ((0, 0), (2 * slot, back_pad), (0, 0)))
    length_tile = jnp.broadcast_to(lengths.astype(F32), (8, 128))

    def halves(array):
        return array.reshape(segs, 2, half, part)

    matrices = (w_qkv[0], w_proj[0], w_in[0], w_down[0])
    forward_weights = matrices + (gain_one, shift_one, b_in, gain_two, shift_two)
    x, q, kv, att, nb, act, gp, s1, s2, hid, *turned, g0, lens = forward(
        sections, segs, geometry, 0, halves(tokens), halves(cotangent), length_tile, forward_weights
    )
    dpj, dbr, dpre, dfe, dx, memory_term, small = backward(
        sections, segs, geometry, 1, g0, lens, (q, kv, gp, s1, s2), (*turned, gain_one, gain_two)
    )
    memory_term = memory_term.reshape(2, slot, sections, part).transpose(0, 2, 1, 3)
    devices = lax.axis_size("dp")
    lefts, rights = (act, nb, x, att), (dfe, dpre, dpj, dbr)
    vectors = [row.reshape(devices, -1) for row in (small[0], small[1], small[2], small[3], small[4:8])]
    shares = jnp.concatenate(vectors, axis=1)
    line = devices // 2 if D % (devices * BLOCK) == 0 and devices > 2 else 0
    sums = None
    if line:
        tiles = jnp.pad(shares[:, None], ((0, 0), (0, 7), (0, 0))).reshape(line, 16, D)
        sums = (lefts, rights, tiles)
    out_parts, in_parts, memory_part, *reduced = finish(
        sections, segs, line, 2, hid, dx, memory_term, sums
    )

    def owned(parts):
        return parts[:, 2 * slot : 2 * slot + tok]

    position = jnp.arange(segs * tok, dtype=jnp.int32).reshape(segs, tok)
    token_valid = position < lengths[0]
    outputs = jnp.where(token_valid[:, :, None], owned(out_parts), jnp.zeros((), BF))
    input_grad = owned(in_parts)
    memory_grad = memory_part[:mem]

    if line:
        d_in, d_down, d_qkv, d_proj, share = reduced
        share = share[:1]
    else:

        def weight_grad(left, right):
            full = jnp.einsum(
                "rd,re->de",
                left.reshape(2 * segs * half, -1),
                right.reshape(2 * segs * half, -1),
                preferred_element_type=F32,
            )
            return lax.psum_scatter(full.astype(BF), "dp", scatter_dimension=0, tiled=True).astype(F32)

        d_down, d_in, d_qkv, d_proj = [weight_grad(*pair) for pair in zip(lefts, rights)]
        share = lax.psum_scatter(shares, "dp", scatter_dimension=0, tiled=True)
    size = D // devices
    gain_one_share, shift_one_share, gain_two_share, shift_two_share = (
        share[:, k * size : (k + 1) * size] for k in range(4)
    )
    b_in_share = share[:, 4 * size :]

    return (
        outputs[None],
        input_grad[None],
        memory_grad[None],
        d_qkv[None],
        d_proj[None],
        gain_one_share,
        shift_one_share,
        d_in[None],
        b_in_share,
        d_down[None],
        gain_two_share,
        shift_two_share,
    )


def solution(mesh):
    return jax.shard_map(
        functools.partial(on_device, mesh.shape["section"]),
        mesh=mesh,
        in_specs=(
            P("dp", None, None, "section"),
            P("dp", None, None, "section"),
            P("dp", None, "section"),
            P("dp"),
            P("section", None, None),
            P("section", None, None),
            P("section", None),
            P("section", None),
            P("section", None, None),
            P("section", None),
            P("section", None, None),
            P("section", None),
            P("section", None),
        ),
        out_specs=(
            P("dp", None, None, "section"),
            P("dp", None, None, "section"),
            P("dp", None, "section"),
            P("section", "dp", None),
            P("section", "dp", None),
            P("section", "dp"),
            P("section", "dp"),
            P("section", "dp", None),
            P("section", "dp"),
            P("section", "dp", None),
            P("section", "dp"),
            P("section", "dp"),
        ),
        check_vma=False,
    )
```

```python
import functools

import jax
import jax.numpy as jnp
from jax import lax
from jax.experimental import pallas as pl
from jax.experimental.pallas import tpu as pltpu
from jax.sharding import PartitionSpec as P

D = 768
H = 12
HEAD = 64
FF = 3072
PAIRS = H // 2
WIDE = 2 * HEAD
STEP = 256
BLOCK = 16
BF = jnp.bfloat16
F32 = jnp.float32
MESH = pl.DeviceIdType.MESH
ANY = pl.BlockSpec(memory_space=pl.ANY)
VMEM = pl.BlockSpec(memory_space=pltpu.VMEM)
VMEM_LIMIT = 63 * 1024 * 1024


def dot(a, b):
    return jnp.dot(a, b, preferred_element_type=F32)


def dot_nt(a, b):
    return lax.dot_general(a, b, (((1,), (1,)), ((), ())), preferred_element_type=F32)


def dot_tn(a, b):
    return lax.dot_general(a, b, (((0,), (0,)), ((), ())), preferred_element_type=F32)


def cols(index):
    return pl.ds(index * STEP, STEP)


def remote(src, dst, send, recv, target):
    return pltpu.make_async_remote_copy(
        src_ref=src, dst_ref=dst, send_sem=send, recv_sem=recv, device_id=target, device_id_type=MESH
    )


class Place:
    def __init__(self, sections):
        self.s = lax.axis_index("section")
        self.d = lax.axis_index("dp")
        self.c = lax.rem(self.d, 2)
        self.base = self.d - self.c
        self.other = self.base + 1 - self.c
        self.next = lax.rem(self.s + 1, sections)
        self.prev = lax.rem(self.s + sections - 1, sections)


def greet_plane(place, sections):
    barrier = pltpu.get_barrier_semaphore()
    for section in range(sections):
        for core in range(2):

            @pl.when((place.s != section) | (place.c != core))
            def _():
                pl.semaphore_signal(
                    barrier, inc=1, device_id=(section, place.base + core), device_id_type=MESH
                )


def plane_wait(sections, extra):
    pl.semaphore_wait(pltpu.get_barrier_semaphore(), 2 * sections - 1 + extra)


def key_bias(geometry, segment, length, shape, dim):
    mem, slot, tok, rows = geometry
    row = lax.broadcasted_iota(jnp.int32, shape, dim)
    position = row - 2 * slot + segment * tok
    is_token = (row >= 2 * slot) & (row < 2 * slot + tok) & (position.astype(F32) < length)
    is_memory = (row < mem) | ((row >= slot) & (row < slot + mem))
    return jnp.where(is_token | is_memory, 0.0, -1e30)


def stacked_pair(pair):
    lane = lax.broadcasted_iota(jnp.int32, pair.shape, 1)
    zero = jnp.zeros_like(pair)
    return jnp.concatenate(
        [jnp.where(lane < HEAD, pair, zero), jnp.where(lane >= HEAD, pair, zero)], axis=0
    )


def folded_pair(both):
    half = both.shape[0] // 2
    lane = lax.broadcasted_iota(jnp.int32, (half, WIDE), 1)
    return jnp.where(lane < HEAD, both[:half], both[half:])


def upright(both):
    size = both.shape[1] // 2
    row = lax.broadcasted_iota(jnp.int32, (WIDE, size), 0)
    return jnp.transpose(jnp.where(row < HEAD, both[:, :size], both[:, size:]))


def scaled_queries(queries):
    return stacked_pair(queries * jnp.asarray(HEAD**-0.5, BF))


def normalized(rows):
    center = rows - jnp.mean(rows, axis=-1, keepdims=True)
    spread_of = jnp.mean(center * center, axis=-1, keepdims=True)
    scale = lax.rsqrt(spread_of + 1e-06)
    return center * scale, scale


def pieces(width, step=STEP):
    return [slice(start, start + step) for start in range(0, width, step)]


def row_chunks(half):
    first = half // 2 // BLOCK * BLOCK
    return ((0, first), (first, half - first))


def lane_starts(chunks):
    starts, total = [], 0
    for _, size in chunks:
        starts.append(total)
        total += -(-2 * size // 128) * 128
    return starts, total


def row_blocks(start, size):
    return [pl.ds(start + offset, BLOCK) for offset in range(0, size, BLOCK)]


def pair_span(pair, offset=0):
    return slice(offset + pair * WIDE, offset + (pair + 1) * WIDE)


def forward_kernel(
    sections,
    segments,
    geometry,
    a_ref,
    g_ref,
    len_ref,
    w_qkv,
    w_proj,
    w_in,
    w_down,
    gain_one,
    shift_one,
    b_in,
    gain_two,
    shift_two,
    o_x,
    o_q,
    o_kv,
    o_att,
    o_nb,
    o_act,
    o_gp,
    o_s1,
    o_s2,
    o_hid,
    t_qkv,
    t_proj,
    t_in,
    t_down,
    o_g,
    o_lens,
    vqkv,
    vproj,
    vin,
    vdown,
    xb,
    kvb,
    qb,
    attb,
    nbb,
    actb,
    gpb,
    s1b,
    s2b,
    hb,
    preb,
    nf,
    memb,
    s_tmp,
    probs,
    turned,
    xp,
    hg,
    lens_ref,
    wsem,
    osem,
    kv_send,
    kv_recv,
    h_send,
    h_recv,
    m_send,
    m_recv,
    tsem,
    a_send,
    a_got,
    g_send,
    g_got,
    l_send,
    l_got,
):
    place = Place(sections)
    s, c = place.s, place.c
    mem, slot, tok, rows = geometry
    half = rows // 2
    last = sections - 1
    steps = 2 * segments
    chunks = row_chunks(half)
    early = s >= 2
    weights = [
        pltpu.make_async_copy(src, dst, wsem.at[k])
        for k, (src, dst) in enumerate(((w_qkv, vqkv), (w_proj, vproj), (w_in, vin), (w_down, vdown)))
    ]

    part = a_ref.shape[-1]
    greet_plane(place, sections)
    plane_wait(sections, 0)

    def spread(src, dst, target, send, got, segment):
        step = 2 * segment + c
        for core in range(2):
            here = (s == target) & (c == core)
            far = functools.partial(remote,
                src.at[segment, core],
                dst.at[step, s],
                send.at[segment, core],
                got.at[step, s],
                (target, place.base + core),
            )
            near = functools.partial(pltpu.make_async_copy, src.at[segment, core], dst.at[step, s], got.at[step, s])
            yield here, far, near

    def tokens(segment):
        return spread(a_ref, xp, 0, a_send, a_got, segment)

    def cotangents(segment):
        return spread(g_ref, o_g, last, g_send, g_got, segment)

    def begin(moves):
        for here, far, near in moves:
            pl.when(jnp.logical_not(here))(lambda far=far: far().start())
            pl.when(here)(lambda near=near: near().start())

    def sent(moves):
        for here, far, _ in moves:
            pl.when(jnp.logical_not(here))(lambda far=far: far().wait_send())

    def arrived(src, dst, got, target, step, section):
        side = lax.rem(step, 2)
        here = (section == target) & (side == c)
        far = functools.partial(remote,
            src.at[0, 0], dst.at[step, section], a_send.at[0, 0], got.at[step, section], (s, place.d)
        )
        near = functools.partial(pltpu.make_async_copy, src.at[0, 0], dst.at[step, section], got.at[step, section])
        pl.when(jnp.logical_not(here))(lambda far=far: far().wait_recv())
        pl.when(here)(lambda near=near: near().wait())

    begin(tokens(0))
    length_move = remote(len_ref, lens_ref.at[c], l_send.at[0], l_got.at[0], (s, place.other))
    length_move.start()
    lens_ref[c] = len_ref[...]
    for copy in weights:
        copy.start()
    sent(tokens(0))
    for segment in range(1, segments):
        begin(tokens(segment))
    for segment in range(segments):
        begin(cotangents(segment))
    remote(len_ref, lens_ref.at[1 - c], l_send.at[0], l_got.at[0], (s, place.other)).wait_recv()

    def outgoing(step):
        side = lax.rem(step, 2)
        pairs = (
            (xb.at[step], o_x),
            (kvb.at[step], o_kv),
            (qb.at[side], o_q),
            (attb.at[side], o_att),
            (nbb.at[side], o_nb),
            (actb.at[side], o_act),
            (gpb.at[side], o_gp),
            (s1b.at[side], o_s1),
            (s2b.at[side], o_s2),
            (hg.at[side], o_hid),
        )
        return [
            pltpu.make_async_copy(src, dst.at[step], osem.at[side, k])
            for k, (src, dst) in enumerate(pairs)
        ]

    def handoff(step, index):
        start, size = chunks[index]
        side = lax.rem(step, 2)
        span = pl.ds(start, size)
        return remote(
            hb.at[side, span],
            xb.at[step, span],
            h_send.at[side, index],
            h_recv.at[step, index],
            (place.next, place.d),
        )

    def memory_move(step):
        side = lax.rem(step, 2)
        return remote(
            hb.at[side, pl.ds(slot, slot)], memb.at[step], m_send.at[side], m_recv.at[step], (0, place.d)
        )

    def exchange(step, index):
        start, size = chunks[index]
        span = pl.ds(pl.multiple_of(c * half + start, BLOCK), size)
        return remote(
            kvb.at[step, span],
            kvb.at[step, span],
            kv_send.at[index],
            kv_recv.at[step, index],
            (s, place.other),
        )

    def settle(step):
        @pl.when(s < last)
        def _():
            for index in range(len(chunks)):
                handoff(step, index).wait_send()

        @pl.when((s == last) & (c == 0) & (step < steps - 2))
        def _():
            memory_move(step).wait_send()

        for copy in outgoing(step):
            copy.wait()

    def turn_weights():
        @pl.when(early)
        def _():
            for copy in weights:
                copy.wait()

        blocks = []
        for src, dst in ((vqkv, t_qkv), (vproj, t_proj), (vin, t_in), (vdown, t_down)):
            for block in range(src.shape[0] * src.shape[1] // (D * D)):
                span = pl.ds(block * D, D)
                if src.shape[0] == D:
                    blocks.append((src, (slice(None), span), dst.at[span]))
                else:
                    blocks.append((src, (span, slice(None)), dst.at[:, span]))
        moves = []
        for index, (src, where, dst) in enumerate(blocks):
            spot = index % 3
            if index >= 3:
                moves[index - 3].wait()
            turned[spot] = jnp.transpose(src[where])
            moves.append(pltpu.make_async_copy(turned.at[spot], dst, tsem.at[spot]))
            moves[-1].start()
        for move in moves[-3:]:
            move.wait()

    def one_step(step, state):
        pl.when(step == jnp.where(early, 0, steps))(turn_weights)
        pl.when(step < steps)(lambda: compute_step(step))
        return state

    def compute_step(step):
        side = lax.rem(step, 2)
        segment = lax.div(step, 2)
        first = (step == 0) & jnp.logical_not(early)

        @pl.when(s == 0)
        def _():
            for section in range(sections):
                arrived(a_ref, xp, a_got, 0, step, section)
                xb[step, :, section * part : (section + 1) * part] = xp[step, section]

            @pl.when((c == 0) & (step >= 2))
            def _():
                memory_move(step - 2).wait_recv()
                xb[step, :slot] = memb[step - 2]
                xb[step, slot : 2 * slot] = memb[step - 2]

        pl.when(step >= 2)(lambda: settle(step - 2))
        for index, (start, size) in enumerate(chunks):
            span = pl.ds(start, size)

            @pl.when(s > 0)
            def _():
                handoff(step, index).wait_recv()

            if index == 0:
                pl.when(first)(weights[0].wait)
            own = pl.ds(pl.multiple_of(c * half + start, BLOCK), size)
            for lanes in pieces(2 * D):
                kvb[step, own, lanes] = dot(
                    xb[step, span], vqkv[:, D + lanes.start : D + lanes.stop]
                ).astype(BF)
            exchange(step, index).start()
            for lanes in pieces(D):
                qb[side, span, lanes] = dot(xb[step, span], vqkv[:, lanes]).astype(BF)
        bias = key_bias(geometry, segment, lens_ref[side, :1, :1], (1, rows), 1)
        for index in range(len(chunks)):
            exchange(step, index).wait_recv()
        for index, (start, size) in enumerate(chunks):
            span = pl.ds(start, size)
            for pair in range(PAIRS):
                lanes = pair_span(pair)
                s_tmp[pair % 2, : 2 * size] = dot_nt(
                    scaled_queries(qb[side, span, lanes]), kvb[step, :, lanes]
                )
                for offset in range(0, 2 * size, 2 * BLOCK):
                    block = pl.ds(offset, 2 * BLOCK)
                    scores = s_tmp[pair % 2, block, :] + bias
                    exponent = jnp.exp(scores - jnp.max(scores, axis=-1, keepdims=True))
                    inverse = 1.0 / jnp.sum(exponent, axis=-1, keepdims=True)
                    probs[pair, block, :] = (exponent * inverse).astype(BF)
            for pair in range(PAIRS):
                mixed = dot(probs[pair, : 2 * size], kvb[step, :, pair_span(pair, D)])
                attb[side, span, pair_span(pair)] = folded_pair(mixed).astype(BF)
            if index == 0:
                pl.when(first)(weights[1].wait)
            for lanes in pieces(D):
                s1b[side, span, lanes] = xb[step, span, lanes].astype(F32) + dot(
                    attb[side, span], vproj[:, lanes]
                )
            for block in row_blocks(start, size):
                z, _ = normalized(s1b[side, block, :])
                normed = z * gain_one[...] + shift_one[...]
                nf[block, :] = normed
                nbb[side, block, :] = normed.astype(BF)
            if index == 0:
                pl.when(first)(weights[2].wait)
            for lanes in pieces(FF):
                pre = dot(nbb[side, span], vin[:, lanes]) + b_in[:, lanes]
                preb[span, lanes] = pre
                actb[side, span, lanes] = (
                    0.5 * pre * (1.0 + lax.erf(pre * 0.7071067811865476))
                ).astype(BF)
            if index == 0:
                pl.when(first)(weights[3].wait)
            for lanes in pieces(D):
                s2b[side, span, lanes] = nf[span, lanes] + dot(actb[side, span], vdown[:, lanes])
            for block in row_blocks(start, size):
                z, _ = normalized(s2b[side, block, :])
                hb[side, block, :] = (z * gain_two[...] + shift_two[...]).astype(BF)

            pl.when(s < last)(handoff(step, index).start)
            if index == 0:

                @pl.when((s == last) & (c == 0) & (step < steps - 2))
                def _():
                    memory_move(step).start()

        for block in row_blocks(0, half):
            pre = preb[block, :]
            density = jnp.exp(-0.5 * pre * pre) * 0.3989422804014327
            slope = 0.5 * (1.0 + lax.erf(pre * 0.7071067811865476)) + pre * density
            gpb[side, block, :] = slope.astype(BF)
        for section in range(sections):
            hg[side, section] = hb[side, :, section * part : (section + 1) * part]
        for copy in outgoing(step):
            copy.start()
        for index in range(len(chunks)):
            exchange(step, index).wait_send()

    lax.fori_loop(0, steps + 1, one_step, 0)
    settle(steps - 2)
    settle(steps - 1)
    o_lens[...] = lens_ref[...]
    length_move.wait_send()
    for segment in range(segments):
        if segment > 0:
            sent(tokens(segment))
        sent(cotangents(segment))

    @pl.when(s == last)
    def _():
        for step in range(steps):
            for section in range(sections):
                arrived(g_ref, o_g, g_got, last, step, section)


def forward(sections, segments, geometry, collective, a, g, length_tile, weights):
    mem, slot, tok, rows = geometry
    half = rows // 2
    steps = 2 * segments
    grouped = (steps, sections, half, a.shape[-1])

    def kept(width, kind, height=half):
        return jax.ShapeDtypeStruct((steps, height, width), kind)

    outs = (
        kept(D, BF),
        kept(D, BF),
        kept(2 * D, BF, rows),
        kept(D, BF),
        kept(D, BF),
        kept(FF, BF),
        kept(FF, BF),
        kept(D, F32),
        kept(D, F32),
        jax.ShapeDtypeStruct(grouped, BF),
        jax.ShapeDtypeStruct((3 * D, D), BF),
        jax.ShapeDtypeStruct((D, D), BF),
        jax.ShapeDtypeStruct((FF, D), BF),
        jax.ShapeDtypeStruct((D, FF), BF),
        jax.ShapeDtypeStruct(grouped, BF),
        jax.ShapeDtypeStruct((2, 8, 128), F32),
    )
    dma = pltpu.SemaphoreType.DMA
    return pl.pallas_call(
        functools.partial(forward_kernel, sections, segments, geometry),
        name="forward_layer",
        out_shape=outs,
        in_specs=[ANY, ANY, VMEM] + [ANY] * 4 + [VMEM] * 5,
        out_specs=(ANY,) * (len(outs) - 1) + (VMEM,),
        scratch_shapes=[
            pltpu.VMEM((D, 3 * D), BF),
            pltpu.VMEM((D, D), BF),
            pltpu.VMEM((D, FF), BF),
            pltpu.VMEM((FF, D), BF),
            pltpu.VMEM((steps, half, D), BF),
            pltpu.VMEM((steps, rows, 2 * D), BF),
            pltpu.VMEM((2, half, D), BF),
            pltpu.VMEM((2, half, D), BF),
            pltpu.VMEM((2, half, D), BF),
            pltpu.VMEM((2, half, FF), BF),
            pltpu.VMEM((2, half, FF), BF),
            pltpu.VMEM((2, half, D), F32),
            pltpu.VMEM((2, half, D), F32),
            pltpu.VMEM((2, half, D), BF),
            pltpu.VMEM((half, FF), F32),
            pltpu.VMEM((half, D), F32),
            pltpu.VMEM((steps, slot, D), BF),
            pltpu.VMEM((2, 2 * row_chunks(half)[-1][1], rows), F32),
            pltpu.VMEM((PAIRS, 2 * row_chunks(half)[-1][1], rows), BF),
            pltpu.VMEM((3, D, D), BF),
            pltpu.VMEM(grouped, BF),
            pltpu.VMEM((2,) + grouped[1:], BF),
            pltpu.VMEM((2, 8, 128), F32),
            dma((4,)),
            dma((2, 10)),
            dma((2,)),
            dma((steps, 2)),
            dma((2, 2)),
            dma((steps, 2)),
            dma((2,)),
            dma((steps,)),
            dma((3,)),
            dma((segments, 2)),
            dma((steps, sections)),
            dma((segments, 2)),
            dma((steps, sections)),
            dma((1,)),
            dma((1,)),
        ],
        compiler_params=pltpu.CompilerParams(
            collective_id=collective, has_side_effects=True, vmem_limit_bytes=VMEM_LIMIT
        ),
    )(a, g, length_tile, *weights)


def backward_kernel(
    sections,
    segments,
    geometry,
    g0_ref,
    lens_ref,
    r_q,
    r_kv,
    r_gp,
    r_s1,
    r_s2,
    w_qkv,
    w_proj,
    w_in,
    w_down,
    gain_one,
    gain_two,
    o_dpj,
    o_dbr,
    o_dpre,
    o_dfe,
    o_dx,
    o_mg,
    o_small,
    vqkv,
    vproj,
    vin,
    vdown,
    gb,
    qb,
    kvb,
    gpb,
    z1b,
    z2b,
    attb,
    r1b,
    r2b,
    probs,
    work,
    dsec,
    dfe,
    dpre,
    dbr,
    da,
    dp_tmp,
    ds_tmp,
    dkv,
    dkv_in,
    dpj,
    dxb,
    mgb,
    carb,
    gp_in,
    dg,
    mg,
    wsem,
    rsem,
    gsem,
    osem,
    kv_send,
    kv_recv,
    h_send,
    h_recv,
    m_send,
    m_recv,
):
    place = Place(sections)
    s, c = place.s, place.c
    mem, slot, tok, rows = geometry
    half = rows // 2
    own = pl.ds(pl.multiple_of(c * half, BLOCK), half)
    theirs = pl.ds(pl.multiple_of((1 - c) * half, BLOCK), half)
    last = sections - 1
    steps = 2 * segments
    part = g0_ref.shape[-1]
    chunks = row_chunks(half)
    weights = [
        pltpu.make_async_copy(src, dst, wsem.at[k])
        for k, (src, dst) in enumerate(((w_down, vdown), (w_in, vin), (w_proj, vproj), (w_qkv, vqkv)))
    ]

    def kept_index(step):
        return 2 * (segments - 1 - lax.div(step, 2)) + lax.rem(step, 2)

    def residuals(step):
        side = lax.rem(step, 2)
        pairs = ((r_q, qb), (r_kv, kvb), (r_s2, z2b), (r_gp, gpb), (r_s1, z1b))
        return [
            pltpu.make_async_copy(src.at[kept_index(step)], dst.at[side], rsem.at[side, k])
            for k, (src, dst) in enumerate(pairs)
        ]

    def seed_copy(step):
        return pltpu.make_async_copy(g0_ref.at[kept_index(step)], gp_in.at[step], gsem.at[step])

    for step in range(2):
        for copy in residuals(step):
            copy.start()
        if step == 0:
            for copy in weights:
                copy.start()

    @pl.when(s == last)
    def _():
        for step in range(steps):
            seed_copy(step).start()

    o_small[...] = jnp.zeros_like(o_small)
    barrier = pltpu.get_barrier_semaphore()
    pl.semaphore_signal(barrier, inc=1, device_id=(place.next, place.d), device_id_type=MESH)
    pl.semaphore_signal(barrier, inc=1, device_id=(s, place.other), device_id_type=MESH)
    pl.semaphore_wait(barrier, 2)

    def outgoing(step):
        pairs = (
            (dpj, o_dpj),
            (dbr, o_dbr),
            (dpre, o_dpre),
            (dfe, o_dfe),
        )
        return [
            pltpu.make_async_copy(src, dst.at[kept_index(step)], osem.at[k])
            for k, (src, dst) in enumerate(pairs)
        ]

    def outgoing_dx(step):
        side = lax.rem(step, 2)
        return pltpu.make_async_copy(dg.at[side], o_dx.at[kept_index(step)], osem.at[4 + side])

    def outgoing_memory(step):
        return pltpu.make_async_copy(mg.at[step % 2], o_mg.at[step % 2], gsem.at[step])

    def handoff(step, index):
        start, size = chunks[index]
        side = lax.rem(step, 2)
        span = pl.ds(start, size)
        return remote(
            dxb.at[side, span],
            gb.at[step, span],
            h_send.at[side, index],
            h_recv.at[step, index],
            (place.prev, place.d),
        )

    def carry_move(step):
        return remote(mgb.at[step], carb.at[step], m_send.at[step], m_recv.at[step], (last, place.d))

    def settle(step):
        @pl.when(s > 0)
        def _():
            for index in range(len(chunks)):
                handoff(step, index).wait_send()

        outgoing_dx(step).wait()

    def prologue(step):
        side = lax.rem(step, 2)
        segment = segments - 1 - lax.div(step, 2)
        for copy in residuals(step):
            copy.wait()
        for z_ref, r_ref in ((z2b, r2b), (z1b, r1b)):
            for block in row_blocks(0, half):
                z, scale = normalized(z_ref[side, block, :])
                z_ref[side, block, :] = z
                r_ref[side, block, :] = jnp.broadcast_to(scale, (BLOCK, 128))
        bias = key_bias(geometry, segment, lens_ref[side, :1, :1], (rows, 128), 0)
        for pair in range(PAIRS):
            lanes = pair_span(pair)
            keys = kvb[side, :, lanes]
            for (start, size), begin in zip(chunks, lane_starts(chunks)[0]):
                queries = scaled_queries(qb[side, pl.ds(start, size), lanes])
                tiles = [bias] * (2 * size // 128)
                if 2 * size % 128:
                    tiles.append(bias[:, : 2 * size % 128])
                scores = dot_nt(keys, queries) + jnp.concatenate(tiles, axis=1)
                exponent = jnp.exp(scores - jnp.max(scores, axis=0, keepdims=True))
                inverse = 1.0 / jnp.sum(exponent, axis=0, keepdims=True)
                probs[side, pair, :, begin : begin + 2 * size] = (exponent * inverse).astype(BF)
            for (start, size), begin in zip(chunks, lane_starts(chunks)[0]):
                mixed = dot_tn(
                    kvb[side, :, pair_span(pair, D)], probs[side, pair, :, begin : begin + 2 * size]
                )
                attb[side, pl.ds(start, size), lanes] = upright(mixed)

    def norm_back(g, z, scale, gain):
        scaled = g * gain
        mean_u = jnp.mean(scaled, axis=-1, keepdims=True)
        mean_uz = jnp.mean(scaled * z, axis=-1, keepdims=True)
        return (scaled - mean_u - z * mean_uz) * scale

    def folded_rows(value):
        return value[: BLOCK // 2] + value[BLOCK // 2 :]

    def main(step):
        side = lax.rem(step, 2)
        segment = segments - 1 - lax.div(step, 2)
        first = step == 0
        pl.when(step >= 2)(lambda: settle(step - 2))

        @pl.when(step >= 1)
        def _():
            for copy in outgoing(step - 1):
                copy.wait()

        @pl.when(s == last)
        def _():
            seed_copy(step).wait()
            length = lens_ref[side, :1, :1]
            for index, block in enumerate(row_blocks(0, half)):
                row = c * half + index * BLOCK + lax.broadcasted_iota(jnp.int32, (BLOCK, part), 0)
                position = row - 2 * slot + segment * tok
                valid = (row >= 2 * slot) & (position.astype(F32) < length)
                for section in range(sections):
                    work[block, section * part : (section + 1) * part] = jnp.where(
                        valid, gp_in[step, section, block, :].astype(F32), 0.0
                    )

            @pl.when((c == 0) & (step >= 2))
            def _():
                carry_move(step - 2).wait_recv()
                work[slot : 2 * slot, :] = carb[step - 2]

        sends = []
        for index, (start, size) in enumerate(chunks):
            span = pl.ds(start, size)

            @pl.when(s < last)
            def _():
                handoff(step, index).wait_recv()
                for block in row_blocks(start, size):
                    work[block, :] = gb[step, block, :].astype(F32)

            gain_sum = jnp.zeros((BLOCK // 2, D), F32)
            shift_sum = jnp.zeros((BLOCK // 2, D), F32)
            for block in row_blocks(start, size):
                g = work[block, :]
                z = z2b[side, block, :]
                back = norm_back(g, z, r2b[side, block, :1], gain_two[...])
                dsec[block, :] = back
                dfe[block, :] = back.astype(BF)
                gain_sum += folded_rows(g * z)
                shift_sum += folded_rows(g)
            o_small[2:3, :] += jnp.sum(gain_sum, axis=0, keepdims=True)
            o_small[3:4, :] += jnp.sum(shift_sum, axis=0, keepdims=True)
            if index == 0:
                pl.when(first)(weights[0].wait)
            for lanes in pieces(FF):
                slope = gpb[side, span, lanes].astype(F32)
                pre = (dot(dfe[span], vdown[:, lanes]) * slope).astype(BF)
                dpre[span, lanes] = pre
                row, column = divmod(lanes.start, D)
                o_small[4 + row : 5 + row, column : column + STEP] += jnp.sum(
                    pre.astype(F32), axis=0, keepdims=True
                )
            if index == 0:
                pl.when(first)(weights[1].wait)
            for lanes in pieces(D):
                work[span, lanes] = dsec[span, lanes] + dot(dpre[span], vin[:, lanes])
            gain_sum = jnp.zeros((BLOCK // 2, D), F32)
            shift_sum = jnp.zeros((BLOCK // 2, D), F32)
            for block in row_blocks(start, size):
                g = work[block, :]
                z = z1b[side, block, :]
                back = norm_back(g, z, r1b[side, block, :1], gain_one[...])
                work[block, :] = back
                dbr[block, :] = back.astype(BF)
                gain_sum += folded_rows(g * z)
                shift_sum += folded_rows(g)
            o_small[0:1, :] += jnp.sum(gain_sum, axis=0, keepdims=True)
            o_small[1:2, :] += jnp.sum(shift_sum, axis=0, keepdims=True)
            if index == 0:
                pl.when(first)(weights[2].wait)
            for lanes in pieces(D):
                da[span, lanes] = dot(dbr[span], vproj[:, lanes]).astype(BF)
            heads = lax.broadcasted_iota(jnp.int32, (16, D), 0)
            columns = lax.broadcasted_iota(jnp.int32, (16, D), 1)
            member = (columns >= heads * HEAD) & (columns < (heads + 1) * HEAD)
            chooser = jnp.where(member, 1.0, 0.0).astype(BF)
            weighed = da[span, :].astype(F32) * attb[side, span, :]
            coarse = weighed.astype(BF)
            fine = (weighed - coarse.astype(F32)).astype(BF)
            row_sums = dot_nt(chooser, coarse) + dot_nt(chooser, fine)
            wide = 2 * size
            lane0 = lane_starts(chunks)[0][index]

            def score_grads(pair):
                values = kvb[side, :, pair_span(pair, D)]
                dp_tmp[pair % 2, :, :wide] = dot_nt(values, stacked_pair(da[span, pair_span(pair)]))

            score_grads(0)
            for pair in range(PAIRS):
                if pair + 1 < PAIRS:
                    score_grads(pair + 1)
                totals = jnp.concatenate(
                    [row_sums[2 * pair : 2 * pair + 1], row_sums[2 * pair + 1 : 2 * pair + 2]], axis=1
                )
                for begin in range(0, wide, 128):
                    lanes = slice(begin, min(begin + 128, wide))
                    kept_lanes = slice(lane0 + begin, lane0 + lanes.stop)
                    for offset in range(0, rows, BLOCK):
                        block = pl.ds(offset, BLOCK)
                        shifted = dp_tmp[pair % 2, block, lanes] - totals[:, lanes]
                        ds_tmp[pair, block, lanes] = (
                            probs[side, pair, block, kept_lanes].astype(F32) * shifted
                        ).astype(BF)
                d_keys = dot(ds_tmp[pair, :, :wide], scaled_queries(qb[side, span, pair_span(pair)]))
                d_values = dot(
                    probs[side, pair, :, lane0 : lane0 + wide], stacked_pair(da[span, pair_span(pair)])
                )
                if index == 0:
                    dkv[pair, :, :WIDE] = d_keys
                    dkv[pair, :, WIDE:] = d_values
                else:
                    dkv[pair, :, :WIDE] += d_keys
                    dkv[pair, :, WIDE:] += d_values
                if index == len(chunks) - 1:
                    move = remote(
                        dkv.at[pair, theirs],
                        dkv_in.at[side, pair],
                        kv_send.at[pair],
                        kv_recv.at[step, pair],
                        (s, place.other),
                    )
                    move.start()
                    sends.append(move)
            for pair in range(PAIRS):
                both = dot_tn(kvb[side, :, pair_span(pair)], ds_tmp[pair, :, :wide])
                dpj[span, pair_span(pair)] = (upright(both) * HEAD**-0.5).astype(BF)
        pl.when(first)(weights[3].wait)
        for lanes in pieces(D):
            work[:, lanes] += dot(dpj[:, :D], vqkv[:D, lanes])
        for pair in range(PAIRS):
            sends[pair].wait_recv()
            for which in range(2):
                lanes = slice(which * WIDE, (which + 1) * WIDE)
                dpj[:, pair_span(pair, (which + 1) * D)] = (
                    dkv[pair, own, lanes] + dkv_in[side, pair, :, lanes]
                ).astype(BF)
        for index, (start, size) in enumerate(chunks):
            span = pl.ds(start, size)
            for lanes in pieces(D):
                dxb[side, span, lanes] = (
                    work[span, lanes] + dot(dpj[span, D:], vqkv[D:, lanes])
                ).astype(BF)
            pl.when(s > 0)(handoff(step, index).start)
            if index == 0:

                @pl.when((s == 0) & (c == 0))
                def _():
                    mgb[step] = dxb[side, :slot].astype(F32) + dxb[side, slot : 2 * slot].astype(F32)
                    pl.when(step < steps - 2)(carry_move(step).start)

        for section in range(sections):
            dg[side, section] = dxb[side, :, section * part : (section + 1) * part]
        for copy in outgoing(step):
            copy.start()
        outgoing_dx(step).start()
        for move in sends:
            move.wait_send()

        @pl.when(step < steps - 2)
        def _():
            for copy in residuals(step + 2):
                copy.start()

    def one_round(turn, state):
        even, odd = 2 * turn, 2 * turn + 1
        late = (s == last) & (turn == 0)
        prologue(even)
        pl.when(jnp.logical_not(late))(lambda: prologue(odd))
        main(even)
        pl.when(late)(lambda: prologue(odd))
        main(odd)
        return state

    lax.fori_loop(0, segments, one_round, 0)
    settle(steps - 2)
    settle(steps - 1)
    for copy in outgoing(steps - 1):
        copy.wait()

    @pl.when((s == 0) & (c == 0))
    def _():
        for step in range(steps - 2, steps):
            for section in range(sections):
                mg[step % 2, section] = mgb[step, :, section * part : (section + 1) * part]
            outgoing_memory(step).start()
        for step in range(steps - 2, steps):
            outgoing_memory(step).wait()
        for step in range(steps - 2):
            carry_move(step).wait_send()


def backward(sections, segments, geometry, collective, g0, lens, kept, weights):
    mem, slot, tok, rows = geometry
    half = rows // 2
    steps = 2 * segments

    def grad(width):
        return jax.ShapeDtypeStruct((steps, half, width), BF)

    outs = (
        grad(3 * D),
        grad(D),
        grad(FF),
        grad(D),
        jax.ShapeDtypeStruct(g0.shape, BF),
        jax.ShapeDtypeStruct((2, g0.shape[1], slot, g0.shape[3]), F32),
        jax.ShapeDtypeStruct((8, D), F32),
    )
    dma = pltpu.SemaphoreType.DMA
    return pl.pallas_call(
        functools.partial(backward_kernel, sections, segments, geometry),
        name="backward_layer",
        out_shape=outs,
        in_specs=[ANY, VMEM] + [ANY] * 5 + [ANY] * 4 + [VMEM] * 2,
        out_specs=(ANY,) * 6 + (VMEM,),
        scratch_shapes=[
            pltpu.VMEM((3 * D, D), BF),
            pltpu.VMEM((D, D), BF),
            pltpu.VMEM((FF, D), BF),
            pltpu.VMEM((D, FF), BF),
            pltpu.VMEM((steps, half, D), BF),
            pltpu.VMEM((2, half, D), BF),
            pltpu.VMEM((2, rows, 2 * D), BF),
            pltpu.VMEM((2, half, FF), BF),
            pltpu.VMEM((2, half, D), F32),
            pltpu.VMEM((2, half, D), F32),
            pltpu.VMEM((2, half, D), F32),
            pltpu.VMEM((2, half, 128), F32),
            pltpu.VMEM((2, half, 128), F32),
            pltpu.VMEM((2, PAIRS, rows, lane_starts(row_chunks(half))[1]), BF),
            pltpu.VMEM((half, D), F32),
            pltpu.VMEM((half, D), F32),
            pltpu.VMEM((half, D), BF),
            pltpu.VMEM((half, FF), BF),
            pltpu.VMEM((half, D), BF),
            pltpu.VMEM((half, D), BF),
            pltpu.VMEM((2, rows, 2 * row_chunks(half)[-1][1]), F32),
            pltpu.VMEM((PAIRS, rows, 2 * row_chunks(half)[-1][1]), BF),
            pltpu.VMEM((PAIRS, rows, 2 * WIDE), F32),
            pltpu.VMEM((2, PAIRS, half, 2 * WIDE), F32),
            pltpu.VMEM((half, 3 * D), BF),
            pltpu.VMEM((2, half, D), BF),
            pltpu.VMEM((steps, slot, D), F32),
            pltpu.VMEM((steps, slot, D), F32),
            pltpu.VMEM(g0.shape, BF),
            pltpu.VMEM((2,) + g0.shape[1:], BF),
            pltpu.VMEM((2, g0.shape[1], slot, g0.shape[3]), F32),
            dma((4,)),
            dma((2, 5)),
            dma((steps,)),
            dma((6,)),
            dma((PAIRS,)),
            dma((steps, PAIRS)),
            dma((2, 2)),
            dma((steps, 2)),
            dma((steps,)),
            dma((steps,)),
        ],
        compiler_params=pltpu.CompilerParams(
            collective_id=collective, has_side_effects=True, vmem_limit_bytes=VMEM_LIMIT
        ),
    )(g0, lens, *kept, *weights)


def reduce_order(line):
    order = []
    low, high = 0, line - 1
    while low <= high:
        order.append(high)
        if low != high:
            order.append(low)
        low, high = low + 1, high - 1
    return order


def arrival_orders(line):
    def moment(chip, dest):
        upward = (line - 1 - dest) + chip
        downward = dest + (line - 1 - chip)
        if dest == chip:
            return line
        return upward if dest > chip else downward

    return [
        sorted(range(line), key=functools.partial(moment, chip)) for chip in range(line)
    ]


def finish_kernel(sections, segments, line, *refs):
    refs = list(refs)

    def take(count):
        taken = refs[:count]
        del refs[:count]
        return taken

    hid, dx, mem_in = take(3)
    lefts_in, rights_in, small_in = (take(4), take(4), take(1)[0]) if line else ((), (), None)
    o_h, o_x, o_m = take(3)
    outs = take(5) if line else ()
    h_send, h_got, x_send, x_got, m_send, m_got = take(6)
    place = Place(sections)
    s, c, d = place.s, place.c, place.d
    last = sections - 1
    steps = 2 * segments
    half = hid.shape[2]
    z = lax.div(d, 2)
    greet_plane(place, sections)
    if line:
        parts, sibs, ins, accs = take(5), take(5), take(5), take(5)
        big0, big1, flat0, flat1, flat2, flat3, turned = take(7)
        load, c_send, c_got, z_send, z_right, z_left, fin = take(7)
        up, down = (s, d + 2), (s, d - 2)

        def greet(target):
            pl.semaphore_signal(
                pltpu.get_barrier_semaphore(), inc=1, device_id=target, device_id_type=MESH
            )

        pl.when(z < line - 1)(lambda: greet(up))
        pl.when(z > 0)(lambda: greet(down))
        ends = (z == 0) | (z == line - 1)
        plane_wait(sections, jnp.where(ends, 1, 2))
    else:
        plane_wait(sections, 0)

    def deliveries():
        for src, dst, origin, send, got in (
            (hid, o_h, last, h_send, h_got),
            (dx, o_x, 0, x_send, x_got),
        ):
            for step in range(steps):
                segment, item = divmod(step, 2)
                rows = pl.ds(pl.multiple_of(c * half, BLOCK), half)
                for section in range(sections):
                    here = (s == section) & (c == item)
                    far = functools.partial(remote,
                        src.at[step, section],
                        dst.at[segment, rows],
                        send.at[step, section],
                        got.at[segment, c],
                        (section, place.base + item),
                    )
                    near = functools.partial(pltpu.make_async_copy,
                        src.at[step, section], dst.at[segment, rows], got.at[segment, c]
                    )
                    yield s == origin, here, far, near
        for item in range(2):
            for section in range(sections):
                here = (s == section) & (c == item)
                far = functools.partial(remote,
                    mem_in.at[item, section],
                    o_m,
                    m_send.at[item, section],
                    m_got.at[0],
                    (section, place.base + item),
                )
                near = functools.partial(pltpu.make_async_copy, mem_in.at[item, section], o_m, m_got.at[0])
                yield (s == 0) & (c == 0), here, far, near

    for mine, here, far, near in deliveries():
        pl.when(mine & jnp.logical_not(here))(lambda far=far: far().start())
        pl.when(mine & here)(lambda near=near: near().start())

    if line:
        act_in, nb_in, x_in, att_in = lefts_in
        dfe_in, dpre_in, dpj_in, dbr_in = rights_in

        def fetch(src, dst, slot):
            width = src.shape[-1]
            return [
                pltpu.make_async_copy(
                    src.at[step], dst.at[pl.ds(step * half, half), :width], load.at[slot, step]
                )
                for step in range(steps)
            ]

        loads = {
            "att": fetch(att_in, flat2, 4),
            "dbr": fetch(dbr_in, flat3, 5),
            "x": fetch(x_in, flat0, 3),
            "dpj": fetch(dpj_in, big0, 2),
            "nb": fetch(nb_in, flat1, 0),
            "dpre": fetch(dpre_in, big1, 1),
            "act": fetch(act_in, big0, 2),
            "dfe": fetch(dfe_in, flat0, 3),
        }

        def begin(name):
            for copy in loads[name]:
                copy.start()

        def ready(name):
            for copy in loads[name]:
                copy.wait()

        for name in ("att", "dbr", "x", "dpj", "nb", "dpre"):
            begin(name)
        order = reduce_order(line)
        kinds = (4, 3, 2, 0, 1)
        flows = [(kind, dest) for kind in kinds for dest in order]
        depth = 2
        ends_first = (
            ([flow for flow in flows if flow[1] > 0], 1, 0),
            ([flow for flow in flows if flow[1] < line - 1], -1, line - 1),
        )

        def arrival(position):
            dest = 0
            for chip, row in enumerate(arrival_orders(line)):
                for index, value in enumerate(row):
                    dest += jnp.where((z == chip) & (position == index), value, 0)
            return dest

        def own_rows(kind):
            block = parts[kind].shape[1] // 2
            return pl.ds(pl.multiple_of(c * block, 8), block)

        def core_move(kind, dest):
            block = parts[kind].shape[1] // 2
            theirs = pl.ds(pl.multiple_of((1 - c) * block, 8), block)
            return remote(
                parts[kind].at[dest, theirs],
                sibs[kind].at[dest],
                c_send.at[kind, dest],
                c_got.at[kind, dest],
                (s, place.other),
            )

        def line_move(kind, dest, towards):
            if towards > 0:
                slot, target, got = dest, up, z_right
            else:
                slot, target, got = jnp.where(z - 1 == dest, line, dest), down, z_left
            return remote(
                parts[kind].at[dest, own_rows(kind)],
                ins[kind].at[slot],
                z_send.at[kind, dest],
                got.at[kind, dest],
                target,
            )

        def add(kind, dest, ref, slot):
            acc = accs[kind]
            rows = min(BLOCK, acc.shape[0])

            def block(index, state):
                span = pl.ds(pl.multiple_of(index * rows, rows), rows)
                acc[span, :] += ref[slot, span, :].astype(F32)
                return state

            lax.fori_loop(0, acc.shape[0] // rows, block, 0)

        def hop(kind, dest):
            acc = accs[kind]
            core_move(kind, dest).wait_recv()
            acc[...] = parts[kind][dest, own_rows(kind), :].astype(F32)
            add(kind, dest, sibs[kind], dest)

            @pl.when((z > 0) & (z <= dest))
            def _():
                line_move(kind, dest, 1).wait_recv()
                add(kind, dest, ins[kind], dest)

            @pl.when((z < line - 1) & (z >= dest))
            def _():
                line_move(kind, dest, -1).wait_recv()
                add(kind, dest, ins[kind], jnp.where(z == dest, line, dest))

            @pl.when(z != dest)
            def _():
                parts[kind][dest, own_rows(kind), :] = acc[...].astype(parts[kind].dtype)

            for sequence, towards, end in ends_first if isinstance(dest, int) else ():
                spot = sequence.index((kind, dest)) if (kind, dest) in sequence else 0
                if spot >= depth:
                    earlier = functools.partial(line_move, *sequence[spot - depth], towards)
                    pl.when(z == end)(lambda earlier=earlier: earlier().wait_send())
            pl.when(z < dest)(lambda: line_move(kind, dest, 1).start())
            pl.when(z > dest)(lambda: line_move(kind, dest, -1).start())

            @pl.when(z == dest)
            def _():
                copy = pltpu.make_async_copy(acc, outs[kind], fin.at[kind])
                copy.start()
                copy.wait()

        def no_wait(dest):
            return ((z == 0) & (dest > 0)) | ((z == line - 1) & (dest < line - 1))

        matrices = (
            ("nb", "dpre", flat1, big1, FF),
            ("act", "dfe", big0, flat0, D),
            ("x", "dpj", flat0, big0, 3 * D),
            ("att", "dbr", flat2, flat3, D),
        )
        size = D // (2 * line)
        long = FF // (2 * line)
        for dest in order:
            parts[4][dest] = jnp.zeros(parts[4].shape[1:], F32)
            for core in range(2):
                index = 2 * dest + core
                for row in range(4):
                    parts[4][dest, 8 * core + row : 8 * core + row + 1, :size] = small_in[
                        row : row + 1, index * size : (index + 1) * size
                    ]
                row, column = divmod(index * long, D)
                parts[4][dest, 8 * core + 4 : 8 * core + 5, :] = small_in[
                    4 + row : 5 + row, column : column + long
                ]
            core_move(4, dest).start()
        for spot, dest in enumerate(order[:-1]):
            pl.when(no_wait(dest))(functools.partial(hop, 4, dest))
        for kind in kinds[1:]:
            left_name, right_name, left, right, width = matrices[kind]
            if kind == 1:
                begin(left_name)
                begin(right_name)
            ready(left_name)
            ready(right_name)
            block = parts[kind].shape[1]
            for dest in order:
                turned[:block, :] = jnp.transpose(left[:, dest * block : (dest + 1) * block])
                for lanes in pieces(width):
                    parts[kind][dest, :, lanes] = dot(turned[:block, :], right[:, lanes]).astype(BF)
                core_move(kind, dest).start()
                place_in_flow = flows.index((kind, dest))
                if place_in_flow > 0:
                    before = flows[place_in_flow - 1]
                    pl.when(no_wait(before[1]))(functools.partial(hop, *before))
        pl.when(no_wait(flows[-1][1]))(functools.partial(hop, *flows[-1]))
        for kind in kinds:

            def by_arrival(position, state):
                dest = arrival(position)
                pl.when(jnp.logical_not(no_wait(dest)))(lambda: hop(kind, dest))
                return state

            lax.fori_loop(0, line, by_arrival, 0)
        for kind, dest in flows:
            core_move(kind, dest).wait_send()
            for sequence, towards, end in ends_first:
                if (kind, dest) in sequence:
                    pending = (z < dest) if towards > 0 else (z > dest)
                    if (kind, dest) not in sequence[-depth:]:
                        pending &= z != end
                    pl.when(pending)(lambda: line_move(kind, dest, towards).wait_send())

    for mine, here, far, near in deliveries():
        pl.when(mine & jnp.logical_not(here))(lambda far=far: far().wait_send())
    for src, dst, origin, got in ((hid, o_h, last, h_got), (dx, o_x, 0, x_got)):
        for segment in range(segments):
            for core in range(2):
                rows = pl.ds(core * half, half)
                here = (s == origin) & (c == core)
                far = functools.partial(remote,
                    src.at[0, 0], dst.at[segment, rows], h_send.at[0, 0], got.at[segment, core], (s, d)
                )
                near = functools.partial(pltpu.make_async_copy, src.at[0, 0], dst.at[segment, rows], got.at[segment, core])
                pl.when(jnp.logical_not(here))(lambda far=far: far().wait_recv())
                pl.when(here)(lambda near=near: near().wait())
    here = (s == 0) & (c == 0)
    far = functools.partial(remote, mem_in.at[0, 0], o_m, m_send.at[0, 0], m_got.at[0], (s, d))
    near = functools.partial(pltpu.make_async_copy, mem_in.at[0, 0], o_m, m_got.at[0])
    pl.when(jnp.logical_not(here))(lambda far=far: far().wait_recv())
    pl.when(here)(lambda near=near: near().wait())


def finish(sections, segments, line, collective, hid, dx, memory_term, sums):
    steps, _, half, part = hid.shape
    slot = memory_term.shape[2]
    dma = pltpu.SemaphoreType.DMA
    outs = [
        jax.ShapeDtypeStruct((segments, 2 * half, part), BF),
        jax.ShapeDtypeStruct((segments, 2 * half, part), BF),
        jax.ShapeDtypeStruct((slot, part), F32),
    ]
    scratch = [
        dma((steps, sections)),
        dma((segments, 2)),
        dma((steps, sections)),
        dma((segments, 2)),
        dma((2, sections)),
        dma((1,)),
    ]
    operands = [hid, dx, memory_term]
    if line:
        lefts, rights, small = sums
        operands += [*lefts, *rights, small]
        block = D // (2 * line)
        shapes = (
            (block, FF, BF),
            (FF // (2 * line), D, BF),
            (block, 3 * D, BF),
            (block, D, BF),
            (8, FF // (2 * line), F32),
        )
        outs += [jax.ShapeDtypeStruct(shape[:2], F32) for shape in shapes]
        total = steps * half
        scratch += [pltpu.VMEM((line, 2 * rows, width), kind) for rows, width, kind in shapes]
        scratch += [pltpu.VMEM((line, rows, width), kind) for rows, width, kind in shapes]
        scratch += [pltpu.VMEM((line + 1, rows, width), kind) for rows, width, kind in shapes]
        scratch += [pltpu.VMEM((rows, width), F32) for rows, width, kind in shapes]
        scratch += [pltpu.VMEM((total, FF), BF)] * 2 + [pltpu.VMEM((total, D), BF)] * 4
        scratch += [pltpu.VMEM((FF // line, total), BF)]
        scratch += [
            dma((6, steps)),
            dma((5, line)),
            dma((5, line)),
            dma((5, line)),
            dma((5, line)),
            dma((5, line)),
            dma((5,)),
        ]
    return pl.pallas_call(
        functools.partial(finish_kernel, sections, segments, line),
        name="finish",
        out_shape=tuple(outs),
        in_specs=[ANY] * (len(operands) - bool(line)) + [VMEM] * bool(line),
        out_specs=(ANY,) * len(outs),
        scratch_shapes=scratch,
        compiler_params=pltpu.CompilerParams(
            collective_id=collective, has_side_effects=True, vmem_limit_bytes=VMEM_LIMIT
        ),
    )(*operands)


def on_device(
    sections,
    inputs,
    out_grad,
    memory,
    lengths,
    w_qkv,
    w_proj,
    gain_one,
    shift_one,
    w_in,
    b_in,
    w_down,
    gain_two,
    shift_two,
):
    segs, tok, part = inputs.shape[1:]
    mem = memory.shape[1]
    slot = -(-mem // BLOCK) * BLOCK
    rows = -(-(2 * slot + tok) // (2 * BLOCK)) * 2 * BLOCK
    half = rows // 2
    geometry = (mem, slot, tok, rows)
    back_pad = rows - 2 * slot - tok

    head = jnp.pad(memory[:1], ((0, segs - 1), (0, slot - mem), (0, 0)))
    blank = jnp.zeros((segs, back_pad, part), BF)
    tokens = jnp.concatenate([head, head, inputs[0], blank], axis=1)
    cotangent = jnp.pad(out_grad[0], ((0, 0), (2 * slot, back_pad), (0, 0)))
    length_tile = jnp.broadcast_to(lengths.astype(F32), (8, 128))

    def halves(array):
        return array.reshape(segs, 2, half, part)

    matrices = (w_qkv[0], w_proj[0], w_in[0], w_down[0])
    forward_weights = matrices + (gain_one, shift_one, b_in, gain_two, shift_two)
    x, q, kv, att, nb, act, gp, s1, s2, hid, *turned, g0, lens = forward(
        sections, segs, geometry, 0, halves(tokens), halves(cotangent), length_tile, forward_weights
    )
    dpj, dbr, dpre, dfe, dx, memory_term, small = backward(
        sections, segs, geometry, 1, g0, lens, (q, kv, gp, s1, s2), (*turned, gain_one, gain_two)
    )
    devices = lax.axis_size("dp")
    lefts, rights = (act, nb, x, att), (dfe, dpre, dpj, dbr)
    line = devices // 2 if D % (devices * BLOCK) == 0 and FF % (devices * 128) == 0 and devices > 2 else 0
    sums = None
    if line:
        sums = (lefts, rights, small)
    out_parts, in_parts, memory_part, *reduced = finish(
        sections, segs, line, 2, hid, dx, memory_term, sums
    )

    def owned(parts):
        return parts[:, 2 * slot : 2 * slot + tok]

    position = jnp.arange(segs * tok, dtype=jnp.int32).reshape(segs, tok)
    token_valid = position < lengths[0]
    outputs = jnp.where(token_valid[:, :, None], owned(out_parts), jnp.zeros((), BF))
    input_grad = owned(in_parts)
    memory_grad = memory_part[:mem]

    if line:
        d_in, d_down, d_qkv, d_proj, share = reduced
        size = D // devices
        vectors = [share[k : k + 1, :size] for k in range(4)] + [share[4:5]]
    else:

        def weight_grad(left, right):
            full = jnp.einsum(
                "rd,re->de",
                left.reshape(2 * segs * half, -1),
                right.reshape(2 * segs * half, -1),
                preferred_element_type=F32,
            )
            return lax.psum_scatter(full.astype(BF), "dp", scatter_dimension=0, tiled=True).astype(F32)

        d_down, d_in, d_qkv, d_proj = [weight_grad(*pair) for pair in zip(lefts, rights)]
        vectors = [
            lax.psum_scatter(rows.reshape(1, -1), "dp", scatter_dimension=1, tiled=True)
            for rows in (small[0], small[1], small[2], small[3], small[4:8])
        ]
    gain_one_share, shift_one_share, gain_two_share, shift_two_share, b_in_share = vectors

    return (
        outputs[None],
        input_grad[None],
        memory_grad[None],
        d_qkv[None],
        d_proj[None],
        gain_one_share,
        shift_one_share,
        d_in[None],
        b_in_share,
        d_down[None],
        gain_two_share,
        shift_two_share,
    )


def solution(mesh):
    return jax.shard_map(
        functools.partial(on_device, mesh.shape["section"]),
        mesh=mesh,
        in_specs=(
            P("dp", None, None, "section"),
            P("dp", None, None, "section"),
            P("dp", None, "section"),
            P("dp"),
            P("section", None, None),
            P("section", None, None),
            P("section", None),
            P("section", None),
            P("section", None, None),
            P("section", None),
            P("section", None, None),
            P("section", None),
            P("section", None),
        ),
        out_specs=(
            P("dp", None, None, "section"),
            P("dp", None, None, "section"),
            P("dp", None, "section"),
            P("section", "dp", None),
            P("section", "dp", None),
            P("section", "dp"),
            P("section", "dp"),
            P("section", "dp", None),
            P("section", "dp"),
            P("section", "dp", None),
            P("section", "dp"),
            P("section", "dp"),
        ),
        check_vma=False,
    )
```

```python
import functools

import jax
import jax.numpy as jnp
from jax import lax
from jax.experimental import pallas as pl
from jax.experimental.pallas import tpu as pltpu
from jax.sharding import PartitionSpec as P

D = 768
H = 12
HEAD = 64
FF = 3072
PAIRS = H // 2
WIDE = 2 * HEAD
STEP = 256
BLOCK = 16
BF = jnp.bfloat16
F32 = jnp.float32
MESH = pl.DeviceIdType.MESH
ANY = pl.BlockSpec(memory_space=pl.ANY)
VMEM = pl.BlockSpec(memory_space=pltpu.VMEM)
VMEM_LIMIT = 63 * 1024 * 1024


def dot(a, b):
    return jnp.dot(a, b, preferred_element_type=F32)


def dot_nt(a, b):
    return lax.dot_general(a, b, (((1,), (1,)), ((), ())), preferred_element_type=F32)


def dot_tn(a, b):
    return lax.dot_general(a, b, (((0,), (0,)), ((), ())), preferred_element_type=F32)


def cols(index):
    return pl.ds(index * STEP, STEP)


def remote(src, dst, send, recv, target):
    return pltpu.make_async_remote_copy(
        src_ref=src, dst_ref=dst, send_sem=send, recv_sem=recv, device_id=target, device_id_type=MESH
    )


class Place:
    def __init__(self, sections):
        self.s = lax.axis_index("section")
        self.d = lax.axis_index("dp")
        self.c = lax.rem(self.d, 2)
        self.base = self.d - self.c
        self.other = self.base + 1 - self.c
        self.next = lax.rem(self.s + 1, sections)
        self.prev = lax.rem(self.s + sections - 1, sections)


def greet_plane(place, sections):
    barrier = pltpu.get_barrier_semaphore()
    for section in range(sections):
        for core in range(2):

            @pl.when((place.s != section) | (place.c != core))
            def _():
                pl.semaphore_signal(
                    barrier, inc=1, device_id=(section, place.base + core), device_id_type=MESH
                )


def plane_wait(sections, extra):
    pl.semaphore_wait(pltpu.get_barrier_semaphore(), 2 * sections - 1 + extra)


def key_bias(geometry, segment, length, shape, dim):
    mem, slot, tok, rows = geometry
    row = lax.broadcasted_iota(jnp.int32, shape, dim)
    position = row - 2 * slot + segment * tok
    is_token = (row >= 2 * slot) & (row < 2 * slot + tok) & (position.astype(F32) < length)
    is_memory = (row < mem) | ((row >= slot) & (row < slot + mem))
    return jnp.where(is_token | is_memory, 0.0, -1e30)


def stacked_pair(pair):
    lane = lax.broadcasted_iota(jnp.int32, pair.shape, 1)
    zero = jnp.zeros_like(pair)
    return jnp.concatenate(
        [jnp.where(lane < HEAD, pair, zero), jnp.where(lane >= HEAD, pair, zero)], axis=0
    )


def folded_pair(both):
    half = both.shape[0] // 2
    lane = lax.broadcasted_iota(jnp.int32, (half, WIDE), 1)
    return jnp.where(lane < HEAD, both[:half], both[half:])


def upright(both):
    size = both.shape[1] // 2
    row = lax.broadcasted_iota(jnp.int32, (WIDE, size), 0)
    return jnp.transpose(jnp.where(row < HEAD, both[:, :size], both[:, size:]))


def scaled_queries(queries):
    return stacked_pair(queries * jnp.asarray(HEAD**-0.5, BF))


def normalized(rows):
    center = rows - jnp.mean(rows, axis=-1, keepdims=True)
    spread_of = jnp.mean(center * center, axis=-1, keepdims=True)
    scale = lax.rsqrt(spread_of + 1e-06)
    return center * scale, scale


def pieces(width, step=STEP):
    return [slice(start, start + step) for start in range(0, width, step)]


def row_chunks(half):
    first = half // 2 // BLOCK * BLOCK
    return ((0, first), (first, half - first))


def lane_starts(chunks):
    starts, total = [], 0
    for _, size in chunks:
        starts.append(total)
        total += -(-2 * size // 128) * 128
    return starts, total


def row_blocks(start, size):
    return [pl.ds(start + offset, BLOCK) for offset in range(0, size, BLOCK)]


def pair_span(pair, offset=0):
    return slice(offset + pair * WIDE, offset + (pair + 1) * WIDE)


def forward_kernel(
    sections,
    segments,
    geometry,
    a_ref,
    g_ref,
    len_ref,
    w_qkv,
    w_proj,
    w_in,
    w_down,
    gain_one,
    shift_one,
    b_in,
    gain_two,
    shift_two,
    o_x,
    o_q,
    o_kv,
    o_att,
    o_nb,
    o_act,
    o_gp,
    o_s1,
    o_s2,
    o_hid,
    t_qkv,
    t_proj,
    t_in,
    t_down,
    o_g,
    o_lens,
    vqkv,
    vproj,
    vin,
    vdown,
    xb,
    kvb,
    qb,
    attb,
    nbb,
    actb,
    gpb,
    s1b,
    s2b,
    hb,
    preb,
    nf,
    memb,
    s_tmp,
    probs,
    turned,
    xp,
    hg,
    lens_ref,
    wsem,
    osem,
    kv_send,
    kv_recv,
    h_send,
    h_recv,
    m_send,
    m_recv,
    tsem,
    a_send,
    a_got,
    g_send,
    g_got,
    l_send,
    l_got,
):
    place = Place(sections)
    s, c = place.s, place.c
    mem, slot, tok, rows = geometry
    half = rows // 2
    last = sections - 1
    steps = 2 * segments
    chunks = row_chunks(half)
    early = s >= 2
    weights = [
        pltpu.make_async_copy(src, dst, wsem.at[k])
        for k, (src, dst) in enumerate(((w_qkv, vqkv), (w_proj, vproj), (w_in, vin), (w_down, vdown)))
    ]

    part = a_ref.shape[-1]
    greet_plane(place, sections)
    plane_wait(sections, 0)

    def spread(src, dst, target, send, got, segment):
        step = 2 * segment + c
        for core in range(2):
            here = (s == target) & (c == core)
            far = functools.partial(remote,
                src.at[segment, core],
                dst.at[step, s],
                send.at[segment, core],
                got.at[step, s],
                (target, place.base + core),
            )
            near = functools.partial(pltpu.make_async_copy, src.at[segment, core], dst.at[step, s], got.at[step, s])
            yield here, far, near

    def tokens(segment):
        return spread(a_ref, xp, 0, a_send, a_got, segment)

    def cotangents(segment):
        return spread(g_ref, o_g, last, g_send, g_got, segment)

    def begin(moves):
        for here, far, near in moves:
            pl.when(jnp.logical_not(here))(lambda far=far: far().start())
            pl.when(here)(lambda near=near: near().start())

    def sent(moves):
        for here, far, _ in moves:
            pl.when(jnp.logical_not(here))(lambda far=far: far().wait_send())

    def arrived(src, dst, got, target, step, section):
        side = lax.rem(step, 2)
        here = (section == target) & (side == c)
        far = functools.partial(remote,
            src.at[0, 0], dst.at[step, section], a_send.at[0, 0], got.at[step, section], (s, place.d)
        )
        near = functools.partial(pltpu.make_async_copy, src.at[0, 0], dst.at[step, section], got.at[step, section])
        pl.when(jnp.logical_not(here))(lambda far=far: far().wait_recv())
        pl.when(here)(lambda near=near: near().wait())

    begin(tokens(0))
    length_move = remote(len_ref, lens_ref.at[c], l_send.at[0], l_got.at[0], (s, place.other))
    length_move.start()
    lens_ref[c] = len_ref[...]
    for copy in weights:
        copy.start()
    sent(tokens(0))
    for segment in range(1, segments):
        begin(tokens(segment))
    for segment in range(segments):
        begin(cotangents(segment))
    remote(len_ref, lens_ref.at[1 - c], l_send.at[0], l_got.at[0], (s, place.other)).wait_recv()

    def outgoing(step):
        side = lax.rem(step, 2)
        pairs = (
            (xb.at[step], o_x),
            (kvb.at[step], o_kv),
            (qb.at[side], o_q),
            (attb.at[side], o_att),
            (nbb.at[side], o_nb),
            (actb.at[side], o_act),
            (gpb.at[side], o_gp),
            (s1b.at[side], o_s1),
            (s2b.at[side], o_s2),
            (hg.at[side], o_hid),
        )
        return [
            pltpu.make_async_copy(src, dst.at[step], osem.at[side, k])
            for k, (src, dst) in enumerate(pairs)
        ]

    def handoff(step, index):
        start, size = chunks[index]
        side = lax.rem(step, 2)
        span = pl.ds(start, size)
        return remote(
            hb.at[side, span],
            xb.at[step, span],
            h_send.at[side, index],
            h_recv.at[step, index],
            (place.next, place.d),
        )

    def memory_move(step):
        side = lax.rem(step, 2)
        return remote(
            hb.at[side, pl.ds(slot, slot)], memb.at[step], m_send.at[side], m_recv.at[step], (0, place.d)
        )

    def exchange(step, index):
        start, size = chunks[index]
        span = pl.ds(pl.multiple_of(c * half + start, BLOCK), size)
        return remote(
            kvb.at[step, span],
            kvb.at[step, span],
            kv_send.at[index],
            kv_recv.at[step, index],
            (s, place.other),
        )

    def settle(step):
        @pl.when(s < last)
        def _():
            for index in range(len(chunks)):
                handoff(step, index).wait_send()

        @pl.when((s == last) & (c == 0) & (step < steps - 2))
        def _():
            memory_move(step).wait_send()

        for copy in outgoing(step):
            copy.wait()

    def turn_weights():
        @pl.when(early)
        def _():
            for copy in weights:
                copy.wait()

        blocks = []
        for src, dst in ((vqkv, t_qkv), (vproj, t_proj), (vin, t_in), (vdown, t_down)):
            for block in range(src.shape[0] * src.shape[1] // (D * D)):
                span = pl.ds(block * D, D)
                if src.shape[0] == D:
                    blocks.append((src, (slice(None), span), dst.at[span]))
                else:
                    blocks.append((src, (span, slice(None)), dst.at[:, span]))
        moves = []
        for index, (src, where, dst) in enumerate(blocks):
            spot = index % 3
            if index >= 3:
                moves[index - 3].wait()
            turned[spot] = jnp.transpose(src[where])
            moves.append(pltpu.make_async_copy(turned.at[spot], dst, tsem.at[spot]))
            moves[-1].start()
        for move in moves[-3:]:
            move.wait()

    def one_step(step, state):
        pl.when(step == jnp.where(early, 0, steps))(turn_weights)
        pl.when(step < steps)(lambda: compute_step(step))
        return state

    def compute_step(step):
        side = lax.rem(step, 2)
        segment = lax.div(step, 2)
        first = (step == 0) & jnp.logical_not(early)

        @pl.when(s == 0)
        def _():
            for section in range(sections):
                arrived(a_ref, xp, a_got, 0, step, section)
                xb[step, :, section * part : (section + 1) * part] = xp[step, section]

            @pl.when((c == 0) & (step >= 2))
            def _():
                memory_move(step - 2).wait_recv()
                xb[step, :slot] = memb[step - 2]
                xb[step, slot : 2 * slot] = memb[step - 2]

        pl.when(step >= 2)(lambda: settle(step - 2))
        for index, (start, size) in enumerate(chunks):
            span = pl.ds(start, size)

            @pl.when(s > 0)
            def _():
                handoff(step, index).wait_recv()

            if index == 0:
                pl.when(first)(weights[0].wait)
            own = pl.ds(pl.multiple_of(c * half + start, BLOCK), size)
            for lanes in pieces(2 * D):
                kvb[step, own, lanes] = dot(
                    xb[step, span], vqkv[:, D + lanes.start : D + lanes.stop]
                ).astype(BF)
            exchange(step, index).start()
            for lanes in pieces(D):
                qb[side, span, lanes] = dot(xb[step, span], vqkv[:, lanes]).astype(BF)
        bias = key_bias(geometry, segment, lens_ref[side, :1, :1], (1, rows), 1)
        for index in range(len(chunks)):
            exchange(step, index).wait_recv()
        for index, (start, size) in enumerate(chunks):
            span = pl.ds(start, size)

            def score(pair):
                lanes = pair_span(pair)
                s_tmp[pair % 2, : 2 * size] = dot_nt(
                    scaled_queries(qb[side, span, lanes]), kvb[step, :, lanes]
                )

            score(0)
            for pair in range(PAIRS):
                if pair + 1 < PAIRS:
                    score(pair + 1)
                for offset in range(0, 2 * size, 2 * BLOCK):
                    block = pl.ds(offset, 2 * BLOCK)
                    scores = s_tmp[pair % 2, block, :] + bias
                    exponent = jnp.exp(scores - jnp.max(scores, axis=-1, keepdims=True))
                    inverse = 1.0 / jnp.sum(exponent, axis=-1, keepdims=True)
                    probs[pair, block, :] = (exponent * inverse).astype(BF)
            for pair in range(PAIRS):
                mixed = dot(probs[pair, : 2 * size], kvb[step, :, pair_span(pair, D)])
                attb[side, span, pair_span(pair)] = folded_pair(mixed).astype(BF)
            if index == 0:
                pl.when(first)(weights[1].wait)
            for lanes in pieces(D):
                s1b[side, span, lanes] = xb[step, span, lanes].astype(F32) + dot(
                    attb[side, span], vproj[:, lanes]
                )
            for block in row_blocks(start, size):
                z, _ = normalized(s1b[side, block, :])
                normed = z * gain_one[...] + shift_one[...]
                nf[block, :] = normed
                nbb[side, block, :] = normed.astype(BF)
            if index == 0:
                pl.when(first)(weights[2].wait)
            for lanes in pieces(FF):
                pre = dot(nbb[side, span], vin[:, lanes]) + b_in[:, lanes]
                preb[span, lanes] = pre
                actb[side, span, lanes] = (
                    0.5 * pre * (1.0 + lax.erf(pre * 0.7071067811865476))
                ).astype(BF)
            if index == 0:
                pl.when(first)(weights[3].wait)
            for lanes in pieces(D):
                s2b[side, span, lanes] = nf[span, lanes] + dot(actb[side, span], vdown[:, lanes])
            for block in row_blocks(start, size):
                z, _ = normalized(s2b[side, block, :])
                hb[side, block, :] = (z * gain_two[...] + shift_two[...]).astype(BF)

            pl.when(s < last)(handoff(step, index).start)
            if index == 0:

                @pl.when((s == last) & (c == 0) & (step < steps - 2))
                def _():
                    memory_move(step).start()

        for block in row_blocks(0, half):
            pre = preb[block, :]
            density = jnp.exp(-0.5 * pre * pre) * 0.3989422804014327
            slope = 0.5 * (1.0 + lax.erf(pre * 0.7071067811865476)) + pre * density
            gpb[side, block, :] = slope.astype(BF)
        for section in range(sections):
            hg[side, section] = hb[side, :, section * part : (section + 1) * part]
        for copy in outgoing(step):
            copy.start()
        for index in range(len(chunks)):
            exchange(step, index).wait_send()

    lax.fori_loop(0, steps + 1, one_step, 0)
    settle(steps - 2)
    settle(steps - 1)
    o_lens[...] = lens_ref[...]
    length_move.wait_send()
    for segment in range(segments):
        if segment > 0:
            sent(tokens(segment))
        sent(cotangents(segment))

    @pl.when(s == last)
    def _():
        for step in range(steps):
            for section in range(sections):
                arrived(g_ref, o_g, g_got, last, step, section)


def forward(sections, segments, geometry, collective, a, g, length_tile, weights):
    mem, slot, tok, rows = geometry
    half = rows // 2
    steps = 2 * segments
    grouped = (steps, sections, half, a.shape[-1])

    def kept(width, kind, height=half):
        return jax.ShapeDtypeStruct((steps, height, width), kind)

    outs = (
        kept(D, BF),
        kept(D, BF),
        kept(2 * D, BF, rows),
        kept(D, BF),
        kept(D, BF),
        kept(FF, BF),
        kept(FF, BF),
        kept(D, F32),
        kept(D, F32),
        jax.ShapeDtypeStruct(grouped, BF),
        jax.ShapeDtypeStruct((3 * D, D), BF),
        jax.ShapeDtypeStruct((D, D), BF),
        jax.ShapeDtypeStruct((FF, D), BF),
        jax.ShapeDtypeStruct((D, FF), BF),
        jax.ShapeDtypeStruct(grouped, BF),
        jax.ShapeDtypeStruct((2, 8, 128), F32),
    )
    dma = pltpu.SemaphoreType.DMA
    return pl.pallas_call(
        functools.partial(forward_kernel, sections, segments, geometry),
        name="forward_layer",
        out_shape=outs,
        in_specs=[ANY, ANY, VMEM] + [ANY] * 4 + [VMEM] * 5,
        out_specs=(ANY,) * (len(outs) - 1) + (VMEM,),
        scratch_shapes=[
            pltpu.VMEM((D, 3 * D), BF),
            pltpu.VMEM((D, D), BF),
            pltpu.VMEM((D, FF), BF),
            pltpu.VMEM((FF, D), BF),
            pltpu.VMEM((steps, half, D), BF),
            pltpu.VMEM((steps, rows, 2 * D), BF),
            pltpu.VMEM((2, half, D), BF),
            pltpu.VMEM((2, half, D), BF),
            pltpu.VMEM((2, half, D), BF),
            pltpu.VMEM((2, half, FF), BF),
            pltpu.VMEM((2, half, FF), BF),
            pltpu.VMEM((2, half, D), F32),
            pltpu.VMEM((2, half, D), F32),
            pltpu.VMEM((2, half, D), BF),
            pltpu.VMEM((half, FF), F32),
            pltpu.VMEM((half, D), F32),
            pltpu.VMEM((steps, slot, D), BF),
            pltpu.VMEM((2, 2 * row_chunks(half)[-1][1], rows), F32),
            pltpu.VMEM((PAIRS, 2 * row_chunks(half)[-1][1], rows), BF),
            pltpu.VMEM((3, D, D), BF),
            pltpu.VMEM(grouped, BF),
            pltpu.VMEM((2,) + grouped[1:], BF),
            pltpu.VMEM((2, 8, 128), F32),
            dma((4,)),
            dma((2, 10)),
            dma((2,)),
            dma((steps, 2)),
            dma((2, 2)),
            dma((steps, 2)),
            dma((2,)),
            dma((steps,)),
            dma((3,)),
            dma((segments, 2)),
            dma((steps, sections)),
            dma((segments, 2)),
            dma((steps, sections)),
            dma((1,)),
            dma((1,)),
        ],
        compiler_params=pltpu.CompilerParams(
            collective_id=collective, has_side_effects=True, vmem_limit_bytes=VMEM_LIMIT
        ),
    )(a, g, length_tile, *weights)


def backward_kernel(
    sections,
    segments,
    geometry,
    g0_ref,
    lens_ref,
    r_q,
    r_kv,
    r_gp,
    r_s1,
    r_s2,
    w_qkv,
    w_proj,
    w_in,
    w_down,
    gain_one,
    gain_two,
    o_dpj,
    o_dbr,
    o_dpre,
    o_dfe,
    o_dx,
    o_mg,
    o_small,
    vqkv,
    vproj,
    vin,
    vdown,
    gb,
    qb,
    kvb,
    gpb,
    z1b,
    z2b,
    attb,
    r1b,
    r2b,
    probs,
    work,
    dsec,
    dfe,
    dpre,
    dbr,
    da,
    dp_tmp,
    ds_tmp,
    dkv,
    dkv_in,
    dpj,
    dxb,
    mgb,
    carb,
    gp_in,
    dg,
    mg,
    wsem,
    rsem,
    gsem,
    osem,
    kv_send,
    kv_recv,
    h_send,
    h_recv,
    m_send,
    m_recv,
):
    place = Place(sections)
    s, c = place.s, place.c
    mem, slot, tok, rows = geometry
    half = rows // 2
    own = pl.ds(pl.multiple_of(c * half, BLOCK), half)
    theirs = pl.ds(pl.multiple_of((1 - c) * half, BLOCK), half)
    last = sections - 1
    steps = 2 * segments
    part = g0_ref.shape[-1]
    chunks = row_chunks(half)
    weights = [
        pltpu.make_async_copy(src, dst, wsem.at[k])
        for k, (src, dst) in enumerate(((w_down, vdown), (w_in, vin), (w_proj, vproj), (w_qkv, vqkv)))
    ]

    def kept_index(step):
        return 2 * (segments - 1 - lax.div(step, 2)) + lax.rem(step, 2)

    def residuals(step):
        side = lax.rem(step, 2)
        pairs = ((r_q, qb), (r_kv, kvb), (r_s2, z2b), (r_gp, gpb), (r_s1, z1b))
        return [
            pltpu.make_async_copy(src.at[kept_index(step)], dst.at[side], rsem.at[side, k])
            for k, (src, dst) in enumerate(pairs)
        ]

    def seed_copy(step):
        return pltpu.make_async_copy(g0_ref.at[kept_index(step)], gp_in.at[step], gsem.at[step])

    for step in range(2):
        for copy in residuals(step):
            copy.start()
        if step == 0:
            for copy in weights:
                copy.start()

    @pl.when(s == last)
    def _():
        for step in range(steps):
            seed_copy(step).start()

    o_small[...] = jnp.zeros_like(o_small)
    barrier = pltpu.get_barrier_semaphore()
    pl.semaphore_signal(barrier, inc=1, device_id=(place.next, place.d), device_id_type=MESH)
    pl.semaphore_signal(barrier, inc=1, device_id=(s, place.other), device_id_type=MESH)
    pl.semaphore_wait(barrier, 2)

    def outgoing(step):
        pairs = (
            (dpj, o_dpj),
            (dbr, o_dbr),
            (dpre, o_dpre),
            (dfe, o_dfe),
        )
        return [
            pltpu.make_async_copy(src, dst.at[kept_index(step)], osem.at[k])
            for k, (src, dst) in enumerate(pairs)
        ]

    def outgoing_dx(step):
        side = lax.rem(step, 2)
        return pltpu.make_async_copy(dg.at[side], o_dx.at[kept_index(step)], osem.at[4 + side])

    def outgoing_memory(step):
        return pltpu.make_async_copy(mg.at[step % 2], o_mg.at[step % 2], gsem.at[step])

    def handoff(step, index):
        start, size = chunks[index]
        side = lax.rem(step, 2)
        span = pl.ds(start, size)
        return remote(
            dxb.at[side, span],
            gb.at[step, span],
            h_send.at[side, index],
            h_recv.at[step, index],
            (place.prev, place.d),
        )

    def carry_move(step):
        return remote(mgb.at[step], carb.at[step], m_send.at[step], m_recv.at[step], (last, place.d))

    def settle(step):
        @pl.when(s > 0)
        def _():
            for index in range(len(chunks)):
                handoff(step, index).wait_send()

        outgoing_dx(step).wait()

    def prologue(step):
        side = lax.rem(step, 2)
        segment = segments - 1 - lax.div(step, 2)
        for copy in residuals(step):
            copy.wait()
        for z_ref, r_ref in ((z2b, r2b), (z1b, r1b)):
            for block in row_blocks(0, half):
                z, scale = normalized(z_ref[side, block, :])
                z_ref[side, block, :] = z
                r_ref[side, block, :] = jnp.broadcast_to(scale, (BLOCK, 128))
        bias = key_bias(geometry, segment, lens_ref[side, :1, :1], (rows, 128), 0)
        for pair in range(PAIRS):
            lanes = pair_span(pair)
            keys = kvb[side, :, lanes]
            for (start, size), begin in zip(chunks, lane_starts(chunks)[0]):
                queries = scaled_queries(qb[side, pl.ds(start, size), lanes])
                tiles = [bias] * (2 * size // 128)
                if 2 * size % 128:
                    tiles.append(bias[:, : 2 * size % 128])
                scores = dot_nt(keys, queries) + jnp.concatenate(tiles, axis=1)
                exponent = jnp.exp(scores - jnp.max(scores, axis=0, keepdims=True))
                inverse = 1.0 / jnp.sum(exponent, axis=0, keepdims=True)
                probs[side, pair, :, begin : begin + 2 * size] = (exponent * inverse).astype(BF)
            for (start, size), begin in zip(chunks, lane_starts(chunks)[0]):
                mixed = dot_tn(
                    kvb[side, :, pair_span(pair, D)], probs[side, pair, :, begin : begin + 2 * size]
                )
                attb[side, pl.ds(start, size), lanes] = upright(mixed)

    def norm_back(g, z, scale, gain):
        scaled = g * gain
        mean_u = jnp.mean(scaled, axis=-1, keepdims=True)
        mean_uz = jnp.mean(scaled * z, axis=-1, keepdims=True)
        return (scaled - mean_u - z * mean_uz) * scale

    def folded_rows(value):
        return value[: BLOCK // 2] + value[BLOCK // 2 :]

    def main(step):
        side = lax.rem(step, 2)
        segment = segments - 1 - lax.div(step, 2)
        first = step == 0
        pl.when(step >= 2)(lambda: settle(step - 2))

        @pl.when(step >= 1)
        def _():
            for copy in outgoing(step - 1):
                copy.wait()

        @pl.when(s == last)
        def _():
            seed_copy(step).wait()
            length = lens_ref[side, :1, :1]
            for index, block in enumerate(row_blocks(0, half)):
                row = c * half + index * BLOCK + lax.broadcasted_iota(jnp.int32, (BLOCK, part), 0)
                position = row - 2 * slot + segment * tok
                valid = (row >= 2 * slot) & (position.astype(F32) < length)
                for section in range(sections):
                    work[block, section * part : (section + 1) * part] = jnp.where(
                        valid, gp_in[step, section, block, :].astype(F32), 0.0
                    )

            @pl.when((c == 0) & (step >= 2))
            def _():
                carry_move(step - 2).wait_recv()
                work[slot : 2 * slot, :] = carb[step - 2]

        sends = []
        for index, (start, size) in enumerate(chunks):
            span = pl.ds(start, size)

            @pl.when(s < last)
            def _():
                handoff(step, index).wait_recv()
                for block in row_blocks(start, size):
                    work[block, :] = gb[step, block, :].astype(F32)

            gain_sum = jnp.zeros((BLOCK // 2, D), F32)
            shift_sum = jnp.zeros((BLOCK // 2, D), F32)
            for block in row_blocks(start, size):
                g = work[block, :]
                z = z2b[side, block, :]
                back = norm_back(g, z, r2b[side, block, :1], gain_two[...])
                dsec[block, :] = back
                dfe[block, :] = back.astype(BF)
                gain_sum += folded_rows(g * z)
                shift_sum += folded_rows(g)
            o_small[2:3, :] += jnp.sum(gain_sum, axis=0, keepdims=True)
            o_small[3:4, :] += jnp.sum(shift_sum, axis=0, keepdims=True)
            if index == 0:
                pl.when(first)(weights[0].wait)
            for lanes in pieces(FF):
                slope = gpb[side, span, lanes].astype(F32)
                pre = (dot(dfe[span], vdown[:, lanes]) * slope).astype(BF)
                dpre[span, lanes] = pre
                row, column = divmod(lanes.start, D)
                o_small[4 + row : 5 + row, column : column + STEP] += jnp.sum(
                    pre.astype(F32), axis=0, keepdims=True
                )
            if index == 0:
                pl.when(first)(weights[1].wait)
            for lanes in pieces(D):
                work[span, lanes] = dsec[span, lanes] + dot(dpre[span], vin[:, lanes])
            gain_sum = jnp.zeros((BLOCK // 2, D), F32)
            shift_sum = jnp.zeros((BLOCK // 2, D), F32)
            for block in row_blocks(start, size):
                g = work[block, :]
                z = z1b[side, block, :]
                back = norm_back(g, z, r1b[side, block, :1], gain_one[...])
                work[block, :] = back
                dbr[block, :] = back.astype(BF)
                gain_sum += folded_rows(g * z)
                shift_sum += folded_rows(g)
            o_small[0:1, :] += jnp.sum(gain_sum, axis=0, keepdims=True)
            o_small[1:2, :] += jnp.sum(shift_sum, axis=0, keepdims=True)
            if index == 0:
                pl.when(first)(weights[2].wait)
            for lanes in pieces(D):
                da[span, lanes] = dot(dbr[span], vproj[:, lanes]).astype(BF)
            heads = lax.broadcasted_iota(jnp.int32, (16, D), 0)
            columns = lax.broadcasted_iota(jnp.int32, (16, D), 1)
            member = (columns >= heads * HEAD) & (columns < (heads + 1) * HEAD)
            chooser = jnp.where(member, 1.0, 0.0).astype(BF)
            weighed = da[span, :].astype(F32) * attb[side, span, :]
            coarse = weighed.astype(BF)
            fine = (weighed - coarse.astype(F32)).astype(BF)
            row_sums = dot_nt(chooser, coarse) + dot_nt(chooser, fine)
            wide = 2 * size
            lane0 = lane_starts(chunks)[0][index]

            def score_grads(pair):
                values = kvb[side, :, pair_span(pair, D)]
                dp_tmp[pair % 2, :, :wide] = dot_nt(values, stacked_pair(da[span, pair_span(pair)]))

            score_grads(0)
            for pair in range(PAIRS):
                if pair + 1 < PAIRS:
                    score_grads(pair + 1)
                totals = jnp.concatenate(
                    [row_sums[2 * pair : 2 * pair + 1], row_sums[2 * pair + 1 : 2 * pair + 2]], axis=1
                )
                for begin in range(0, wide, 128):
                    lanes = slice(begin, min(begin + 128, wide))
                    kept_lanes = slice(lane0 + begin, lane0 + lanes.stop)
                    for offset in range(0, rows, BLOCK):
                        block = pl.ds(offset, BLOCK)
                        shifted = dp_tmp[pair % 2, block, lanes] - totals[:, lanes]
                        ds_tmp[pair, block, lanes] = (
                            probs[side, pair, block, kept_lanes].astype(F32) * shifted
                        ).astype(BF)
                d_keys = dot(ds_tmp[pair, :, :wide], scaled_queries(qb[side, span, pair_span(pair)]))
                d_values = dot(
                    probs[side, pair, :, lane0 : lane0 + wide], stacked_pair(da[span, pair_span(pair)])
                )
                if index == 0:
                    dkv[pair, :, :WIDE] = d_keys
                    dkv[pair, :, WIDE:] = d_values
                else:
                    dkv[pair, :, :WIDE] += d_keys
                    dkv[pair, :, WIDE:] += d_values
                if index == len(chunks) - 1:
                    move = remote(
                        dkv.at[pair, theirs],
                        dkv_in.at[side, pair],
                        kv_send.at[pair],
                        kv_recv.at[step, pair],
                        (s, place.other),
                    )
                    move.start()
                    sends.append(move)
            for pair in range(PAIRS):
                both = dot_tn(kvb[side, :, pair_span(pair)], ds_tmp[pair, :, :wide])
                dpj[span, pair_span(pair)] = (upright(both) * HEAD**-0.5).astype(BF)
        pl.when(first)(weights[3].wait)
        for lanes in pieces(D):
            work[:, lanes] += dot(dpj[:, :D], vqkv[:D, lanes])
        for pair in range(PAIRS):
            sends[pair].wait_recv()
            for which in range(2):
                lanes = slice(which * WIDE, (which + 1) * WIDE)
                dpj[:, pair_span(pair, (which + 1) * D)] = (
                    dkv[pair, own, lanes] + dkv_in[side, pair, :, lanes]
                ).astype(BF)
        for index, (start, size) in enumerate(chunks):
            span = pl.ds(start, size)
            for lanes in pieces(D):
                dxb[side, span, lanes] = (
                    work[span, lanes] + dot(dpj[span, D:], vqkv[D:, lanes])
                ).astype(BF)
            pl.when(s > 0)(handoff(step, index).start)
            if index == 0:

                @pl.when((s == 0) & (c == 0))
                def _():
                    mgb[step] = dxb[side, :slot].astype(F32) + dxb[side, slot : 2 * slot].astype(F32)
                    pl.when(step < steps - 2)(carry_move(step).start)

        for section in range(sections):
            dg[side, section] = dxb[side, :, section * part : (section + 1) * part]
        for copy in outgoing(step):
            copy.start()
        outgoing_dx(step).start()
        for move in sends:
            move.wait_send()

        @pl.when(step < steps - 2)
        def _():
            for copy in residuals(step + 2):
                copy.start()

    def one_round(turn, state):
        even, odd = 2 * turn, 2 * turn + 1
        late = (s == last) & (turn == 0)
        prologue(even)
        pl.when(jnp.logical_not(late))(lambda: prologue(odd))
        main(even)
        pl.when(late)(lambda: prologue(odd))
        main(odd)
        return state

    lax.fori_loop(0, segments, one_round, 0)
    settle(steps - 2)
    settle(steps - 1)
    for copy in outgoing(steps - 1):
        copy.wait()

    @pl.when((s == 0) & (c == 0))
    def _():
        for step in range(steps - 2, steps):
            for section in range(sections):
                mg[step % 2, section] = mgb[step, :, section * part : (section + 1) * part]
            outgoing_memory(step).start()
        for step in range(steps - 2, steps):
            outgoing_memory(step).wait()
        for step in range(steps - 2):
            carry_move(step).wait_send()


def backward(sections, segments, geometry, collective, g0, lens, kept, weights):
    mem, slot, tok, rows = geometry
    half = rows // 2
    steps = 2 * segments

    def grad(width):
        return jax.ShapeDtypeStruct((steps, half, width), BF)

    outs = (
        grad(3 * D),
        grad(D),
        grad(FF),
        grad(D),
        jax.ShapeDtypeStruct(g0.shape, BF),
        jax.ShapeDtypeStruct((2, g0.shape[1], slot, g0.shape[3]), F32),
        jax.ShapeDtypeStruct((8, D), F32),
    )
    dma = pltpu.SemaphoreType.DMA
    return pl.pallas_call(
        functools.partial(backward_kernel, sections, segments, geometry),
        name="backward_layer",
        out_shape=outs,
        in_specs=[ANY, VMEM] + [ANY] * 5 + [ANY] * 4 + [VMEM] * 2,
        out_specs=(ANY,) * 6 + (VMEM,),
        scratch_shapes=[
            pltpu.VMEM((3 * D, D), BF),
            pltpu.VMEM((D, D), BF),
            pltpu.VMEM((FF, D), BF),
            pltpu.VMEM((D, FF), BF),
            pltpu.VMEM((steps, half, D), BF),
            pltpu.VMEM((2, half, D), BF),
            pltpu.VMEM((2, rows, 2 * D), BF),
            pltpu.VMEM((2, half, FF), BF),
            pltpu.VMEM((2, half, D), F32),
            pltpu.VMEM((2, half, D), F32),
            pltpu.VMEM((2, half, D), F32),
            pltpu.VMEM((2, half, 128), F32),
            pltpu.VMEM((2, half, 128), F32),
            pltpu.VMEM((2, PAIRS, rows, lane_starts(row_chunks(half))[1]), BF),
            pltpu.VMEM((half, D), F32),
            pltpu.VMEM((half, D), F32),
            pltpu.VMEM((half, D), BF),
            pltpu.VMEM((half, FF), BF),
            pltpu.VMEM((half, D), BF),
            pltpu.VMEM((half, D), BF),
            pltpu.VMEM((2, rows, 2 * row_chunks(half)[-1][1]), F32),
            pltpu.VMEM((PAIRS, rows, 2 * row_chunks(half)[-1][1]), BF),
            pltpu.VMEM((PAIRS, rows, 2 * WIDE), F32),
            pltpu.VMEM((2, PAIRS, half, 2 * WIDE), F32),
            pltpu.VMEM((half, 3 * D), BF),
            pltpu.VMEM((2, half, D), BF),
            pltpu.VMEM((steps, slot, D), F32),
            pltpu.VMEM((steps, slot, D), F32),
            pltpu.VMEM(g0.shape, BF),
            pltpu.VMEM((2,) + g0.shape[1:], BF),
            pltpu.VMEM((2, g0.shape[1], slot, g0.shape[3]), F32),
            dma((4,)),
            dma((2, 5)),
            dma((steps,)),
            dma((6,)),
            dma((PAIRS,)),
            dma((steps, PAIRS)),
            dma((2, 2)),
            dma((steps, 2)),
            dma((steps,)),
            dma((steps,)),
        ],
        compiler_params=pltpu.CompilerParams(
            collective_id=collective, has_side_effects=True, vmem_limit_bytes=VMEM_LIMIT
        ),
    )(g0, lens, *kept, *weights)


def reduce_order(line):
    order = []
    low, high = 0, line - 1
    while low <= high:
        order.append(high)
        if low != high:
            order.append(low)
        low, high = low + 1, high - 1
    return order


def arrival_orders(line):
    def moment(chip, dest):
        upward = (line - 1 - dest) + chip
        downward = dest + (line - 1 - chip)
        if dest == chip:
            return line
        return upward if dest > chip else downward

    return [
        sorted(range(line), key=functools.partial(moment, chip)) for chip in range(line)
    ]


def finish_kernel(sections, segments, line, *refs):
    refs = list(refs)

    def take(count):
        taken = refs[:count]
        del refs[:count]
        return taken

    hid, dx, mem_in = take(3)
    lefts_in, rights_in, small_in = (take(4), take(4), take(1)[0]) if line else ((), (), None)
    o_h, o_x, o_m = take(3)
    outs = take(5) if line else ()
    h_send, h_got, x_send, x_got, m_send, m_got = take(6)
    place = Place(sections)
    s, c, d = place.s, place.c, place.d
    last = sections - 1
    steps = 2 * segments
    half = hid.shape[2]
    z = lax.div(d, 2)
    greet_plane(place, sections)
    if line:
        parts, sibs, ins, accs = take(5), take(5), take(5), take(5)
        big0, big1, flat0, flat1, flat2, flat3, turned = take(7)
        load, c_send, c_got, z_send, z_right, z_left, fin = take(7)
        up, down = (s, d + 2), (s, d - 2)

        def greet(target):
            pl.semaphore_signal(
                pltpu.get_barrier_semaphore(), inc=1, device_id=target, device_id_type=MESH
            )

        pl.when(z < line - 1)(lambda: greet(up))
        pl.when(z > 0)(lambda: greet(down))
        ends = (z == 0) | (z == line - 1)
        plane_wait(sections, jnp.where(ends, 1, 2))
    else:
        plane_wait(sections, 0)

    def deliveries():
        for src, dst, origin, send, got in (
            (hid, o_h, last, h_send, h_got),
            (dx, o_x, 0, x_send, x_got),
        ):
            for step in range(steps):
                segment, item = divmod(step, 2)
                rows = pl.ds(pl.multiple_of(c * half, BLOCK), half)
                for section in range(sections):
                    here = (s == section) & (c == item)
                    far = functools.partial(remote,
                        src.at[step, section],
                        dst.at[segment, rows],
                        send.at[step, section],
                        got.at[segment, c],
                        (section, place.base + item),
                    )
                    near = functools.partial(pltpu.make_async_copy,
                        src.at[step, section], dst.at[segment, rows], got.at[segment, c]
                    )
                    yield s == origin, here, far, near
        for item in range(2):
            for section in range(sections):
                here = (s == section) & (c == item)
                far = functools.partial(remote,
                    mem_in.at[item, section],
                    o_m,
                    m_send.at[item, section],
                    m_got.at[0],
                    (section, place.base + item),
                )
                near = functools.partial(pltpu.make_async_copy, mem_in.at[item, section], o_m, m_got.at[0])
                yield (s == 0) & (c == 0), here, far, near

    for mine, here, far, near in deliveries():
        pl.when(mine & jnp.logical_not(here))(lambda far=far: far().start())
        pl.when(mine & here)(lambda near=near: near().start())

    if line:
        act_in, nb_in, x_in, att_in = lefts_in
        dfe_in, dpre_in, dpj_in, dbr_in = rights_in

        def fetch(src, dst, slot):
            width = src.shape[-1]
            return [
                pltpu.make_async_copy(
                    src.at[step], dst.at[pl.ds(step * half, half), :width], load.at[slot, step]
                )
                for step in range(steps)
            ]

        loads = {
            "att": fetch(att_in, flat2, 4),
            "dbr": fetch(dbr_in, flat3, 5),
            "x": fetch(x_in, flat0, 3),
            "dpj": fetch(dpj_in, big0, 2),
            "nb": fetch(nb_in, flat1, 0),
            "dpre": fetch(dpre_in, big1, 1),
            "act": fetch(act_in, big0, 2),
            "dfe": fetch(dfe_in, flat0, 3),
        }

        def begin(name):
            for copy in loads[name]:
                copy.start()

        def ready(name):
            for copy in loads[name]:
                copy.wait()

        for name in ("att", "dbr", "x", "dpj", "nb", "dpre"):
            begin(name)
        order = reduce_order(line)
        kinds = (4, 3, 2, 0, 1)
        flows = [(kind, dest) for kind in kinds for dest in order]
        depth = 2
        far_up, far_down = range(line - 1, 0, -1), range(line - 1)
        ends_first = (
            ([(kind, dest) for kind in kinds for dest in far_up], 1, 0),
            ([(kind, dest) for kind in kinds for dest in far_down], -1, line - 1),
        )

        def arrival(position):
            dest = 0
            for chip, row in enumerate(arrival_orders(line)):
                for index, value in enumerate(row):
                    dest += jnp.where((z == chip) & (position == index), value, 0)
            return dest

        def own_rows(kind):
            block = parts[kind].shape[1] // 2
            return pl.ds(pl.multiple_of(c * block, 8), block)

        def core_move(kind, dest):
            block = parts[kind].shape[1] // 2
            theirs = pl.ds(pl.multiple_of((1 - c) * block, 8), block)
            return remote(
                parts[kind].at[dest, theirs],
                sibs[kind].at[dest],
                c_send.at[kind, dest],
                c_got.at[kind, dest],
                (s, place.other),
            )

        def line_move(kind, dest, towards):
            if towards > 0:
                slot, target, got = dest, up, z_right
            else:
                slot, target, got = jnp.where(z - 1 == dest, line, dest), down, z_left
            return remote(
                parts[kind].at[dest, own_rows(kind)],
                ins[kind].at[slot],
                z_send.at[kind, dest],
                got.at[kind, dest],
                target,
            )

        def add(kind, dest, ref, slot):
            acc = accs[kind]
            rows = min(BLOCK, acc.shape[0])

            def block(index, state):
                span = pl.ds(pl.multiple_of(index * rows, rows), rows)
                acc[span, :] += ref[slot, span, :].astype(F32)
                return state

            lax.fori_loop(0, acc.shape[0] // rows, block, 0)

        def hop(kind, dest):
            acc = accs[kind]
            core_move(kind, dest).wait_recv()
            acc[...] = parts[kind][dest, own_rows(kind), :].astype(F32)
            add(kind, dest, sibs[kind], dest)

            @pl.when((z > 0) & (z <= dest))
            def _():
                line_move(kind, dest, 1).wait_recv()
                add(kind, dest, ins[kind], dest)

            @pl.when((z < line - 1) & (z >= dest))
            def _():
                line_move(kind, dest, -1).wait_recv()
                add(kind, dest, ins[kind], jnp.where(z == dest, line, dest))

            @pl.when(z != dest)
            def _():
                parts[kind][dest, own_rows(kind), :] = acc[...].astype(parts[kind].dtype)

            for sequence, towards, end in ends_first if isinstance(dest, int) else ():
                spot = sequence.index((kind, dest)) if (kind, dest) in sequence else 0
                if spot >= depth:
                    earlier = functools.partial(line_move, *sequence[spot - depth], towards)
                    pl.when(z == end)(lambda earlier=earlier: earlier().wait_send())
            pl.when(z < dest)(lambda: line_move(kind, dest, 1).start())
            pl.when(z > dest)(lambda: line_move(kind, dest, -1).start())

            @pl.when(z == dest)
            def _():
                copy = pltpu.make_async_copy(acc, outs[kind], fin.at[kind])
                copy.start()
                copy.wait()

        def no_wait(dest):
            return ((z == 0) & (dest > 0)) | ((z == line - 1) & (dest < line - 1))

        matrices = (
            ("nb", "dpre", flat1, big1, FF),
            ("act", "dfe", big0, flat0, D),
            ("x", "dpj", flat0, big0, 3 * D),
            ("att", "dbr", flat2, flat3, D),
        )
        size = D // (2 * line)
        long = FF // (2 * line)
        for dest in order:
            parts[4][dest] = jnp.zeros(parts[4].shape[1:], F32)
            for core in range(2):
                index = 2 * dest + core
                for row in range(4):
                    parts[4][dest, 8 * core + row : 8 * core + row + 1, :size] = small_in[
                        row : row + 1, index * size : (index + 1) * size
                    ]
                row, column = divmod(index * long, D)
                parts[4][dest, 8 * core + 4 : 8 * core + 5, :] = small_in[
                    4 + row : 5 + row, column : column + long
                ]
            core_move(4, dest).start()

        def from_ends(kind):
            for dest in far_up:
                pl.when(z == 0)(functools.partial(hop, kind, dest))
            for dest in far_down:
                pl.when(z == line - 1)(functools.partial(hop, kind, dest))

        from_ends(4)
        for kind in kinds[1:]:
            left_name, right_name, left, right, width = matrices[kind]
            if kind == 1:
                begin(left_name)
                begin(right_name)
            ready(left_name)
            ready(right_name)
            block = parts[kind].shape[1]
            for dest in order:
                turned[:block, :] = jnp.transpose(left[:, dest * block : (dest + 1) * block])
                for lanes in pieces(width):
                    parts[kind][dest, :, lanes] = dot(turned[:block, :], right[:, lanes]).astype(BF)
                core_move(kind, dest).start()
            from_ends(kind)
        for kind in kinds:

            def by_arrival(position, state):
                dest = arrival(position)
                pl.when(jnp.logical_not(no_wait(dest)))(lambda: hop(kind, dest))
                return state

            lax.fori_loop(0, line, by_arrival, 0)
        for kind, dest in flows:
            core_move(kind, dest).wait_send()
            for sequence, towards, end in ends_first:
                if (kind, dest) in sequence:
                    pending = (z < dest) if towards > 0 else (z > dest)
                    if (kind, dest) not in sequence[-depth:]:
                        pending &= z != end
                    pl.when(pending)(lambda: line_move(kind, dest, towards).wait_send())

    for mine, here, far, near in deliveries():
        pl.when(mine & jnp.logical_not(here))(lambda far=far: far().wait_send())
    for src, dst, origin, got in ((hid, o_h, last, h_got), (dx, o_x, 0, x_got)):
        for segment in range(segments):
            for core in range(2):
                rows = pl.ds(core * half, half)
                here = (s == origin) & (c == core)
                far = functools.partial(remote,
                    src.at[0, 0], dst.at[segment, rows], h_send.at[0, 0], got.at[segment, core], (s, d)
                )
                near = functools.partial(pltpu.make_async_copy, src.at[0, 0], dst.at[segment, rows], got.at[segment, core])
                pl.when(jnp.logical_not(here))(lambda far=far: far().wait_recv())
                pl.when(here)(lambda near=near: near().wait())
    here = (s == 0) & (c == 0)
    far = functools.partial(remote, mem_in.at[0, 0], o_m, m_send.at[0, 0], m_got.at[0], (s, d))
    near = functools.partial(pltpu.make_async_copy, mem_in.at[0, 0], o_m, m_got.at[0])
    pl.when(jnp.logical_not(here))(lambda far=far: far().wait_recv())
    pl.when(here)(lambda near=near: near().wait())


def finish(sections, segments, line, collective, hid, dx, memory_term, sums):
    steps, _, half, part = hid.shape
    slot = memory_term.shape[2]
    dma = pltpu.SemaphoreType.DMA
    outs = [
        jax.ShapeDtypeStruct((segments, 2 * half, part), BF),
        jax.ShapeDtypeStruct((segments, 2 * half, part), BF),
        jax.ShapeDtypeStruct((slot, part), F32),
    ]
    scratch = [
        dma((steps, sections)),
        dma((segments, 2)),
        dma((steps, sections)),
        dma((segments, 2)),
        dma((2, sections)),
        dma((1,)),
    ]
    operands = [hid, dx, memory_term]
    if line:
        lefts, rights, small = sums
        operands += [*lefts, *rights, small]
        block = D // (2 * line)
        shapes = (
            (block, FF, BF),
            (FF // (2 * line), D, BF),
            (block, 3 * D, BF),
            (block, D, BF),
            (8, FF // (2 * line), F32),
        )
        outs += [jax.ShapeDtypeStruct(shape[:2], F32) for shape in shapes]
        total = steps * half
        scratch += [pltpu.VMEM((line, 2 * rows, width), kind) for rows, width, kind in shapes]
        scratch += [pltpu.VMEM((line, rows, width), kind) for rows, width, kind in shapes]
        scratch += [pltpu.VMEM((line + 1, rows, width), kind) for rows, width, kind in shapes]
        scratch += [pltpu.VMEM((rows, width), F32) for rows, width, kind in shapes]
        scratch += [pltpu.VMEM((total, FF), BF)] * 2 + [pltpu.VMEM((total, D), BF)] * 4
        scratch += [pltpu.VMEM((FF // line, total), BF)]
        scratch += [
            dma((6, steps)),
            dma((5, line)),
            dma((5, line)),
            dma((5, line)),
            dma((5, line)),
            dma((5, line)),
            dma((5,)),
        ]
    return pl.pallas_call(
        functools.partial(finish_kernel, sections, segments, line),
        name="finish",
        out_shape=tuple(outs),
        in_specs=[ANY] * (len(operands) - bool(line)) + [VMEM] * bool(line),
        out_specs=(ANY,) * len(outs),
        scratch_shapes=scratch,
        compiler_params=pltpu.CompilerParams(
            collective_id=collective, has_side_effects=True, vmem_limit_bytes=VMEM_LIMIT
        ),
    )(*operands)


def on_device(
    sections,
    inputs,
    out_grad,
    memory,
    lengths,
    w_qkv,
    w_proj,
    gain_one,
    shift_one,
    w_in,
    b_in,
    w_down,
    gain_two,
    shift_two,
):
    segs, tok, part = inputs.shape[1:]
    mem = memory.shape[1]
    slot = -(-mem // BLOCK) * BLOCK
    rows = -(-(2 * slot + tok) // (2 * BLOCK)) * 2 * BLOCK
    half = rows // 2
    geometry = (mem, slot, tok, rows)
    back_pad = rows - 2 * slot - tok

    head = jnp.pad(memory[:1], ((0, segs - 1), (0, slot - mem), (0, 0)))
    blank = jnp.zeros((segs, back_pad, part), BF)
    tokens = jnp.concatenate([head, head, inputs[0], blank], axis=1)
    cotangent = jnp.pad(out_grad[0], ((0, 0), (2 * slot, back_pad), (0, 0)))
    length_tile = jnp.broadcast_to(lengths.astype(F32), (8, 128))

    def halves(array):
        return array.reshape(segs, 2, half, part)

    matrices = (w_qkv[0], w_proj[0], w_in[0], w_down[0])
    forward_weights = matrices + (gain_one, shift_one, b_in, gain_two, shift_two)
    x, q, kv, att, nb, act, gp, s1, s2, hid, *turned, g0, lens = forward(
        sections, segs, geometry, 0, halves(tokens), halves(cotangent), length_tile, forward_weights
    )
    dpj, dbr, dpre, dfe, dx, memory_term, small = backward(
        sections, segs, geometry, 1, g0, lens, (q, kv, gp, s1, s2), (*turned, gain_one, gain_two)
    )
    devices = lax.axis_size("dp")
    lefts, rights = (act, nb, x, att), (dfe, dpre, dpj, dbr)
    line = devices // 2 if D % (devices * BLOCK) == 0 and FF % (devices * 128) == 0 and devices > 2 else 0
    sums = None
    if line:
        sums = (lefts, rights, small)
    out_parts, in_parts, memory_part, *reduced = finish(
        sections, segs, line, 2, hid, dx, memory_term, sums
    )

    def owned(parts):
        return parts[:, 2 * slot : 2 * slot + tok]

    position = jnp.arange(segs * tok, dtype=jnp.int32).reshape(segs, tok)
    token_valid = position < lengths[0]
    outputs = jnp.where(token_valid[:, :, None], owned(out_parts), jnp.zeros((), BF))
    input_grad = owned(in_parts)
    memory_grad = memory_part[:mem]

    if line:
        d_in, d_down, d_qkv, d_proj, share = reduced
        size = D // devices
        vectors = [share[k : k + 1, :size] for k in range(4)] + [share[4:5]]
    else:

        def weight_grad(left, right):
            full = jnp.einsum(
                "rd,re->de",
                left.reshape(2 * segs * half, -1),
                right.reshape(2 * segs * half, -1),
                preferred_element_type=F32,
            )
            return lax.psum_scatter(full.astype(BF), "dp", scatter_dimension=0, tiled=True).astype(F32)

        d_down, d_in, d_qkv, d_proj = [weight_grad(*pair) for pair in zip(lefts, rights)]
        vectors = [
            lax.psum_scatter(rows.reshape(1, -1), "dp", scatter_dimension=1, tiled=True)
            for rows in (small[0], small[1], small[2], small[3], small[4:8])
        ]
    gain_one_share, shift_one_share, gain_two_share, shift_two_share, b_in_share = vectors

    return (
        outputs[None],
        input_grad[None],
        memory_grad[None],
        d_qkv[None],
        d_proj[None],
        gain_one_share,
        shift_one_share,
        d_in[None],
        b_in_share,
        d_down[None],
        gain_two_share,
        shift_two_share,
    )


def solution(mesh):
    return jax.shard_map(
        functools.partial(on_device, mesh.shape["section"]),
        mesh=mesh,
        in_specs=(
            P("dp", None, None, "section"),
            P("dp", None, None, "section"),
            P("dp", None, "section"),
            P("dp"),
            P("section", None, None),
            P("section", None, None),
            P("section", None),
            P("section", None),
            P("section", None, None),
            P("section", None),
            P("section", None, None),
            P("section", None),
            P("section", None),
        ),
        out_specs=(
            P("dp", None, None, "section"),
            P("dp", None, None, "section"),
            P("dp", None, "section"),
            P("section", "dp", None),
            P("section", "dp", None),
            P("section", "dp"),
            P("section", "dp"),
            P("section", "dp", None),
            P("section", "dp"),
            P("section", "dp", None),
            P("section", "dp"),
            P("section", "dp"),
        ),
        check_vma=False,
    )
```

```python
import functools

import jax
import jax.numpy as jnp
from jax import lax
from jax.experimental import pallas as pl
from jax.experimental.pallas import tpu as pltpu
from jax.sharding import PartitionSpec as P

D = 768
H = 12
HEAD = 64
FF = 3072
PAIRS = H // 2
WIDE = 2 * HEAD
STEP = 256
BLOCK = 16
BF = jnp.bfloat16
F32 = jnp.float32
MESH = pl.DeviceIdType.MESH
ANY = pl.BlockSpec(memory_space=pl.ANY)
VMEM = pl.BlockSpec(memory_space=pltpu.VMEM)
VMEM_LIMIT = 63 * 1024 * 1024


def dot(a, b):
    return jnp.dot(a, b, preferred_element_type=F32)


def dot_nt(a, b):
    return lax.dot_general(a, b, (((1,), (1,)), ((), ())), preferred_element_type=F32)


def dot_tn(a, b):
    return lax.dot_general(a, b, (((0,), (0,)), ((), ())), preferred_element_type=F32)


def cols(index):
    return pl.ds(index * STEP, STEP)


def remote(src, dst, send, recv, target):
    return pltpu.make_async_remote_copy(
        src_ref=src, dst_ref=dst, send_sem=send, recv_sem=recv, device_id=target, device_id_type=MESH
    )


class Place:
    def __init__(self, sections):
        self.s = lax.axis_index("section")
        self.d = lax.axis_index("dp")
        self.c = lax.rem(self.d, 2)
        self.base = self.d - self.c
        self.other = self.base + 1 - self.c
        self.next = lax.rem(self.s + 1, sections)
        self.prev = lax.rem(self.s + sections - 1, sections)


def greet_plane(place, sections):
    barrier = pltpu.get_barrier_semaphore()
    for section in range(sections):
        for core in range(2):

            @pl.when((place.s != section) | (place.c != core))
            def _():
                pl.semaphore_signal(
                    barrier, inc=1, device_id=(section, place.base + core), device_id_type=MESH
                )


def plane_wait(sections, extra):
    pl.semaphore_wait(pltpu.get_barrier_semaphore(), 2 * sections - 1 + extra)


def key_bias(geometry, segment, length, shape, dim):
    mem, slot, tok, rows = geometry
    row = lax.broadcasted_iota(jnp.int32, shape, dim)
    position = row - 2 * slot + segment * tok
    is_token = (row >= 2 * slot) & (row < 2 * slot + tok) & (position.astype(F32) < length)
    is_memory = (row < mem) | ((row >= slot) & (row < slot + mem))
    return jnp.where(is_token | is_memory, 0.0, -1e30)


def stacked_pair(pair):
    lane = lax.broadcasted_iota(jnp.int32, pair.shape, 1)
    zero = jnp.zeros_like(pair)
    return jnp.concatenate(
        [jnp.where(lane < HEAD, pair, zero), jnp.where(lane >= HEAD, pair, zero)], axis=0
    )


def folded_pair(both):
    half = both.shape[0] // 2
    lane = lax.broadcasted_iota(jnp.int32, (half, WIDE), 1)
    return jnp.where(lane < HEAD, both[:half], both[half:])


def upright(both):
    size = both.shape[1] // 2
    row = lax.broadcasted_iota(jnp.int32, (WIDE, size), 0)
    return jnp.transpose(jnp.where(row < HEAD, both[:, :size], both[:, size:]))


def scaled_queries(queries):
    return stacked_pair(queries * jnp.asarray(HEAD**-0.5, BF))


def normalized(rows):
    center = rows - jnp.mean(rows, axis=-1, keepdims=True)
    spread_of = jnp.mean(center * center, axis=-1, keepdims=True)
    scale = lax.rsqrt(spread_of + 1e-06)
    return center * scale, scale


def pieces(width, step=STEP):
    return [slice(start, start + step) for start in range(0, width, step)]


def row_chunks(half):
    first = half // 2 // BLOCK * BLOCK
    return ((0, first), (first, half - first))


def lane_starts(chunks):
    starts, total = [], 0
    for _, size in chunks:
        starts.append(total)
        total += -(-2 * size // 128) * 128
    return starts, total


def row_blocks(start, size):
    return [pl.ds(start + offset, BLOCK) for offset in range(0, size, BLOCK)]


def pair_span(pair, offset=0):
    return slice(offset + pair * WIDE, offset + (pair + 1) * WIDE)


def forward_kernel(
    sections,
    segments,
    geometry,
    a_ref,
    g_ref,
    len_ref,
    w_qkv,
    w_proj,
    w_in,
    w_down,
    gain_one,
    shift_one,
    b_in,
    gain_two,
    shift_two,
    o_x,
    o_q,
    o_kv,
    o_att,
    o_nb,
    o_act,
    o_gp,
    o_s1,
    o_s2,
    o_hid,
    t_qkv,
    t_proj,
    t_in,
    t_down,
    o_g,
    o_lens,
    vqkv,
    vproj,
    vin,
    vdown,
    xb,
    kvb,
    qb,
    attb,
    nbb,
    actb,
    gpb,
    s1b,
    s2b,
    hb,
    preb,
    nf,
    memb,
    s_tmp,
    probs,
    turned,
    xp,
    hg,
    lens_ref,
    wsem,
    osem,
    kv_send,
    kv_recv,
    h_send,
    h_recv,
    m_send,
    m_recv,
    tsem,
    a_send,
    a_got,
    g_send,
    g_got,
    l_send,
    l_got,
):
    place = Place(sections)
    s, c = place.s, place.c
    mem, slot, tok, rows = geometry
    half = rows // 2
    last = sections - 1
    steps = 2 * segments
    chunks = row_chunks(half)
    early = s >= 2
    weights = [
        pltpu.make_async_copy(src, dst, wsem.at[k])
        for k, (src, dst) in enumerate(((w_qkv, vqkv), (w_proj, vproj), (w_in, vin), (w_down, vdown)))
    ]

    part = a_ref.shape[-1]
    greet_plane(place, sections)
    plane_wait(sections, 0)

    def spread(src, dst, target, send, got, segment):
        step = 2 * segment + c
        for core in range(2):
            here = (s == target) & (c == core)
            far = functools.partial(remote,
                src.at[segment, core],
                dst.at[step, s],
                send.at[segment, core],
                got.at[step, s],
                (target, place.base + core),
            )
            near = functools.partial(pltpu.make_async_copy, src.at[segment, core], dst.at[step, s], got.at[step, s])
            yield here, far, near

    def tokens(segment):
        return spread(a_ref, xp, 0, a_send, a_got, segment)

    def cotangents(segment):
        return spread(g_ref, o_g, last, g_send, g_got, segment)

    def begin(moves):
        for here, far, near in moves:
            pl.when(jnp.logical_not(here))(lambda far=far: far().start())
            pl.when(here)(lambda near=near: near().start())

    def sent(moves):
        for here, far, _ in moves:
            pl.when(jnp.logical_not(here))(lambda far=far: far().wait_send())

    def arrived(src, dst, got, target, step, section):
        side = lax.rem(step, 2)
        here = (section == target) & (side == c)
        far = functools.partial(remote,
            src.at[0, 0], dst.at[step, section], a_send.at[0, 0], got.at[step, section], (s, place.d)
        )
        near = functools.partial(pltpu.make_async_copy, src.at[0, 0], dst.at[step, section], got.at[step, section])
        pl.when(jnp.logical_not(here))(lambda far=far: far().wait_recv())
        pl.when(here)(lambda near=near: near().wait())

    begin(tokens(0))
    length_move = remote(len_ref, lens_ref.at[c], l_send.at[0], l_got.at[0], (s, place.other))
    length_move.start()
    lens_ref[c] = len_ref[...]
    for copy in weights:
        copy.start()
    sent(tokens(0))
    for segment in range(1, segments):
        begin(tokens(segment))
    for segment in range(segments):
        begin(cotangents(segment))
    remote(len_ref, lens_ref.at[1 - c], l_send.at[0], l_got.at[0], (s, place.other)).wait_recv()

    def outgoing(step):
        side = lax.rem(step, 2)
        pairs = (
            (xb.at[step], o_x),
            (kvb.at[step], o_kv),
            (qb.at[side], o_q),
            (attb.at[side], o_att),
            (nbb.at[side], o_nb),
            (actb.at[side], o_act),
            (gpb.at[side], o_gp),
            (s1b.at[side], o_s1),
            (s2b.at[side], o_s2),
            (hg.at[side], o_hid),
        )
        return [
            pltpu.make_async_copy(src, dst.at[step], osem.at[side, k])
            for k, (src, dst) in enumerate(pairs)
        ]

    def handoff(step, index):
        start, size = chunks[index]
        side = lax.rem(step, 2)
        span = pl.ds(start, size)
        return remote(
            hb.at[side, span],
            xb.at[step, span],
            h_send.at[side, index],
            h_recv.at[step, index],
            (place.next, place.d),
        )

    def memory_move(step):
        side = lax.rem(step, 2)
        return remote(
            hb.at[side, pl.ds(slot, slot)], memb.at[step], m_send.at[side], m_recv.at[step], (0, place.d)
        )

    def exchange(step, index):
        start, size = chunks[index]
        span = pl.ds(pl.multiple_of(c * half + start, BLOCK), size)
        return remote(
            kvb.at[step, span],
            kvb.at[step, span],
            kv_send.at[index],
            kv_recv.at[step, index],
            (s, place.other),
        )

    def settle(step):
        @pl.when(s < last)
        def _():
            for index in range(len(chunks)):
                handoff(step, index).wait_send()

        @pl.when((s == last) & (c == 0) & (step < steps - 2))
        def _():
            memory_move(step).wait_send()

        for copy in outgoing(step):
            copy.wait()

    def turn_weights():
        @pl.when(early)
        def _():
            for copy in weights:
                copy.wait()

        blocks = []
        for src, dst in ((vqkv, t_qkv), (vproj, t_proj), (vin, t_in), (vdown, t_down)):
            for block in range(src.shape[0] * src.shape[1] // (D * D)):
                span = pl.ds(block * D, D)
                if src.shape[0] == D:
                    blocks.append((src, (slice(None), span), dst.at[span]))
                else:
                    blocks.append((src, (span, slice(None)), dst.at[:, span]))
        moves = []
        for index, (src, where, dst) in enumerate(blocks):
            spot = index % 3
            if index >= 3:
                moves[index - 3].wait()
            turned[spot] = jnp.transpose(src[where])
            moves.append(pltpu.make_async_copy(turned.at[spot], dst, tsem.at[spot]))
            moves[-1].start()
        for move in moves[-3:]:
            move.wait()

    def one_step(step, state):
        pl.when(step == jnp.where(early, 0, steps))(turn_weights)
        pl.when(step < steps)(lambda: compute_step(step))
        return state

    def compute_step(step):
        side = lax.rem(step, 2)
        segment = lax.div(step, 2)
        first = (step == 0) & jnp.logical_not(early)

        @pl.when(s == 0)
        def _():
            for section in range(sections):
                arrived(a_ref, xp, a_got, 0, step, section)
                xb[step, :, section * part : (section + 1) * part] = xp[step, section]

            @pl.when((c == 0) & (step >= 2))
            def _():
                memory_move(step - 2).wait_recv()
                xb[step, :slot] = memb[step - 2]
                xb[step, slot : 2 * slot] = memb[step - 2]

        pl.when(step >= 2)(lambda: settle(step - 2))
        for index, (start, size) in enumerate(chunks):
            span = pl.ds(start, size)

            @pl.when(s > 0)
            def _():
                handoff(step, index).wait_recv()

            if index == 0:
                pl.when(first)(weights[0].wait)
            own = pl.ds(pl.multiple_of(c * half + start, BLOCK), size)
            for lanes in pieces(2 * D):
                kvb[step, own, lanes] = dot(
                    xb[step, span], vqkv[:, D + lanes.start : D + lanes.stop]
                ).astype(BF)
            exchange(step, index).start()
            for lanes in pieces(D):
                qb[side, span, lanes] = dot(xb[step, span], vqkv[:, lanes]).astype(BF)
        bias = key_bias(geometry, segment, lens_ref[side, :1, :1], (1, rows), 1)
        for index in range(len(chunks)):
            exchange(step, index).wait_recv()
        for index, (start, size) in enumerate(chunks):
            span = pl.ds(start, size)

            def score(pair):
                lanes = pair_span(pair)
                s_tmp[pair % 2, : 2 * size] = dot_nt(
                    scaled_queries(qb[side, span, lanes]), kvb[step, :, lanes]
                )

            score(0)
            for pair in range(PAIRS):
                if pair + 1 < PAIRS:
                    score(pair + 1)
                for offset in range(0, 2 * size, 2 * BLOCK):
                    block = pl.ds(offset, 2 * BLOCK)
                    scores = s_tmp[pair % 2, block, :] + bias
                    exponent = jnp.exp(scores - jnp.max(scores, axis=-1, keepdims=True))
                    inverse = 1.0 / jnp.sum(exponent, axis=-1, keepdims=True)
                    probs[pair, block, :] = (exponent * inverse).astype(BF)
            for pair in range(PAIRS):
                mixed = dot(probs[pair, : 2 * size], kvb[step, :, pair_span(pair, D)])
                attb[side, span, pair_span(pair)] = folded_pair(mixed).astype(BF)
            if index == 0:
                pl.when(first)(weights[1].wait)
            for lanes in pieces(D):
                s1b[side, span, lanes] = xb[step, span, lanes].astype(F32) + dot(
                    attb[side, span], vproj[:, lanes]
                )
            for block in row_blocks(start, size):
                z, _ = normalized(s1b[side, block, :])
                normed = z * gain_one[...] + shift_one[...]
                nf[block, :] = normed
                nbb[side, block, :] = normed.astype(BF)
            if index == 0:
                pl.when(first)(weights[2].wait)
            for lanes in pieces(FF):
                pre = dot(nbb[side, span], vin[:, lanes]) + b_in[:, lanes]
                preb[span, lanes] = pre
                actb[side, span, lanes] = (
                    0.5 * pre * (1.0 + lax.erf(pre * 0.7071067811865476))
                ).astype(BF)
            if index == 0:
                pl.when(first)(weights[3].wait)
            for lanes in pieces(D):
                s2b[side, span, lanes] = nf[span, lanes] + dot(actb[side, span], vdown[:, lanes])
            for block in row_blocks(start, size):
                z, _ = normalized(s2b[side, block, :])
                hb[side, block, :] = (z * gain_two[...] + shift_two[...]).astype(BF)

            pl.when(s < last)(handoff(step, index).start)
            if index == 0:

                @pl.when((s == last) & (c == 0) & (step < steps - 2))
                def _():
                    memory_move(step).start()

        for block in row_blocks(0, half):
            pre = preb[block, :]
            density = jnp.exp(-0.5 * pre * pre) * 0.3989422804014327
            slope = 0.5 * (1.0 + lax.erf(pre * 0.7071067811865476)) + pre * density
            gpb[side, block, :] = slope.astype(BF)
        for section in range(sections):
            hg[side, section] = hb[side, :, section * part : (section + 1) * part]
        for copy in outgoing(step):
            copy.start()
        for index in range(len(chunks)):
            exchange(step, index).wait_send()

    lax.fori_loop(0, steps + 1, one_step, 0)
    settle(steps - 2)
    settle(steps - 1)
    o_lens[...] = lens_ref[...]
    length_move.wait_send()
    for segment in range(segments):
        if segment > 0:
            sent(tokens(segment))
        sent(cotangents(segment))

    @pl.when(s == last)
    def _():
        for step in range(steps):
            for section in range(sections):
                arrived(g_ref, o_g, g_got, last, step, section)


def forward(sections, segments, geometry, collective, a, g, length_tile, weights):
    mem, slot, tok, rows = geometry
    half = rows // 2
    steps = 2 * segments
    grouped = (steps, sections, half, a.shape[-1])

    def kept(width, kind, height=half):
        return jax.ShapeDtypeStruct((steps, height, width), kind)

    outs = (
        kept(D, BF),
        kept(D, BF),
        kept(2 * D, BF, rows),
        kept(D, BF),
        kept(D, BF),
        kept(FF, BF),
        kept(FF, BF),
        kept(D, F32),
        kept(D, F32),
        jax.ShapeDtypeStruct(grouped, BF),
        jax.ShapeDtypeStruct((3 * D, D), BF),
        jax.ShapeDtypeStruct((D, D), BF),
        jax.ShapeDtypeStruct((FF, D), BF),
        jax.ShapeDtypeStruct((D, FF), BF),
        jax.ShapeDtypeStruct(grouped, BF),
        jax.ShapeDtypeStruct((2, 8, 128), F32),
    )
    dma = pltpu.SemaphoreType.DMA
    return pl.pallas_call(
        functools.partial(forward_kernel, sections, segments, geometry),
        name="forward_layer",
        out_shape=outs,
        in_specs=[ANY, ANY, VMEM] + [ANY] * 4 + [VMEM] * 5,
        out_specs=(ANY,) * (len(outs) - 1) + (VMEM,),
        scratch_shapes=[
            pltpu.VMEM((D, 3 * D), BF),
            pltpu.VMEM((D, D), BF),
            pltpu.VMEM((D, FF), BF),
            pltpu.VMEM((FF, D), BF),
            pltpu.VMEM((steps, half, D), BF),
            pltpu.VMEM((steps, rows, 2 * D), BF),
            pltpu.VMEM((2, half, D), BF),
            pltpu.VMEM((2, half, D), BF),
            pltpu.VMEM((2, half, D), BF),
            pltpu.VMEM((2, half, FF), BF),
            pltpu.VMEM((2, half, FF), BF),
            pltpu.VMEM((2, half, D), F32),
            pltpu.VMEM((2, half, D), F32),
            pltpu.VMEM((2, half, D), BF),
            pltpu.VMEM((half, FF), F32),
            pltpu.VMEM((half, D), F32),
            pltpu.VMEM((steps, slot, D), BF),
            pltpu.VMEM((2, 2 * row_chunks(half)[-1][1], rows), F32),
            pltpu.VMEM((PAIRS, 2 * row_chunks(half)[-1][1], rows), BF),
            pltpu.VMEM((3, D, D), BF),
            pltpu.VMEM(grouped, BF),
            pltpu.VMEM((2,) + grouped[1:], BF),
            pltpu.VMEM((2, 8, 128), F32),
            dma((4,)),
            dma((2, 10)),
            dma((2,)),
            dma((steps, 2)),
            dma((2, 2)),
            dma((steps, 2)),
            dma((2,)),
            dma((steps,)),
            dma((3,)),
            dma((segments, 2)),
            dma((steps, sections)),
            dma((segments, 2)),
            dma((steps, sections)),
            dma((1,)),
            dma((1,)),
        ],
        compiler_params=pltpu.CompilerParams(
            collective_id=collective, has_side_effects=True, vmem_limit_bytes=VMEM_LIMIT
        ),
    )(a, g, length_tile, *weights)


def backward_kernel(
    sections,
    segments,
    geometry,
    g0_ref,
    lens_ref,
    r_q,
    r_kv,
    r_gp,
    r_s1,
    r_s2,
    w_qkv,
    w_proj,
    w_in,
    w_down,
    gain_one,
    gain_two,
    o_dpj,
    o_dbr,
    o_dpre,
    o_dfe,
    o_dx,
    o_mg,
    o_small,
    vqkv,
    vproj,
    vin,
    vdown,
    gb,
    qb,
    kvb,
    gpb,
    z1b,
    z2b,
    attb,
    r1b,
    r2b,
    probs,
    work,
    dsec,
    dfe,
    dpre,
    dbr,
    da,
    dp_tmp,
    ds_tmp,
    dkv,
    dkv_in,
    dpj,
    dxb,
    mgb,
    carb,
    gp_in,
    dg,
    mg,
    wsem,
    rsem,
    gsem,
    osem,
    kv_send,
    kv_recv,
    h_send,
    h_recv,
    m_send,
    m_recv,
):
    place = Place(sections)
    s, c = place.s, place.c
    mem, slot, tok, rows = geometry
    half = rows // 2
    own = pl.ds(pl.multiple_of(c * half, BLOCK), half)
    theirs = pl.ds(pl.multiple_of((1 - c) * half, BLOCK), half)
    last = sections - 1
    steps = 2 * segments
    part = g0_ref.shape[-1]
    chunks = row_chunks(half)
    weights = [
        pltpu.make_async_copy(src, dst, wsem.at[k])
        for k, (src, dst) in enumerate(((w_down, vdown), (w_in, vin), (w_proj, vproj), (w_qkv, vqkv)))
    ]

    def kept_index(step):
        return 2 * (segments - 1 - lax.div(step, 2)) + lax.rem(step, 2)

    def residuals(step):
        side = lax.rem(step, 2)
        pairs = ((r_q, qb), (r_kv, kvb), (r_s2, z2b), (r_gp, gpb), (r_s1, z1b))
        return [
            pltpu.make_async_copy(src.at[kept_index(step)], dst.at[side], rsem.at[side, k])
            for k, (src, dst) in enumerate(pairs)
        ]

    def seed_copy(step):
        return pltpu.make_async_copy(g0_ref.at[kept_index(step)], gp_in.at[lax.rem(step, 2)], gsem.at[step])

    for step in range(2):
        for copy in residuals(step):
            copy.start()
        if step == 0:
            for copy in weights:
                copy.start()

    @pl.when(s == last)
    def _():
        for step in range(2):
            seed_copy(step).start()

    o_small[...] = jnp.zeros_like(o_small)
    barrier = pltpu.get_barrier_semaphore()
    pl.semaphore_signal(barrier, inc=1, device_id=(place.next, place.d), device_id_type=MESH)
    pl.semaphore_signal(barrier, inc=1, device_id=(s, place.other), device_id_type=MESH)
    pl.semaphore_wait(barrier, 2)

    def outgoing(step):
        pairs = (
            (dpj, o_dpj),
            (dbr, o_dbr),
            (dpre, o_dpre),
            (dfe, o_dfe),
        )
        return [
            pltpu.make_async_copy(src, dst.at[kept_index(step)], osem.at[k])
            for k, (src, dst) in enumerate(pairs)
        ]

    def outgoing_dx(step):
        side = lax.rem(step, 2)
        return pltpu.make_async_copy(dg.at[side], o_dx.at[kept_index(step)], osem.at[4 + side])

    def outgoing_memory(step):
        return pltpu.make_async_copy(mg.at[step % 2], o_mg.at[step % 2], gsem.at[step])

    def handoff(step, index):
        start, size = chunks[index]
        side = lax.rem(step, 2)
        span = pl.ds(start, size)
        return remote(
            dxb.at[side, span],
            gb.at[step, span],
            h_send.at[side, index],
            h_recv.at[step, index],
            (place.prev, place.d),
        )

    def carry_move(step):
        return remote(mgb.at[step], carb.at[step], m_send.at[step], m_recv.at[step], (last, place.d))

    def settle(step):
        @pl.when(s > 0)
        def _():
            for index in range(len(chunks)):
                handoff(step, index).wait_send()

        outgoing_dx(step).wait()

    def prologue(step):
        side = lax.rem(step, 2)
        segment = segments - 1 - lax.div(step, 2)
        for copy in residuals(step):
            copy.wait()
        for z_ref, r_ref in ((z2b, r2b), (z1b, r1b)):
            for block in row_blocks(0, half):
                z, scale = normalized(z_ref[side, block, :])
                z_ref[side, block, :] = z
                r_ref[side, block, :] = jnp.broadcast_to(scale, (BLOCK, 128))
        bias = key_bias(geometry, segment, lens_ref[side, :1, :1], (rows, 128), 0)

        def recompute(pair):
            for (start, size), begin in zip(chunks, lane_starts(chunks)[0]):
                mixed = dot_tn(
                    kvb[side, :, pair_span(pair, D)], probs[side, pair, :, begin : begin + 2 * size]
                )
                attb[side, pl.ds(start, size), pair_span(pair)] = upright(mixed)

        for pair in range(PAIRS):
            lanes = pair_span(pair)
            keys = kvb[side, :, lanes]
            for (start, size), begin in zip(chunks, lane_starts(chunks)[0]):
                queries = scaled_queries(qb[side, pl.ds(start, size), lanes])
                tiles = [bias] * (2 * size // 128)
                if 2 * size % 128:
                    tiles.append(bias[:, : 2 * size % 128])
                scores = dot_nt(keys, queries) + jnp.concatenate(tiles, axis=1)
                exponent = jnp.exp(scores - jnp.max(scores, axis=0, keepdims=True))
                inverse = 1.0 / jnp.sum(exponent, axis=0, keepdims=True)
                probs[side, pair, :, begin : begin + 2 * size] = (exponent * inverse).astype(BF)
            if pair > 0:
                recompute(pair - 1)
        recompute(PAIRS - 1)

    def norm_back(g, z, scale, gain):
        scaled = g * gain
        mean_u = jnp.mean(scaled, axis=-1, keepdims=True)
        mean_uz = jnp.mean(scaled * z, axis=-1, keepdims=True)
        return (scaled - mean_u - z * mean_uz) * scale

    def folded_rows(value):
        return value[: BLOCK // 2] + value[BLOCK // 2 :]

    def main(step):
        side = lax.rem(step, 2)
        segment = segments - 1 - lax.div(step, 2)
        first = step == 0
        pl.when(step >= 2)(lambda: settle(step - 2))

        @pl.when(step >= 1)
        def _():
            for copy in outgoing(step - 1):
                copy.wait()

        @pl.when(s == last)
        def _():
            seed_copy(step).wait()
            length = lens_ref[side, :1, :1]
            for index, block in enumerate(row_blocks(0, half)):
                row = c * half + index * BLOCK + lax.broadcasted_iota(jnp.int32, (BLOCK, part), 0)
                position = row - 2 * slot + segment * tok
                valid = (row >= 2 * slot) & (position.astype(F32) < length)
                for section in range(sections):
                    work[block, section * part : (section + 1) * part] = jnp.where(
                        valid, gp_in[side, section, block, :].astype(F32), 0.0
                    )

            @pl.when((c == 0) & (step >= 2))
            def _():
                carry_move(step - 2).wait_recv()
                work[slot : 2 * slot, :] = carb[step - 2]

        sends = []
        for index, (start, size) in enumerate(chunks):
            span = pl.ds(start, size)

            @pl.when(s < last)
            def _():
                handoff(step, index).wait_recv()
                for block in row_blocks(start, size):
                    work[block, :] = gb[step, block, :].astype(F32)

            gain_sum = jnp.zeros((BLOCK // 2, D), F32)
            shift_sum = jnp.zeros((BLOCK // 2, D), F32)
            for block in row_blocks(start, size):
                g = work[block, :]
                z = z2b[side, block, :]
                back = norm_back(g, z, r2b[side, block, :1], gain_two[...])
                dsec[block, :] = back
                dfe[block, :] = back.astype(BF)
                gain_sum += folded_rows(g * z)
                shift_sum += folded_rows(g)
            o_small[2:3, :] += jnp.sum(gain_sum, axis=0, keepdims=True)
            o_small[3:4, :] += jnp.sum(shift_sum, axis=0, keepdims=True)
            if index == 0:
                pl.when(first)(weights[0].wait)
            for lanes in pieces(FF):
                slope = gpb[side, span, lanes].astype(F32)
                pre = (dot(dfe[span], vdown[:, lanes]) * slope).astype(BF)
                dpre[span, lanes] = pre
                row, column = divmod(lanes.start, D)
                o_small[4 + row : 5 + row, column : column + STEP] += jnp.sum(
                    pre.astype(F32), axis=0, keepdims=True
                )
            if index == 0:
                pl.when(first)(weights[1].wait)
            for lanes in pieces(D):
                work[span, lanes] = dsec[span, lanes] + dot(dpre[span], vin[:, lanes])
            gain_sum = jnp.zeros((BLOCK // 2, D), F32)
            shift_sum = jnp.zeros((BLOCK // 2, D), F32)
            for block in row_blocks(start, size):
                g = work[block, :]
                z = z1b[side, block, :]
                back = norm_back(g, z, r1b[side, block, :1], gain_one[...])
                work[block, :] = back
                dbr[block, :] = back.astype(BF)
                gain_sum += folded_rows(g * z)
                shift_sum += folded_rows(g)
            o_small[0:1, :] += jnp.sum(gain_sum, axis=0, keepdims=True)
            o_small[1:2, :] += jnp.sum(shift_sum, axis=0, keepdims=True)
            if index == 0:
                pl.when(first)(weights[2].wait)
            for lanes in pieces(D):
                da[span, lanes] = dot(dbr[span], vproj[:, lanes]).astype(BF)
            heads = lax.broadcasted_iota(jnp.int32, (16, D), 0)
            columns = lax.broadcasted_iota(jnp.int32, (16, D), 1)
            member = (columns >= heads * HEAD) & (columns < (heads + 1) * HEAD)
            chooser = jnp.where(member, 1.0, 0.0).astype(BF)
            weighed = da[span, :].astype(F32) * attb[side, span, :]
            coarse = weighed.astype(BF)
            fine = (weighed - coarse.astype(F32)).astype(BF)
            row_sums = dot_nt(chooser, coarse) + dot_nt(chooser, fine)
            wide = 2 * size
            lane0 = lane_starts(chunks)[0][index]

            def score_grads(pair):
                values = kvb[side, :, pair_span(pair, D)]
                dp_tmp[pair % 2, :, :wide] = dot_nt(values, stacked_pair(da[span, pair_span(pair)]))

            score_grads(0)
            for pair in range(PAIRS):
                if pair + 1 < PAIRS:
                    score_grads(pair + 1)
                totals = jnp.concatenate(
                    [row_sums[2 * pair : 2 * pair + 1], row_sums[2 * pair + 1 : 2 * pair + 2]], axis=1
                )
                for begin in range(0, wide, 128):
                    lanes = slice(begin, min(begin + 128, wide))
                    kept_lanes = slice(lane0 + begin, lane0 + lanes.stop)
                    for offset in range(0, rows, BLOCK):
                        block = pl.ds(offset, BLOCK)
                        shifted = dp_tmp[pair % 2, block, lanes] - totals[:, lanes]
                        ds_tmp[pair, block, lanes] = (
                            probs[side, pair, block, kept_lanes].astype(F32) * shifted
                        ).astype(BF)
                d_keys = dot(ds_tmp[pair, :, :wide], scaled_queries(qb[side, span, pair_span(pair)]))
                d_values = dot(
                    probs[side, pair, :, lane0 : lane0 + wide], stacked_pair(da[span, pair_span(pair)])
                )
                if index == 0:
                    dkv[pair, :, :WIDE] = d_keys
                    dkv[pair, :, WIDE:] = d_values
                else:
                    dkv[pair, :, :WIDE] += d_keys
                    dkv[pair, :, WIDE:] += d_values
                if index == len(chunks) - 1:
                    move = remote(
                        dkv.at[pair, theirs],
                        dkv_in.at[side, pair],
                        kv_send.at[pair],
                        kv_recv.at[step, pair],
                        (s, place.other),
                    )
                    move.start()
                    sends.append(move)
            for pair in range(PAIRS):
                both = dot_tn(kvb[side, :, pair_span(pair)], ds_tmp[pair, :, :wide])
                dpj[span, pair_span(pair)] = (upright(both) * HEAD**-0.5).astype(BF)
        pl.when(first)(weights[3].wait)
        for lanes in pieces(D):
            work[:, lanes] += dot(dpj[:, :D], vqkv[:D, lanes])
        for pair in range(PAIRS):
            sends[pair].wait_recv()
            for which in range(2):
                lanes = slice(which * WIDE, (which + 1) * WIDE)
                dpj[:, pair_span(pair, (which + 1) * D)] = (
                    dkv[pair, own, lanes] + dkv_in[side, pair, :, lanes]
                ).astype(BF)
        for index, (start, size) in enumerate(chunks):
            span = pl.ds(start, size)
            for lanes in pieces(D):
                dxb[side, span, lanes] = (
                    work[span, lanes] + dot(dpj[span, D:], vqkv[D:, lanes])
                ).astype(BF)
            pl.when(s > 0)(handoff(step, index).start)
            if index == 0:

                @pl.when((s == 0) & (c == 0))
                def _():
                    mgb[step] = dxb[side, :slot].astype(F32) + dxb[side, slot : 2 * slot].astype(F32)
                    pl.when(step < steps - 2)(carry_move(step).start)

        for section in range(sections):
            dg[side, section] = dxb[side, :, section * part : (section + 1) * part]
        for copy in outgoing(step):
            copy.start()
        outgoing_dx(step).start()
        for move in sends:
            move.wait_send()

        @pl.when(step < steps - 2)
        def _():
            for copy in residuals(step + 2):
                copy.start()
            pl.when(s == last)(lambda: seed_copy(step + 2).start())

    def one_round(turn, state):
        even, odd = 2 * turn, 2 * turn + 1
        late = (s == last) & (turn == 0)
        prologue(even)
        pl.when(jnp.logical_not(late))(lambda: prologue(odd))
        main(even)
        pl.when(late)(lambda: prologue(odd))
        main(odd)
        return state

    lax.fori_loop(0, segments, one_round, 0)
    settle(steps - 2)
    settle(steps - 1)
    for copy in outgoing(steps - 1):
        copy.wait()

    @pl.when((s == 0) & (c == 0))
    def _():
        for step in range(steps - 2, steps):
            for section in range(sections):
                mg[step % 2, section] = mgb[step, :, section * part : (section + 1) * part]
            outgoing_memory(step).start()
        for step in range(steps - 2, steps):
            outgoing_memory(step).wait()
        for step in range(steps - 2):
            carry_move(step).wait_send()


def backward(sections, segments, geometry, collective, g0, lens, kept, weights):
    mem, slot, tok, rows = geometry
    half = rows // 2
    steps = 2 * segments

    def grad(width):
        return jax.ShapeDtypeStruct((steps, half, width), BF)

    outs = (
        grad(3 * D),
        grad(D),
        grad(FF),
        grad(D),
        jax.ShapeDtypeStruct(g0.shape, BF),
        jax.ShapeDtypeStruct((2, g0.shape[1], slot, g0.shape[3]), F32),
        jax.ShapeDtypeStruct((8, D), F32),
    )
    dma = pltpu.SemaphoreType.DMA
    return pl.pallas_call(
        functools.partial(backward_kernel, sections, segments, geometry),
        name="backward_layer",
        out_shape=outs,
        in_specs=[ANY, VMEM] + [ANY] * 5 + [ANY] * 4 + [VMEM] * 2,
        out_specs=(ANY,) * 6 + (VMEM,),
        scratch_shapes=[
            pltpu.VMEM((3 * D, D), BF),
            pltpu.VMEM((D, D), BF),
            pltpu.VMEM((FF, D), BF),
            pltpu.VMEM((D, FF), BF),
            pltpu.VMEM((steps, half, D), BF),
            pltpu.VMEM((2, half, D), BF),
            pltpu.VMEM((2, rows, 2 * D), BF),
            pltpu.VMEM((2, half, FF), BF),
            pltpu.VMEM((2, half, D), F32),
            pltpu.VMEM((2, half, D), F32),
            pltpu.VMEM((2, half, D), F32),
            pltpu.VMEM((2, half, 128), F32),
            pltpu.VMEM((2, half, 128), F32),
            pltpu.VMEM((2, PAIRS, rows, lane_starts(row_chunks(half))[1]), BF),
            pltpu.VMEM((half, D), F32),
            pltpu.VMEM((half, D), F32),
            pltpu.VMEM((half, D), BF),
            pltpu.VMEM((half, FF), BF),
            pltpu.VMEM((half, D), BF),
            pltpu.VMEM((half, D), BF),
            pltpu.VMEM((2, rows, 2 * row_chunks(half)[-1][1]), F32),
            pltpu.VMEM((PAIRS, rows, 2 * row_chunks(half)[-1][1]), BF),
            pltpu.VMEM((PAIRS, rows, 2 * WIDE), F32),
            pltpu.VMEM((2, PAIRS, half, 2 * WIDE), F32),
            pltpu.VMEM((half, 3 * D), BF),
            pltpu.VMEM((2, half, D), BF),
            pltpu.VMEM((steps, slot, D), F32),
            pltpu.VMEM((steps, slot, D), F32),
            pltpu.VMEM((2,) + g0.shape[1:], BF),
            pltpu.VMEM((2,) + g0.shape[1:], BF),
            pltpu.VMEM((2, g0.shape[1], slot, g0.shape[3]), F32),
            dma((4,)),
            dma((2, 5)),
            dma((steps,)),
            dma((6,)),
            dma((PAIRS,)),
            dma((steps, PAIRS)),
            dma((2, 2)),
            dma((steps, 2)),
            dma((steps,)),
            dma((steps,)),
        ],
        compiler_params=pltpu.CompilerParams(
            collective_id=collective, has_side_effects=True, vmem_limit_bytes=VMEM_LIMIT
        ),
    )(g0, lens, *kept, *weights)


def reduce_order(line):
    order = []
    low, high = 0, line - 1
    while low <= high:
        order.append(high)
        if low != high:
            order.append(low)
        low, high = low + 1, high - 1
    return order


def arrival_orders(line):
    def moment(chip, dest):
        upward = (line - 1 - dest) + chip
        downward = dest + (line - 1 - chip)
        if dest == chip:
            return line
        return upward if dest > chip else downward

    return [
        sorted(range(line), key=functools.partial(moment, chip)) for chip in range(line)
    ]


def finish_kernel(sections, segments, line, *refs):
    refs = list(refs)

    def take(count):
        taken = refs[:count]
        del refs[:count]
        return taken

    hid, dx, mem_in = take(3)
    lefts_in, rights_in, small_in = (take(4), take(4), take(1)[0]) if line else ((), (), None)
    o_h, o_x, o_m = take(3)
    outs = take(5) if line else ()
    h_send, h_got, x_send, x_got, m_send, m_got = take(6)
    place = Place(sections)
    s, c, d = place.s, place.c, place.d
    last = sections - 1
    steps = 2 * segments
    half = hid.shape[2]
    z = lax.div(d, 2)
    greet_plane(place, sections)
    if line:
        parts, sibs, ins, accs = take(5), take(5), take(5), take(5)
        big0, big1, flat0, flat1, flat2, flat3, turned = take(7)
        load, c_send, c_got, z_send, z_right, z_left, fin = take(7)
        up, down = (s, d + 2), (s, d - 2)

        def greet(target):
            pl.semaphore_signal(
                pltpu.get_barrier_semaphore(), inc=1, device_id=target, device_id_type=MESH
            )

        pl.when(z < line - 1)(lambda: greet(up))
        pl.when(z > 0)(lambda: greet(down))
        ends = (z == 0) | (z == line - 1)
        plane_wait(sections, jnp.where(ends, 1, 2))
    else:
        plane_wait(sections, 0)

    def deliveries():
        for src, dst, origin, send, got in (
            (hid, o_h, last, h_send, h_got),
            (dx, o_x, 0, x_send, x_got),
        ):
            for step in range(steps):
                segment, item = divmod(step, 2)
                rows = pl.ds(pl.multiple_of(c * half, BLOCK), half)
                for section in range(sections):
                    here = (s == section) & (c == item)
                    far = functools.partial(remote,
                        src.at[step, section],
                        dst.at[segment, rows],
                        send.at[step, section],
                        got.at[segment, c],
                        (section, place.base + item),
                    )
                    near = functools.partial(pltpu.make_async_copy,
                        src.at[step, section], dst.at[segment, rows], got.at[segment, c]
                    )
                    yield s == origin, here, far, near
        for item in range(2):
            for section in range(sections):
                here = (s == section) & (c == item)
                far = functools.partial(remote,
                    mem_in.at[item, section],
                    o_m,
                    m_send.at[item, section],
                    m_got.at[0],
                    (section, place.base + item),
                )
                near = functools.partial(pltpu.make_async_copy, mem_in.at[item, section], o_m, m_got.at[0])
                yield (s == 0) & (c == 0), here, far, near

    for mine, here, far, near in deliveries():
        pl.when(mine & jnp.logical_not(here))(lambda far=far: far().start())
        pl.when(mine & here)(lambda near=near: near().start())

    if line:
        act_in, nb_in, x_in, att_in = lefts_in
        dfe_in, dpre_in, dpj_in, dbr_in = rights_in

        def fetch(src, dst, slot):
            width = src.shape[-1]
            return [
                pltpu.make_async_copy(
                    src.at[step], dst.at[pl.ds(step * half, half), :width], load.at[slot, step]
                )
                for step in range(steps)
            ]

        loads = {
            "att": fetch(att_in, flat2, 4),
            "dbr": fetch(dbr_in, flat3, 5),
            "x": fetch(x_in, flat0, 3),
            "dpj": fetch(dpj_in, big0, 2),
            "nb": fetch(nb_in, flat1, 0),
            "dpre": fetch(dpre_in, big1, 1),
            "act": fetch(act_in, big0, 2),
            "dfe": fetch(dfe_in, flat0, 3),
        }

        def begin(name):
            for copy in loads[name]:
                copy.start()

        def ready(name):
            for copy in loads[name]:
                copy.wait()

        for name in ("att", "dbr", "x", "dpj", "nb", "dpre"):
            begin(name)
        order = reduce_order(line)
        kinds = (4, 3, 2, 0, 1)
        flows = [(kind, dest) for kind in kinds for dest in order]
        depth = 2
        far_up, far_down = range(line - 1, 0, -1), range(line - 1)
        ends_first = (
            ([(kind, dest) for kind in kinds for dest in far_up], 1, 0),
            ([(kind, dest) for kind in kinds for dest in far_down], -1, line - 1),
        )

        def arrival(position):
            dest = 0
            for chip, row in enumerate(arrival_orders(line)):
                for index, value in enumerate(row):
                    dest += jnp.where((z == chip) & (position == index), value, 0)
            return dest

        def own_rows(kind):
            block = parts[kind].shape[1] // 2
            return pl.ds(pl.multiple_of(c * block, 8), block)

        def core_move(kind, dest):
            block = parts[kind].shape[1] // 2
            theirs = pl.ds(pl.multiple_of((1 - c) * block, 8), block)
            return remote(
                parts[kind].at[dest, theirs],
                sibs[kind].at[dest],
                c_send.at[kind, dest],
                c_got.at[kind, dest],
                (s, place.other),
            )

        def line_move(kind, dest, towards):
            if towards > 0:
                slot, target, got = dest, up, z_right
            else:
                slot, target, got = jnp.where(z - 1 == dest, line, dest), down, z_left
            return remote(
                parts[kind].at[dest, own_rows(kind)],
                ins[kind].at[slot],
                z_send.at[kind, dest],
                got.at[kind, dest],
                target,
            )

        def add(kind, dest, ref, slot):
            acc = accs[kind]
            rows = min(BLOCK, acc.shape[0])

            def block(index, state):
                span = pl.ds(pl.multiple_of(index * rows, rows), rows)
                acc[span, :] += ref[slot, span, :].astype(F32)
                return state

            lax.fori_loop(0, acc.shape[0] // rows, block, 0)

        def hop(kind, dest):
            acc = accs[kind]
            core_move(kind, dest).wait_recv()
            acc[...] = parts[kind][dest, own_rows(kind), :].astype(F32)
            add(kind, dest, sibs[kind], dest)

            @pl.when((z > 0) & (z <= dest))
            def _():
                line_move(kind, dest, 1).wait_recv()
                add(kind, dest, ins[kind], dest)

            @pl.when((z < line - 1) & (z >= dest))
            def _():
                line_move(kind, dest, -1).wait_recv()
                add(kind, dest, ins[kind], jnp.where(z == dest, line, dest))

            @pl.when(z != dest)
            def _():
                parts[kind][dest, own_rows(kind), :] = acc[...].astype(parts[kind].dtype)

            for sequence, towards, end in ends_first if isinstance(dest, int) else ():
                spot = sequence.index((kind, dest)) if (kind, dest) in sequence else 0
                if spot >= depth:
                    earlier = functools.partial(line_move, *sequence[spot - depth], towards)
                    pl.when(z == end)(lambda earlier=earlier: earlier().wait_send())
            pl.when(z < dest)(lambda: line_move(kind, dest, 1).start())
            pl.when(z > dest)(lambda: line_move(kind, dest, -1).start())

            @pl.when(z == dest)
            def _():
                copy = pltpu.make_async_copy(acc, outs[kind], fin.at[kind])
                copy.start()
                copy.wait()

        def no_wait(dest):
            return ((z == 0) & (dest > 0)) | ((z == line - 1) & (dest < line - 1))

        matrices = (
            ("nb", "dpre", flat1, big1, FF),
            ("act", "dfe", big0, flat0, D),
            ("x", "dpj", flat0, big0, 3 * D),
            ("att", "dbr", flat2, flat3, D),
        )
        size = D // (2 * line)
        long = FF // (2 * line)
        for dest in order:
            parts[4][dest] = jnp.zeros(parts[4].shape[1:], F32)
            for core in range(2):
                index = 2 * dest + core
                for row in range(4):
                    parts[4][dest, 8 * core + row : 8 * core + row + 1, :size] = small_in[
                        row : row + 1, index * size : (index + 1) * size
                    ]
                row, column = divmod(index * long, D)
                parts[4][dest, 8 * core + 4 : 8 * core + 5, :] = small_in[
                    4 + row : 5 + row, column : column + long
                ]
            core_move(4, dest).start()

        def from_ends(kind):
            for dest in far_up:
                pl.when(z == 0)(functools.partial(hop, kind, dest))
            for dest in far_down:
                pl.when(z == line - 1)(functools.partial(hop, kind, dest))

        from_ends(4)
        for kind in kinds[1:]:
            left_name, right_name, left, right, width = matrices[kind]
            if kind == 1:
                begin(left_name)
                begin(right_name)
            ready(left_name)
            ready(right_name)
            block = parts[kind].shape[1]
            for dest in order:
                turned[:block, :] = jnp.transpose(left[:, dest * block : (dest + 1) * block])
                for lanes in pieces(width):
                    parts[kind][dest, :, lanes] = dot(turned[:block, :], right[:, lanes]).astype(BF)
                core_move(kind, dest).start()
            from_ends(kind)
        for kind in kinds:

            def by_arrival(position, state):
                dest = arrival(position)
                pl.when(jnp.logical_not(no_wait(dest)))(lambda: hop(kind, dest))
                return state

            lax.fori_loop(0, line, by_arrival, 0)
        for kind, dest in flows:
            core_move(kind, dest).wait_send()
            for sequence, towards, end in ends_first:
                if (kind, dest) in sequence:
                    pending = (z < dest) if towards > 0 else (z > dest)
                    if (kind, dest) not in sequence[-depth:]:
                        pending &= z != end
                    pl.when(pending)(lambda: line_move(kind, dest, towards).wait_send())

    for mine, here, far, near in deliveries():
        pl.when(mine & jnp.logical_not(here))(lambda far=far: far().wait_send())
    for src, dst, origin, got in ((hid, o_h, last, h_got), (dx, o_x, 0, x_got)):
        for segment in range(segments):
            for core in range(2):
                rows = pl.ds(core * half, half)
                here = (s == origin) & (c == core)
                far = functools.partial(remote,
                    src.at[0, 0], dst.at[segment, rows], h_send.at[0, 0], got.at[segment, core], (s, d)
                )
                near = functools.partial(pltpu.make_async_copy, src.at[0, 0], dst.at[segment, rows], got.at[segment, core])
                pl.when(jnp.logical_not(here))(lambda far=far: far().wait_recv())
                pl.when(here)(lambda near=near: near().wait())
    here = (s == 0) & (c == 0)
    far = functools.partial(remote, mem_in.at[0, 0], o_m, m_send.at[0, 0], m_got.at[0], (s, d))
    near = functools.partial(pltpu.make_async_copy, mem_in.at[0, 0], o_m, m_got.at[0])
    pl.when(jnp.logical_not(here))(lambda far=far: far().wait_recv())
    pl.when(here)(lambda near=near: near().wait())


def finish(sections, segments, line, collective, hid, dx, memory_term, sums):
    steps, _, half, part = hid.shape
    slot = memory_term.shape[2]
    dma = pltpu.SemaphoreType.DMA
    outs = [
        jax.ShapeDtypeStruct((segments, 2 * half, part), BF),
        jax.ShapeDtypeStruct((segments, 2 * half, part), BF),
        jax.ShapeDtypeStruct((slot, part), F32),
    ]
    scratch = [
        dma((steps, sections)),
        dma((segments, 2)),
        dma((steps, sections)),
        dma((segments, 2)),
        dma((2, sections)),
        dma((1,)),
    ]
    operands = [hid, dx, memory_term]
    if line:
        lefts, rights, small = sums
        operands += [*lefts, *rights, small]
        block = D // (2 * line)
        shapes = (
            (block, FF, BF),
            (FF // (2 * line), D, BF),
            (block, 3 * D, BF),
            (block, D, BF),
            (8, FF // (2 * line), F32),
        )
        outs += [jax.ShapeDtypeStruct(shape[:2], F32) for shape in shapes]
        total = steps * half
        scratch += [pltpu.VMEM((line, 2 * rows, width), kind) for rows, width, kind in shapes]
        scratch += [pltpu.VMEM((line, rows, width), kind) for rows, width, kind in shapes]
        scratch += [pltpu.VMEM((line + 1, rows, width), kind) for rows, width, kind in shapes]
        scratch += [pltpu.VMEM((rows, width), F32) for rows, width, kind in shapes]
        scratch += [pltpu.VMEM((total, FF), BF)] * 2 + [pltpu.VMEM((total, D), BF)] * 4
        scratch += [pltpu.VMEM((FF // line, total), BF)]
        scratch += [
            dma((6, steps)),
            dma((5, line)),
            dma((5, line)),
            dma((5, line)),
            dma((5, line)),
            dma((5, line)),
            dma((5,)),
        ]
    return pl.pallas_call(
        functools.partial(finish_kernel, sections, segments, line),
        name="finish",
        out_shape=tuple(outs),
        in_specs=[ANY] * (len(operands) - bool(line)) + [VMEM] * bool(line),
        out_specs=(ANY,) * len(outs),
        scratch_shapes=scratch,
        compiler_params=pltpu.CompilerParams(
            collective_id=collective, has_side_effects=True, vmem_limit_bytes=VMEM_LIMIT
        ),
    )(*operands)


def on_device(
    sections,
    inputs,
    out_grad,
    memory,
    lengths,
    w_qkv,
    w_proj,
    gain_one,
    shift_one,
    w_in,
    b_in,
    w_down,
    gain_two,
    shift_two,
):
    segs, tok, part = inputs.shape[1:]
    mem = memory.shape[1]
    slot = -(-mem // BLOCK) * BLOCK
    rows = -(-(2 * slot + tok) // (2 * BLOCK)) * 2 * BLOCK
    half = rows // 2
    geometry = (mem, slot, tok, rows)
    back_pad = rows - 2 * slot - tok

    head = jnp.pad(memory[:1], ((0, segs - 1), (0, slot - mem), (0, 0)))
    blank = jnp.zeros((segs, back_pad, part), BF)
    tokens = jnp.concatenate([head, head, inputs[0], blank], axis=1)
    cotangent = jnp.pad(out_grad[0], ((0, 0), (2 * slot, back_pad), (0, 0)))
    length_tile = jnp.broadcast_to(lengths.astype(F32), (8, 128))

    def halves(array):
        return array.reshape(segs, 2, half, part)

    matrices = (w_qkv[0], w_proj[0], w_in[0], w_down[0])
    forward_weights = matrices + (gain_one, shift_one, b_in, gain_two, shift_two)
    x, q, kv, att, nb, act, gp, s1, s2, hid, *turned, g0, lens = forward(
        sections, segs, geometry, 0, halves(tokens), halves(cotangent), length_tile, forward_weights
    )
    dpj, dbr, dpre, dfe, dx, memory_term, small = backward(
        sections, segs, geometry, 1, g0, lens, (q, kv, gp, s1, s2), (*turned, gain_one, gain_two)
    )
    devices = lax.axis_size("dp")
    lefts, rights = (act, nb, x, att), (dfe, dpre, dpj, dbr)
    line = devices // 2 if D % (devices * BLOCK) == 0 and FF % (devices * 128) == 0 and devices > 2 else 0
    sums = None
    if line:
        sums = (lefts, rights, small)
    out_parts, in_parts, memory_part, *reduced = finish(
        sections, segs, line, 2, hid, dx, memory_term, sums
    )

    def owned(parts):
        return parts[:, 2 * slot : 2 * slot + tok]

    position = jnp.arange(segs * tok, dtype=jnp.int32).reshape(segs, tok)
    token_valid = position < lengths[0]
    outputs = jnp.where(token_valid[:, :, None], owned(out_parts), jnp.zeros((), BF))
    input_grad = owned(in_parts)
    memory_grad = memory_part[:mem]

    if line:
        d_in, d_down, d_qkv, d_proj, share = reduced
        size = D // devices
        vectors = [share[k : k + 1, :size] for k in range(4)] + [share[4:5]]
    else:

        def weight_grad(left, right):
            full = jnp.einsum(
                "rd,re->de",
                left.reshape(2 * segs * half, -1),
                right.reshape(2 * segs * half, -1),
                preferred_element_type=F32,
            )
            return lax.psum_scatter(full.astype(BF), "dp", scatter_dimension=0, tiled=True).astype(F32)

        d_down, d_in, d_qkv, d_proj = [weight_grad(*pair) for pair in zip(lefts, rights)]
        vectors = [
            lax.psum_scatter(rows.reshape(1, -1), "dp", scatter_dimension=1, tiled=True)
            for rows in (small[0], small[1], small[2], small[3], small[4:8])
        ]
    gain_one_share, shift_one_share, gain_two_share, shift_two_share, b_in_share = vectors

    return (
        outputs[None],
        input_grad[None],
        memory_grad[None],
        d_qkv[None],
        d_proj[None],
        gain_one_share,
        shift_one_share,
        d_in[None],
        b_in_share,
        d_down[None],
        gain_two_share,
        shift_two_share,
    )


def solution(mesh):
    return jax.shard_map(
        functools.partial(on_device, mesh.shape["section"]),
        mesh=mesh,
        in_specs=(
            P("dp", None, None, "section"),
            P("dp", None, None, "section"),
            P("dp", None, "section"),
            P("dp"),
            P("section", None, None),
            P("section", None, None),
            P("section", None),
            P("section", None),
            P("section", None, None),
            P("section", None),
            P("section", None, None),
            P("section", None),
            P("section", None),
        ),
        out_specs=(
            P("dp", None, None, "section"),
            P("dp", None, None, "section"),
            P("dp", None, "section"),
            P("section", "dp", None),
            P("section", "dp", None),
            P("section", "dp"),
            P("section", "dp"),
            P("section", "dp", None),
            P("section", "dp"),
            P("section", "dp", None),
            P("section", "dp"),
            P("section", "dp"),
        ),
        check_vma=False,
    )
```
